32 devices in a mesh: row: 4 (over y, x), col: 8 (over z, core).
Axes of the slice: x: 2, y: 2, z: 4, core: 2. Of those that a mesh axis runs over, the one named last changes fastest.
Arguments:
- latent: bfloat16 [2, 128, 128, 512], P(None, 'row', 'col'), may hold values from -6 to 6
- w_qkv: bfloat16 [512, 1536], replicated, may hold values from -3 to 3
- w_out: bfloat16 [512, 512], replicated, may hold values from -0.25 to 0.25
- ln_gain: float32 [512], replicated, may hold values from 0.5 to 2
- dw_kernel: bfloat16 [3, 3, 512], replicated, may hold values from -1.1953125 to 1.1953125
- grad_out: bfloat16 [2, 128, 128, 512], P(None, 'row', 'col'), may hold values from -6 to 6
Outputs:
- grad_latent: bfloat16 [2, 128, 128, 512], P(None, 'row', 'col')
- grad_qkv: float32 [512, 1536], P(('row', 'col'))
- grad_wout: float32 [512, 512], P(('row', 'col'))
- grad_gain: float32 [512], replicated
- grad_kernel: float32 [3, 3, 512], replicated
The draws below stay inside these ranges and needn't reach their ends.
All inputs are finite; a program needn't handle non-finite values.
Results may differ from the reference program's by a relative error of at most 0.03.
The reference program's roundings to bfloat16 on the way count: a program that leaves them out, or rounds other values in their place, can miss the bound.
Values may be sent and summed in bfloat16 or wider, within the bound.
No kernel may reach another device: no remote copies, remote signals or barrier semaphores. Data moves between devices by JAX's collectives and lax.ppermute only.
A program may use at most 128 MiB of HBM per device.

```python
import math
import jax
import jax.numpy as jnp
from jax import lax

D = 512
HEADS = 16
HEAD = 32
GRID = 8
BATCH = 2
LH = 128
LW = 128


def draw_w_qkv(key, part):
    keys = jax.random.split(key, 3)
    first = jnp.clip(jax.random.normal(keys[0], (D, D), jnp.float32), -4.0, 4.0)
    second = jnp.clip(jax.random.normal(keys[1], (D, D), jnp.float32), -4.0, 4.0)
    third = jnp.clip(jax.random.normal(keys[2], (D, D), jnp.float32), -4.0, 4.0)
    query_part = first
    key_part = second
    whole = jnp.concatenate([query_part, key_part, third], axis=1) * D ** (-0.5)
    return whole.astype(jnp.bfloat16)


def steps_of(own_key, dims, cuts, smallest, high):
    gain, own = 1.0, jax.random.fold_in(own_key, 6)
    for position, blocks in cuts:
        steps = jnp.exp(jax.random.uniform(jax.random.fold_in(own, position), (blocks,), jnp.float32, smallest / len(cuts), high / len(cuts)))
        gain = gain * jnp.repeat(steps, dims[position] // blocks).reshape([-1 if axis == position else 1 for axis in range(len(dims))])
    return gain


def noise(stream_key, shape, spread, bound, cuts=(), dtype=jnp.bfloat16):
    factor_of = steps_of(stream_key, shape, cuts, -0.22, 0.18) if cuts else 1.0
    result = jax.random.normal(stream_key, shape, jnp.float32) * spread * factor_of
    return jnp.minimum(jnp.maximum(result, -bound), bound).astype(dtype)


def setup_inputs(seed: int = 0) -> dict:
    splits = jax.random.split(jax.random.key(seed), 7)
    latent = noise(splits[0], (BATCH, LH, LW, D), 1.0, 6.0, ((1, 4), (2, 8)))
    w_qkv = draw_w_qkv(jax.random.fold_in(splits[6], 71), 0)
    w_out = noise(splits[2], (D, D), D ** -0.5, 0.25)
    ln_gain = jnp.clip(jnp.exp(jax.random.uniform(splits[3], (D,), jnp.float32, math.log(0.5), math.log(2.0))), 0.5, 2.0)
    dw_kernel = noise(splits[4], (3, 3, D), 0.3, 1.1953125)
    grad_out = noise(splits[5], (BATCH, LH, LW, D), 1.0, 6.0, ((1, 4), (2, 8)))
    return {"latent": latent, "w_qkv": w_qkv, "w_out": w_out, "ln_gain": ln_gain, "dw_kernel": dw_kernel, "grad_out": grad_out}


def spatial_mix(padded, kernel, rows, cols, flipped):
    total = jnp.zeros((rows, cols, padded.shape[2]), jnp.float32)
    for row_shift in range(3):
        for col_shift in range(3):
            row_start = 2 - row_shift if flipped else row_shift
            col_start = 2 - col_shift if flipped else col_shift
            total = total + kernel[row_shift, col_shift] * padded[row_start:row_start + rows, col_start:col_start + cols]
    return total

def to_windows(field):
    rows, cols, features = field.shape
    shaped = field.reshape(GRID, rows // GRID, GRID, cols // GRID, features)
    return jnp.transpose(shaped, (1, 3, 0, 2, 4)).reshape(-1, GRID * GRID, features)

def from_windows(flat, rows, cols):
    features = flat.shape[-1]
    shaped = flat.reshape(rows // GRID, cols // GRID, GRID, GRID, features)
    return jnp.transpose(shaped, (2, 0, 3, 1, 4)).reshape(rows, cols, features)

def one_sample(inputs, w_qkv, w_out, ln_gain, kernel):
    sample, cotangent = inputs
    rows, cols, features = sample.shape
    score_scale = HEAD ** (-0.5)
    latent_padded = jnp.pad(sample.astype(jnp.float32), ((1, 1), (1, 1), (0, 0)))
    mixed = (sample.astype(jnp.float32) + spatial_mix(latent_padded, kernel, rows, cols, False)).astype(jnp.bfloat16)
    mixed_f = mixed.astype(jnp.float32)
    centred = mixed_f - lax.optimization_barrier(jnp.mean(mixed_f, axis=-1, keepdims=True))
    rstd = lax.rsqrt(lax.optimization_barrier(jnp.mean(centred * centred, axis=-1, keepdims=True)) + 1e-05)
    nhat = centred * rstd
    normed = (nhat * ln_gain).astype(jnp.bfloat16)
    normed_win = to_windows(normed)
    count = normed_win.shape[0]
    normed_flat = normed_win.reshape(-1, features)
    packed = jnp.dot(normed_flat, w_qkv, preferred_element_type=jnp.float32).astype(jnp.bfloat16)
    packed = packed.reshape(count, GRID * GRID, 3, HEADS, HEAD)
    query_b = packed[:, :, 0].astype(jnp.float32)
    key_b = packed[:, :, 1].astype(jnp.float32)
    value_b = packed[:, :, 2].astype(jnp.float32)
    scores = jnp.einsum('wqhd,wkhd->whqk', query_b, key_b) * score_scale
    probs = jax.nn.softmax(scores, axis=-1)
    probs_b = probs.astype(jnp.bfloat16)
    attended = jnp.einsum('whqk,wkhd->wqhd', probs_b.astype(jnp.float32), value_b).astype(jnp.bfloat16)
    attended_flat = attended.reshape(-1, features)
    grad_flat = to_windows(cotangent).reshape(-1, features)
    grad_wout = jnp.dot(attended_flat.T, grad_flat, preferred_element_type=jnp.float32)
    d_att = jnp.dot(grad_flat, w_out.T, preferred_element_type=jnp.float32).astype(jnp.bfloat16)
    d_att = d_att.reshape(count, GRID * GRID, HEADS, HEAD).astype(jnp.float32)
    d_probs = jnp.einsum('wqhd,wkhd->whqk', d_att, value_b)
    d_value = jnp.einsum('whqk,wqhd->wkhd', probs_b.astype(jnp.float32), d_att).astype(jnp.bfloat16)
    d_scores = (probs * (d_probs - lax.optimization_barrier(jnp.sum(probs * d_probs, axis=-1, keepdims=True))) * score_scale).astype(jnp.bfloat16)
    d_scores_f = d_scores.astype(jnp.float32)
    d_query = jnp.einsum('whqk,wkhd->wqhd', d_scores_f, key_b).astype(jnp.bfloat16)
    d_key = jnp.einsum('whqk,wqhd->wkhd', d_scores_f, query_b).astype(jnp.bfloat16)
    d_packed = jnp.stack([d_query, d_key, d_value], axis=2).reshape(-1, 3 * features)
    grad_qkv = jnp.dot(normed_flat.T, d_packed, preferred_element_type=jnp.float32)
    d_normed = jnp.dot(d_packed, w_qkv.T, preferred_element_type=jnp.float32).astype(jnp.bfloat16)
    d_normed = from_windows(d_normed.reshape(count, GRID * GRID, features), rows, cols).astype(jnp.float32)
    grad_gain = lax.optimization_barrier(jnp.sum(d_normed * nhat, axis=(0, 1)))
    scaled = d_normed * ln_gain
    d_mixed = cotangent.astype(jnp.float32) + rstd * (scaled - lax.optimization_barrier(jnp.mean(scaled, axis=-1, keepdims=True)) - nhat * lax.optimization_barrier(jnp.mean(scaled * nhat, axis=-1, keepdims=True)))
    d_mixed = d_mixed.astype(jnp.bfloat16).astype(jnp.float32)
    d_padded = jnp.pad(d_mixed, ((1, 1), (1, 1), (0, 0)))
    grad_latent = (d_mixed + spatial_mix(d_padded, kernel, rows, cols, True)).astype(jnp.bfloat16)
    kernel_terms = []
    for row_shift in range(3):
        for col_shift in range(3):
            kernel_terms.append(lax.optimization_barrier(jnp.sum(d_mixed * latent_padded[row_shift:row_shift + rows, col_shift:col_shift + cols], axis=(0, 1))))
    grad_kernel = jnp.stack(kernel_terms, axis=0).reshape(3, 3, features)
    return (grad_latent, grad_qkv, grad_wout, grad_gain, grad_kernel)

def reference(latent, w_qkv, w_out, ln_gain, dw_kernel, grad_out):
    kernel = dw_kernel.astype(jnp.float32)
    results = lax.map(lambda inputs: one_sample(inputs, w_qkv, w_out, ln_gain, kernel), (latent, grad_out))
    grad_latent, grad_qkv, grad_wout, grad_gain, grad_kernel = results
    return (grad_latent, lax.optimization_barrier(jnp.sum(grad_qkv, axis=0)), lax.optimization_barrier(jnp.sum(grad_wout, axis=0)), lax.optimization_barrier(jnp.sum(grad_gain, axis=0)), lax.optimization_barrier(jnp.sum(grad_kernel, axis=0)))
```

```python
import functools

import jax
import jax.numpy as jnp
import numpy as np
from jax import lax
from jax.experimental import pallas as pl
from jax.experimental.pallas import tpu as pltpu
from jax.sharding import PartitionSpec as P

HEADS = 16
HEAD = 32
GRID = 8
CELLS = GRID * GRID
AXES = ("row", "col")
F32 = jnp.float32
BF16 = jnp.bfloat16
LIMIT = 56 * 1024 * 1024


def dot(left, right, dims=((1,), (0,))):
    return lax.dot_general(left, right, (dims, ((), ())), preferred_element_type=F32)


class Plan:
    def __init__(self, batches, tile_rows, tile_cols, row_count, col_count, cuts):
        devices = row_count * col_count
        high = tile_rows * row_count // GRID
        full = tile_cols * col_count // GRID
        wide = min(full, tile_cols)
        groups = full // wide
        reps_r = tile_rows // high
        reps_s = tile_cols // wide
        reps = reps_r * reps_s
        classes = [(b, a, e) for b in range(batches) for a in range(high) for e in range(wide)]
        edge = [c for c in classes if c[1] in (0, high - 1) or c[2] in (0, wide - 1)]
        rest = [c for c in classes if c not in set(edge)]
        place = {c: (n % devices, n // devices) for n, c in enumerate(edge + rest)}
        slots = len(classes) // devices
        self.edge_slots = -(-len(edge) // devices)
        self.devices = devices
        cells = batches * tile_rows * tile_cols
        bounds = cuts(slots, self.edge_slots)
        self.send, self.sort, self.rows = [], [], []
        self.border = []
        spots = []
        for edge_row in (0, tile_rows - 1):
            spots += [(b, edge_row, w) for b in range(batches) for w in range(tile_cols)]
        for edge_col in (0, tile_cols - 1):
            spots += [(b, h, edge_col) for b in range(batches) for h in range(tile_rows)]
        self.border_tile = np.zeros((len(spots), cells), np.float32)
        for n, (b, h, w) in enumerate(spots):
            self.border_tile[n, (b * tile_rows + h) * tile_cols + w] = 1
        for first, last in zip(bounds[:-1], bounds[1:]):
            size = (last - first) * reps
            rows = devices * size
            send = np.zeros((rows, cells), np.float32)
            for b in range(batches):
                for h in range(tile_rows):
                    for w in range(tile_cols):
                        owner, slot = place[(b, h % high, w % wide)]
                        if first <= slot < last:
                            rep = (h // high) * reps_s + w // wide
                            send[owner * size + (slot - first) * reps + rep, (b * tile_rows + h) * tile_cols + w] = 1
            sort = np.zeros((rows, rows), np.float32)
            for i in range(row_count):
                for j in range(col_count):
                    for slot in range(last - first):
                        for r in range(reps_r):
                            for s in range(reps_s):
                                start = j * tile_cols + s * wide
                                window = slot * groups + (start % full) // wide
                                cell = (i * reps_r + r) * GRID + start // full
                                source = (i * col_count + j) * size + slot * reps + r * reps_s + s
                                sort[window * CELLS + cell, source] = 1
            self.send.append(send)
            self.sort.append(sort)
            self.rows.append(rows)


def pad_rows(matrix, to):
    return np.concatenate([matrix, np.zeros((to - matrix.shape[0], matrix.shape[1]), matrix.dtype)], 0)


def send_kernel(x_ref, *refs):
    count = len(refs) // 2
    for order_ref, out_ref in zip(refs[:count], refs[count:]):
        out_ref[...] = dot(order_ref[...], x_ref[...]).astype(BF16)


def fill_shifts(shift_ref, left_ref, right_ref, side_l, side_r):
    _, batches, rows, cols, feats = shift_ref.shape
    spot = lax.broadcasted_iota(jnp.int32, (cols, feats), 0)
    for b in range(batches):
        side_l[b] = left_ref[b].astype(F32)
        side_r[b] = right_ref[b].astype(F32)

        def step(h, carry, b=b):
            x = shift_ref[1, b, h].astype(F32)
            low = jnp.where(spot == 0, side_l[b, pl.ds(h, 1), :], pltpu.roll(x, 1, 0))
            high = jnp.where(spot == cols - 1, side_r[b, pl.ds(h, 1), :], pltpu.roll(x, cols - 1, 0))
            shift_ref[0, b, h] = low.astype(BF16)
            shift_ref[2, b, h] = high.astype(BF16)
            return carry

        lax.fori_loop(0, rows, step, 0, unroll=2)


def mix_kernel(count, lat_ref, top_ref, bot_ref, left_ref, right_ref, dw_ref, gain_ref, *refs):
    orders = refs[:count]
    outs = refs[count : 2 * count]
    mixed_ref, shift_ref, normed_ref, side_l, side_r = refs[2 * count :]
    batches, rows, cols, feats = lat_ref.shape
    shift_ref[1, :, 1 : rows + 1] = lat_ref[...]
    shift_ref[1, :, 0] = top_ref[:, 0]
    shift_ref[1, :, rows + 1] = bot_ref[:, 0]
    fill_shifts(shift_ref, left_ref, right_ref, side_l, side_r)
    kern = [[dw_ref[i, j : j + 1, :].astype(F32) for j in range(3)] for i in range(3)]
    gain = gain_ref[...]
    for b in range(batches):

        def step(h, carry, b=b):
            total = jnp.zeros((cols, feats), F32)
            for i in range(3):
                for j in range(3):
                    total = total + kern[i][j] * shift_ref[j, b, h + i].astype(F32)
            mixed = (shift_ref[1, b, h + 1].astype(F32) + total).astype(BF16)
            mixed_ref[b, h] = mixed
            mixed = mixed.astype(F32)
            centred = mixed - jnp.mean(mixed, axis=-1, keepdims=True)
            rstd = lax.rsqrt(jnp.mean(centred * centred, axis=-1, keepdims=True) + 1e-05)
            normed_ref[pl.ds(pl.multiple_of((b * rows + h) * cols, cols), cols), :] = (
                centred * rstd * gain
            ).astype(BF16)
            return carry

        lax.fori_loop(0, rows, step, 0, unroll=2)
    for order_ref, out_ref in zip(orders, outs):
        out_ref[...] = dot(order_ref[...], normed_ref[...]).astype(BF16)


def window_kernel(first, last, places, n_ref, g_ref, sort_ref, wqkv_ref, wout_ref, *refs):
    if not first:
        old_ref, refs = refs[0], refs[1:]
    dn_ref, dw_ref, nw, gw, packed, datt, att, dpacked, head_mask, half_mask, acc = refs
    rows, feats = n_ref.shape
    tiles = feats // 256
    scale = HEAD ** (-0.5)
    block = 256 if rows % 256 == 0 else rows

    head_mask[...] = (
        (lax.broadcasted_iota(jnp.int32, (4 * CELLS, 256), 1) // HEAD) % 4
        == lax.broadcasted_iota(jnp.int32, (4 * CELLS, 256), 0) // CELLS
    ).astype(F32).astype(BF16)
    half_mask[...] = (
        lax.broadcasted_iota(jnp.int32, (2 * CELLS, 256), 1) // 128
        == lax.broadcasted_iota(jnp.int32, (2 * CELLS, 256), 0) // CELLS
    ).astype(F32).astype(BF16)

    def project(n, carry):
        at = pl.ds(pl.multiple_of(n * block, block), block)
        normed = dot(sort_ref[at, :], n_ref[...]).astype(BF16)
        nw[at, :] = normed
        packed[at, :] = dot(normed, wqkv_ref[...]).astype(BF16)
        grad = dot(sort_ref[at, :], g_ref[...]).astype(BF16)
        gw[at, :] = grad
        datt[at, :] = dot(grad, wout_ref[...], ((1,), (1,))).astype(BF16)
        return carry

    lax.fori_loop(0, rows // block, project, 0)

    lane = lax.broadcasted_iota(jnp.int32, (CELLS, 256), 1)
    lane_half = lane < 128
    lane_head = (lane // HEAD) % 4

    def fold_heads(full):
        out = full[3 * CELLS :]
        for h in (2, 1, 0):
            out = jnp.where(lane_head == h, full[h * CELLS : (h + 1) * CELLS], out)
        return out

    def one(n, carry):
        at = pl.ds(pl.multiple_of(n * CELLS, CELLS), CELLS)
        for t in range(tiles):
            cols = [slice(p * feats + t * 256, p * feats + (t + 1) * 256) for p in range(3)]
            query = packed[at, cols[0]]
            key = packed[at, cols[1]]
            value = packed[at, cols[2]]
            grad = datt[at, t * 256 : (t + 1) * 256]
            key_big = jnp.concatenate([key] * 4, axis=0) * head_mask[...]
            value_big = jnp.concatenate([value] * 4, axis=0) * head_mask[...]
            query_two = jnp.concatenate([query] * 2, axis=0) * half_mask[...]
            grad_two = jnp.concatenate([grad] * 2, axis=0) * half_mask[...]
            scores = (dot(key_big, query_two, ((1,), (1,))) * scale).reshape(4, CELLS, 2 * CELLS)
            d_probs = dot(value_big, grad_two, ((1,), (1,))).reshape(4, CELLS, 2 * CELLS)
            raised = jnp.exp(scores - jnp.max(scores, axis=1, keepdims=True))
            probs = raised / jnp.sum(raised, axis=1, keepdims=True)
            probs_b = probs.astype(BF16).reshape(4 * CELLS, 2 * CELLS)
            inner = jnp.sum(probs * d_probs, axis=1, keepdims=True)
            d_scores = (
                (probs * (d_probs - inner) * scale).astype(BF16).reshape(4 * CELLS, 2 * CELLS)
            )
            out = dot(probs_b, value_big, ((0,), (0,)))
            att[at, t * 256 : (t + 1) * 256] = jnp.where(
                lane_half, out[:CELLS], out[CELLS:]
            ).astype(BF16)
            d_query = dot(d_scores, key_big, ((0,), (0,)))
            dpacked[at, cols[0]] = jnp.where(
                lane_half, d_query[:CELLS], d_query[CELLS:]
            ).astype(BF16)
            dpacked[at, cols[1]] = fold_heads(dot(d_scores, query_two)).astype(BF16)
            dpacked[at, cols[2]] = fold_heads(dot(probs_b, grad_two)).astype(BF16)
        return carry

    lax.fori_loop(0, rows // CELLS, one, 0)

    def back(n, carry):
        at = pl.ds(pl.multiple_of(n * block, block), block)
        gw_free = dot(dpacked[at, :], wqkv_ref[...], ((1,), (1,))).astype(BF16)
        datt[at, :] = gw_free
        return carry

    lax.fori_loop(0, rows // block, back, 0)
    dn_ref[...] = dot(sort_ref[...], datt[...], ((0,), (0,))).astype(BF16)
    normed_t = nw[...].T
    wide = 3 * feats
    for t in range(wide // 256):
        at = slice(t * 256, (t + 1) * 256)
        acc[:, at] = dot(normed_t, dpacked[:, at])
    acc[:, wide:] = dot(att[...].T, gw[...])
    if not first:
        acc[...] += old_ref[...]
    if last:
        size = feats // len(places)
        for n, place in enumerate(places):
            dw_ref[place * size : (place + 1) * size, :] = acc[n * size : (n + 1) * size, :].astype(BF16)
    else:
        dw_ref[...] = acc[...]


def norm_back(d_normed, mixed, grad, gain):
    mixed = mixed.astype(F32)
    centred = mixed - jnp.mean(mixed, axis=-1, keepdims=True)
    rstd = lax.rsqrt(jnp.mean(centred * centred, axis=-1, keepdims=True) + 1e-05)
    nhat = centred * rstd
    scaled = d_normed * gain
    d_mixed = grad.astype(F32) + rstd * (
        scaled
        - jnp.mean(scaled, axis=-1, keepdims=True)
        - nhat * jnp.mean(scaled * nhat, axis=-1, keepdims=True)
    )
    return d_mixed.astype(BF16), nhat


def border_kernel(dn_ref, mixed_ref, grad_ref, pick_dn_ref, pick_ref, gain_ref, out_ref):
    d_normed = dot(pick_dn_ref[...], dn_ref[...])
    mixed = dot(pick_ref[...], mixed_ref[...])
    grad = dot(pick_ref[...], grad_ref[...])
    out_ref[...] = norm_back(d_normed, mixed, grad, gain_ref[...])[0]


def final_kernel(count, *refs):
    dns, orders, refs = refs[:count], refs[count : 2 * count], refs[2 * count :]
    (mixed_ref, grad_ref, x_ref, top_ref, bot_ref, left_ref, right_ref, dw_ref, gain_ref) = refs[:9]
    out_ref, sums_ref, shift_ref, dn, side_l, side_r = refs[9:]
    batches, rows, cols, feats = mixed_ref.shape
    cells = batches * rows * cols
    block = 256

    def unsort(n, carry):
        at = pl.ds(pl.multiple_of(n * block, block), block)
        total = dot(orders[0][at, :], dns[0][...])
        for order, part in zip(orders[1:], dns[1:]):
            total = total + dot(order[at, :], part[...])
        dn[at, :] = total
        return carry

    lax.fori_loop(0, cells // block, unsort, 0)
    gain = gain_ref[...]
    shift_ref[1, :, 0] = top_ref[:, 0]
    shift_ref[1, :, rows + 1] = bot_ref[:, 0]
    gain_sum = jnp.zeros((cols, feats), F32)
    for b in range(batches):

        def step(h, gain_sum, b=b):
            d_normed = dn[pl.ds(pl.multiple_of((b * rows + h) * cols, cols), cols), :]
            d_mixed, nhat = norm_back(d_normed, mixed_ref[b, h], grad_ref[b, h], gain)
            shift_ref[1, b, h + 1] = d_mixed
            return gain_sum + d_normed * nhat

        gain_sum = lax.fori_loop(0, rows, step, gain_sum, unroll=2)
    sums_ref[9:10, :] = jnp.sum(gain_sum, axis=0, keepdims=True)
    sums_ref[10:, :] = jnp.zeros((sums_ref.shape[0] - 10, feats), F32)
    fill_shifts(shift_ref, left_ref, right_ref, side_l, side_r)
    kern = [[dw_ref[i, j : j + 1, :].astype(F32) for j in range(3)] for i in range(3)]
    for b in range(batches):

        def conv(h, carry, b=b):
            total = jnp.zeros((cols, feats), F32)
            for i in range(3):
                for j in range(3):
                    total = total + kern[i][j] * shift_ref[2 - j, b, h + 2 - i].astype(F32)
            out_ref[b, h] = (shift_ref[1, b, h + 1].astype(F32) + total).astype(BF16)
            return carry

        lax.fori_loop(0, rows, conv, 0, unroll=2)
    for j in range(3):
        sums = [jnp.zeros((cols, feats), F32) for _ in range(3)]
        for b in range(batches):

            def grads(h, sums, b=b, j=j):
                d_mixed = shift_ref[1, b, h + 1].astype(F32)
                return [s + d_mixed * x_ref[j, b, h + i].astype(F32) for i, s in enumerate(sums)]

            sums = lax.fori_loop(0, rows, grads, sums, unroll=2)
        for i in range(3):
            sums_ref[3 * i + j : 3 * i + j + 1, :] = jnp.sum(sums[i], axis=0, keepdims=True)


def call(body, outs, scratch, args, flops, name):
    moved = sum(int(np.prod(o.shape)) * o.dtype.itemsize for o in (*outs, *args))
    vmem = pl.BlockSpec(memory_space=pltpu.VMEM)
    return pl.pallas_call(
        body,
        out_shape=outs,
        in_specs=[vmem] * len(args),
        out_specs=[vmem] * len(outs),
        scratch_shapes=scratch,
        compiler_params=pltpu.CompilerParams(vmem_limit_bytes=LIMIT),
        cost_estimate=pl.CostEstimate(flops=flops, bytes_accessed=moved, transcendentals=0),
        name=name,
    )(*args)


def shape(dims, dtype):
    return jax.ShapeDtypeStruct(tuple(dims), dtype)


def shifted(cells, axis, step):
    count = lax.axis_size(axis)
    return lax.ppermute(cells, axis, [(n, n + step) for n in range(count) if 0 <= n + step < count])


def halos(top, bottom, left, right):
    above = shifted(bottom, "row", 1)
    below = shifted(top, "row", -1)

    def column(own, where):
        corner = lambda rows: rows[:, :, where : where + 1] if where == 0 else rows[:, :, -1:]
        return jnp.concatenate([corner(above), own, corner(below)], axis=1)

    from_left = shifted(column(right, -1), "col", 1)
    from_right = shifted(column(left, 0), "col", -1)
    flat = lambda c: c.reshape(c.shape[0], c.shape[1], c.shape[3])
    return above, below, flat(from_left), flat(from_right)


def bits(row_count, col_count):
    steps = [("col", 1)]
    steps += [("row", 1 << n) for n in range(row_count.bit_length() - 1)]
    steps += [("col", 1 << n) for n in range(1, col_count.bit_length() - 1)]
    return steps


def swap(x, axis, step):
    return lax.ppermute(x, axis, [(n, n ^ step) for n in range(lax.axis_size(axis))])


def halving(x, steps):
    for axis, step in steps:
        half = x.shape[0] // 2
        high = (lax.axis_index(axis) // step) % 2 == 1
        give = jnp.where(high, x[:half], x[half:])
        keep = jnp.where(high, x[half:], x[:half])
        got = swap(give, axis, step)
        x = keep.astype(F32) + got.astype(F32)
        if (axis, step) != steps[-1]:
            x = x.astype(BF16)
    return x


def cuts(slots, edge_slots):
    return [0, slots]


def shards(plan, latent, w_qkv, w_out, ln_gain, dw_kernel, grad_out):
    batches, rows, cols, feats = latent.shape
    row_count, col_count = lax.axis_size("row"), lax.axis_size("col")
    cells = batches * rows * cols
    parts = len(plan.rows)
    steps = bits(row_count, col_count)
    gain = ln_gain.reshape(1, feats)
    send = [jnp.asarray(m, BF16) for m in plan.send]
    back = [jnp.asarray(np.ascontiguousarray(m.T), BF16) for m in plan.send]
    sort = [jnp.asarray(m, BF16) for m in plan.sort]
    chunks = [shape((n, feats), BF16) for n in plan.rows]
    trade = lambda x: lax.all_to_all(x, AXES, split_axis=0, concat_axis=0, tiled=True)
    grad_flat = grad_out.reshape(cells, feats)

    grad_sent = call(send_kernel, chunks, [], [grad_flat, *send], 2 * cells * cells * feats, "grad_send")
    grad_win = [trade(x) for x in grad_sent]

    above, below, left, right = halos(latent[:, :1], latent[:, -1:], latent[:, :, :1], latent[:, :, -1:])
    padded = shape((3, batches, rows + 2, cols, feats), BF16)
    side = pltpu.VMEM((batches, rows + 2, feats), F32)
    *normed, mixed, x_shift = call(
        functools.partial(mix_kernel, parts),
        [*chunks, shape(latent.shape, BF16), padded],
        [pltpu.VMEM((cells, feats), BF16), side, side],
        [latent, above, below, left, right, dw_kernel, gain, *send],
        2 * cells * cells * feats,
        "mix",
    )
    normed_win = [trade(x) for x in normed]

    places = []
    for i in range(row_count):
        for j in range(col_count):
            place = 0
            for axis, step in steps:
                place = 2 * place + (((i if axis == "row" else j) // step) & 1)
            places.append(place)
    weights = None
    d_parts = []
    for n in range(parts):
        count = plan.rows[n]
        last = n == parts - 1
        args = [normed_win[n], grad_win[n], sort[n], w_qkv, w_out]
        if weights is not None:
            args.append(weights)
        d_chunk, weights = call(
            functools.partial(window_kernel, weights is None, last, places),
            [chunks[n], shape((feats, 4 * feats), BF16 if last else F32)],
            [
                pltpu.VMEM((count, feats), BF16),
                pltpu.VMEM((count, feats), BF16),
                pltpu.VMEM((count, 3 * feats), BF16),
                pltpu.VMEM((count, feats), BF16),
                pltpu.VMEM((count, feats), BF16),
                pltpu.VMEM((count, 3 * feats), BF16),
                pltpu.VMEM((4 * CELLS, 256), BF16),
                pltpu.VMEM((2 * CELLS, 256), BF16),
                pltpu.VMEM((feats, 4 * feats), F32),
            ],
            args,
            count * feats * feats * 40,
            "windows",
        )
        d_parts.append(trade(d_chunk))

    pick = plan.border_tile
    pick_dn = jnp.asarray(pick @ plan.send[0].T, BF16)
    (border,) = call(
        border_kernel,
        [shape((pick.shape[0], feats), BF16)],
        [],
        [d_parts[0], mixed.reshape(cells, feats), grad_flat, pick_dn, jnp.asarray(pick, BF16), gain],
        6 * cells * pick.shape[0] * feats,
        "border",
    )
    tops, sides = batches * cols, batches * rows
    d_top = border[:tops].reshape(batches, 1, cols, feats)
    d_bottom = border[tops : 2 * tops].reshape(batches, 1, cols, feats)
    d_left = border[2 * tops : 2 * tops + sides].reshape(batches, rows, 1, feats)
    d_right = border[2 * tops + sides :].reshape(batches, rows, 1, feats)
    above, below, left, right = halos(d_top, d_bottom, d_left, d_right)

    grad_latent, sums = call(
        functools.partial(final_kernel, parts),
        [shape(latent.shape, BF16), shape((16, feats), F32)],
        [
            pltpu.VMEM(padded.shape, BF16),
            pltpu.VMEM((cells, feats), F32),
            side,
            side,
        ],
        [*d_parts, *back, mixed, grad_out, x_shift, above, below, left, right, dw_kernel, gain],
        2 * cells * cells * feats,
        "final",
    )
    weights = halving(weights, steps)
    for axis, step in steps:
        sums = sums + swap(sums, axis, step)
    return (
        grad_latent,
        weights[:, : 3 * feats],
        weights[:, 3 * feats :],
        sums[9],
        sums[:9].reshape(3, 3, feats),
    )


def solution(mesh):
    row_count, col_count = mesh.shape["row"], mesh.shape["col"]

    def run(latent, w_qkv, w_out, ln_gain, dw_kernel, grad_out):
        batches, rows, cols, _ = latent.shape
        plan = Plan(batches, rows // row_count, cols // col_count, row_count, col_count, cuts)
        in_specs = (P(None, "row", "col", None), P(), P(), P(), P(), P(None, "row", "col", None))
        out_specs = (
            P(None, "row", "col", None),
            P(AXES, None),
            P(AXES, None),
            P(),
            P(),
        )
        return jax.shard_map(
            functools.partial(shards, plan),
            mesh=mesh,
            in_specs=in_specs,
            out_specs=out_specs,
            check_vma=False,
        )(latent, w_qkv, w_out, ln_gain, dw_kernel, grad_out)

    return run
```

```python
import functools

import jax
import jax.numpy as jnp
import numpy as np
from jax import lax
from jax.experimental import pallas as pl
from jax.experimental.pallas import tpu as pltpu
from jax.sharding import PartitionSpec as P

HEADS = 16
HEAD = 32
GRID = 8
CELLS = GRID * GRID
AXES = ("row", "col")
F32 = jnp.float32
BF16 = jnp.bfloat16
LIMIT = 56 * 1024 * 1024
UNROLL = 2
GROUP = 16


def dot(left, right, dims=((1,), (0,))):
    return lax.dot_general(left, right, (dims, ((), ())), preferred_element_type=F32)


def moves(pairs, sems):
    copies = [pltpu.make_async_copy(a, b, sems.at[n]) for n, (a, b) in enumerate(pairs)]
    for copy in copies:
        copy.start()
    return copies


class Plan:
    def __init__(self, batches, tile_rows, tile_cols, row_count, col_count):
        devices = row_count * col_count
        high = tile_rows * row_count // GRID
        full = tile_cols * col_count // GRID
        wide = min(full, tile_cols)
        groups = full // wide
        reps_r = tile_rows // high
        reps_s = tile_cols // wide
        reps = reps_r * reps_s
        share = devices // batches
        spots = [(a, e) for a in range(high) for e in range(wide)]
        edge = [c for c in spots if c[0] in (0, high - 1) or c[1] in (0, wide - 1)]
        rest = [c for c in spots if c not in set(edge)]
        place = {c: (n % share, n // share) for n, c in enumerate(edge + rest)}
        slots = len(spots) // share
        edge_slots = -(-len(edge) // share)
        bounds = [0, edge_slots, slots] if edge_slots < slots else [0, slots]
        cells = tile_rows * tile_cols

        def build(first, last):
            size = (last - first) * reps
            send = np.zeros((share * size, cells), np.float32)
            for h in range(tile_rows):
                for w in range(tile_cols):
                    owner, slot = place[(h % high, w % wide)]
                    if first <= slot < last:
                        rep = (h // high) * reps_s + w // wide
                        send[owner * size + (slot - first) * reps + rep, h * tile_cols + w] = 1
            count = (last - first) * groups
            seen = np.zeros((count,), np.int64)
            sort = np.zeros((devices * size, devices * size), np.float32)
            for source in range(devices):
                j = source % col_count
                for slot in range(last - first):
                    for r in range(reps_r):
                        for s in range(reps_s):
                            window = slot * groups + ((j * tile_cols + s * wide) % full) // wide
                            position = int(seen[window])
                            seen[window] += 1
                            chunk, lane = divmod(position, GROUP)
                            row = chunk * GROUP * count + window * GROUP + lane
                            sort[row, source * size + slot * reps + r * reps_s + s] = 1
            step = GROUP * count
            block = sort[:step, :step]
            assert (sort == np.kron(np.eye(CELLS // GROUP), block)).all()
            return send, block

        self.send_all, sort_all = build(0, slots)
        self.send, self.sort, self.take = [], [], []
        for first, last in zip(bounds[:-1], bounds[1:]):
            send, block = build(first, last)
            self.send.append(send)
            self.sort.append(block)
            self.take.append(sort_all[first * groups * GROUP : last * groups * GROUP])
        self.rows = [batches * m.shape[0] for m in self.send]
        spots = []
        for h in (0, tile_rows - 1):
            spots += [(b, h, w) for b in range(batches) for w in range(tile_cols)]
        for w in (0, tile_cols - 1):
            spots += [(b, h, w) for b in range(batches) for h in range(tile_rows)]
        self.pick = np.zeros((len(spots), batches * cells), np.float32)
        for n, (b, h, w) in enumerate(spots):
            self.pick[n, b * cells + h * tile_cols + w] = 1
        self.pick_sent = self.pick @ np.kron(np.eye(batches), self.send[0]).T


def send_kernel(batches, x_ref, order, out):
    cells = x_ref.shape[0] // batches
    for b in range(batches):
        at = slice(b * cells, (b + 1) * cells)
        out[at, :] = dot(order[...], x_ref[at, :]).astype(BF16)


def convolve(pad, left_ref, right_ref, kern, side_l, side_r, out_ref):
    batches, rows, cols, feats = pad.shape
    rows -= 2
    four = 4
    width = 256
    for b in range(batches):
        left, right = left_ref[b].astype(F32), right_ref[b].astype(F32)
        side_l[b] = sum(kern[i][0] * left[i : i + rows] for i in range(3))
        side_r[b] = sum(kern[i][2] * right[i : i + rows] for i in range(3))
    spot = lax.broadcasted_iota(jnp.int32, (cols, width), 0)
    for c in range(feats // width):
        at = slice(c * width, (c + 1) * width)
        taps = [[kern[i][j][:, at] for j in range(3)] for i in range(3)]
        for b in range(batches):

            def step(n, carry, b=b, at=at, taps=taps):
                first = n * four
                x = [pad[b, first + r, :, at].astype(F32) for r in range(four + 2)]
                for r in range(four):
                    low, mid, high = (
                        taps[0][j] * x[r] + taps[1][j] * x[r + 1] + taps[2][j] * x[r + 2]
                        for j in range(3)
                    )
                    h = first + r
                    low = jnp.where(spot == 0, side_l[b, pl.ds(h, 1), at], pltpu.roll(low, 1, 0))
                    high = jnp.where(
                        spot == cols - 1, side_r[b, pl.ds(h, 1), at], pltpu.roll(high, cols - 1, 0)
                    )
                    where = pl.ds(pl.multiple_of((b * rows + h) * cols, cols), cols)
                    out_ref[where, at] = (x[r + 1] + (low + mid + high)).astype(BF16)
                return carry

            lax.fori_loop(0, rows // four, step, 0)


def taps_of(dw_ref, flipped):
    side = lambda n: 2 - n if flipped else n
    return [
        [dw_ref[side(i), side(j) : side(j) + 1, :].astype(F32) for j in range(3)] for i in range(3)
    ]


def mix_kernel(lat_ref, top_ref, bot_ref, left_ref, right_ref, dw_ref, gain_ref, order, *refs):
    out, mixed_out, stat_out, pad_out = refs[:4]
    mixed_ref, stat_ref, pad_ref, normed_ref, side_l, side_r, sems = refs[4:]
    batches, rows, cols, feats = lat_ref.shape
    pad_ref[:, 1 : rows + 1] = lat_ref[...]
    pad_ref[:, 0] = top_ref[...]
    pad_ref[:, rows + 1] = bot_ref[...]
    copies = moves([(pad_ref, pad_out)], sems)
    convolve(pad_ref, left_ref, right_ref, taps_of(dw_ref, False), side_l, side_r, mixed_ref)
    copies += moves([(mixed_ref, mixed_out)], sems.at[1:2])
    block = 64

    def norm(n, carry):
        at = pl.ds(pl.multiple_of(n * block, block), block)
        mixed = mixed_ref[at, :].astype(F32)
        mean = jnp.mean(mixed, axis=-1, keepdims=True)
        centred = mixed - mean
        rstd = lax.rsqrt(jnp.mean(centred * centred, axis=-1, keepdims=True) + 1e-05)
        stat_ref[at, 0:1] = mean
        stat_ref[at, 1:2] = rstd
        normed_ref[at, :] = (centred * rstd * gain_ref[...]).astype(BF16)
        return carry

    lax.fori_loop(0, batches * rows * cols // block, norm, 0, unroll=2)
    copies += moves([(stat_ref, stat_out)], sems.at[2:3])
    send_kernel(batches, normed_ref, order, out)
    for copy in copies:
        copy.wait()


def gather_rows(source, take_ref, target):
    count = target.shape[0] // CELLS
    whole = source.shape[0] * GROUP // CELLS
    for p in range(CELLS // GROUP):
        ordered = dot(take_ref[...], source[p * whole : (p + 1) * whole, :]).astype(BF16)
        for w in range(count):
            target[w * CELLS + p * GROUP : w * CELLS + (p + 1) * GROUP, :] = ordered[
                w * GROUP : (w + 1) * GROUP
            ]


def grads_kernel(parts, g_ref, wout_ref, *refs):
    for n in range(parts):
        gw, datt = refs[parts + 2 * n : parts + 2 * n + 2]
        gather_rows(g_ref, refs[n], gw)
        rows = gw.shape[0]
        for first in range(0, rows, 256):
            at = slice(first, min(first + 256, rows))
            datt[at, :] = dot(gw[at, :], wout_ref[...], ((1,), (1,))).astype(BF16)


def window_kernel(counts, before, n_hbm, datt_hbm, take_ref, sort_ref, wqkv_hbm, *refs):
    n_ref, wqkv_ref, nw, packed, datt, att, dpacked, head_mask, half_mask, in_sems = refs[-10:]
    if counts is None:
        dn_ref, *results, out_sems = refs[:5]
    else:
        mine_ref, gw_hbm, *old = refs[: 4 * before + 2]
        dn_ref, keep_hbm, give_hbm, gw, acc, keep_ref, give_ref, out_sems, old_sems, *old_refs = refs[
            4 * before + 2 : -10
        ]
        late = moves([(gw_hbm, gw), *zip(old, old_refs)], old_sems)
    loads = moves([(n_hbm, n_ref), (wqkv_hbm, wqkv_ref), (datt_hbm, datt)], in_sems)
    rows, feats = dn_ref.shape
    count = rows // CELLS
    part = GROUP * count
    tiles = feats // 256
    scale = HEAD ** (-0.5)
    block = 256 if rows % 256 == 0 else CELLS

    head_mask[...] = (
        (lax.broadcasted_iota(jnp.int32, (4 * CELLS, 256), 1) // HEAD) % 4
        == lax.broadcasted_iota(jnp.int32, (4 * CELLS, 256), 0) // CELLS
    ).astype(F32).astype(BF16)
    half_mask[...] = (
        lax.broadcasted_iota(jnp.int32, (2 * CELLS, 256), 1) // 128
        == lax.broadcasted_iota(jnp.int32, (2 * CELLS, 256), 0) // CELLS
    ).astype(F32).astype(BF16)

    loads[0].wait()
    gather_rows(n_ref, take_ref, nw)
    loads[1].wait()

    def project(n, carry):
        at = pl.ds(pl.multiple_of(n * block, block), block)
        packed[at, :] = dot(nw[at, :], wqkv_ref[...]).astype(BF16)
        return carry

    lax.fori_loop(0, rows // block, project, 0)
    loads[2].wait()

    lane = lax.broadcasted_iota(jnp.int32, (CELLS, 256), 1)
    lane_half = lane < 128
    lane_head = (lane // HEAD) % 4

    def fold_heads(full):
        out = full[3 * CELLS :]
        for h in (2, 1, 0):
            out = jnp.where(lane_head == h, full[h * CELLS : (h + 1) * CELLS], out)
        return out

    def one(n, carry):
        at = pl.ds(pl.multiple_of(n * CELLS, CELLS), CELLS)
        for t in range(tiles):
            cols = [slice(p * feats + t * 256, p * feats + (t + 1) * 256) for p in range(3)]
            query = packed[at, cols[0]]
            key = packed[at, cols[1]]
            value = packed[at, cols[2]]
            grad = datt[at, t * 256 : (t + 1) * 256]
            key_big = jnp.concatenate([key] * 4, axis=0) * head_mask[...]
            value_big = jnp.concatenate([value] * 4, axis=0) * head_mask[...]
            query_two = jnp.concatenate([query] * 2, axis=0) * half_mask[...]
            grad_two = jnp.concatenate([grad] * 2, axis=0) * half_mask[...]
            scores = (dot(key_big, query_two, ((1,), (1,))) * scale).reshape(4, CELLS, 2 * CELLS)
            d_probs = dot(value_big, grad_two, ((1,), (1,))).reshape(4, CELLS, 2 * CELLS)
            raised = jnp.exp(scores - jnp.max(scores, axis=1, keepdims=True))
            probs = raised * (1.0 / jnp.sum(raised, axis=1, keepdims=True))
            probs_b = probs.astype(BF16).reshape(4 * CELLS, 2 * CELLS)
            inner = jnp.sum(probs * d_probs, axis=1, keepdims=True)
            d_scores = (
                (probs * (d_probs - inner) * scale).astype(BF16).reshape(4 * CELLS, 2 * CELLS)
            )
            out = dot(probs_b, value_big, ((0,), (0,)))
            att[at, t * 256 : (t + 1) * 256] = jnp.where(
                lane_half, out[:CELLS], out[CELLS:]
            ).astype(BF16)
            d_query = dot(d_scores, key_big, ((0,), (0,)))
            dpacked[at, cols[0]] = jnp.where(
                lane_half, d_query[:CELLS], d_query[CELLS:]
            ).astype(BF16)
            dpacked[at, cols[1]] = fold_heads(dot(d_scores, query_two)).astype(BF16)
            dpacked[at, cols[2]] = fold_heads(dot(probs_b, grad_two)).astype(BF16)
        return carry

    lax.fori_loop(0, count, one, 0, unroll=UNROLL)
    if counts is None:
        stores = moves(list(zip((nw, att, dpacked), results)), out_sems)
    else:
        for copy in late:
            copy.wait()
        parts = [old_refs[4 * n : 4 * n + 4] for n in range(before)] + [(nw, att, dpacked, gw)]
        weight_sums(parts, counts, mine_ref[0], acc, keep_ref, give_ref)
        stores = moves([(give_ref, give_hbm), (keep_ref, keep_hbm)], out_sems)

    def back(n, carry):
        at = pl.ds(pl.multiple_of(n * block, block), block)
        datt[at, :] = dot(dpacked[at, :], wqkv_ref[...], ((1,), (1,))).astype(BF16)
        return carry

    lax.fori_loop(0, rows // block, back, 0)
    for p in range(CELLS // GROUP):
        ordered = jnp.concatenate(
            [
                datt[w * CELLS + p * GROUP : w * CELLS + (p + 1) * GROUP, :]
                for w in range(count)
            ],
            axis=0,
        )
        dn_ref[p * part : (p + 1) * part, :] = dot(
            sort_ref[...], ordered, ((0,), (0,))
        ).astype(BF16)
    for copy in stores:
        copy.wait()


def place_of(i, j, row_count, chips):
    return (j % 2) * row_count * chips + i * chips + j // 2


def weight_sums(parts, counts, mine, acc, keep_ref, give_ref):
    feats = acc.shape[0]
    row_count, chips = counts
    devices = 2 * row_count * chips
    size = feats // devices
    half = devices // 2
    for left, right, start in ((0, 2, 0), (1, 3, 3 * feats)):
        turned = [part[left][...].T for part in parts]
        for t in range(parts[0][right].shape[1] // 256):
            at = slice(t * 256, (t + 1) * 256)
            acc[:, start + t * 256 : start + (t + 1) * 256] = sum(
                dot(x, part[right][:, at]) for x, part in zip(turned, parts)
            ).astype(BF16)
    if size % 16:
        source = lax.broadcasted_iota(jnp.int32, (feats, feats), 1)
        device = source // size
        place = place_of(device // (2 * chips), device % (2 * chips), row_count, chips)
        target = jnp.bitwise_xor(mine, place) * size + source % size
        order = (lax.broadcasted_iota(jnp.int32, (feats, feats), 0) == target).astype(F32).astype(BF16)
        keep_ref[...] = dot(order[: feats // 2], acc[...]).astype(BF16)
        give_ref[...] = dot(order[feats // 2 :], acc[...]).astype(BF16)
        return
    for n in range(devices):
        place = place_of(n // (2 * chips), n % (2 * chips), row_count, chips)
        block = jnp.bitwise_xor(mine, place)
        rows = acc[n * size : (n + 1) * size, :]
        at = pl.ds(pl.multiple_of((block % half) * size, size), size)

        @pl.when(block < half)
        def _(rows=rows, at=at):
            keep_ref[at, :] = rows

        @pl.when(block >= half)
        def _(rows=rows, at=at):
            give_ref[at, :] = rows


def norm_back(d_normed, nhat, rstd, grad, gain):
    scaled = d_normed * gain
    return (
        grad.astype(F32)
        + rstd
        * (
            scaled
            - jnp.mean(scaled, axis=-1, keepdims=True)
            - nhat * jnp.mean(scaled * nhat, axis=-1, keepdims=True)
        )
    ).astype(BF16)


def border_kernel(dn_ref, mixed_ref, grad_ref, pick_sent_ref, pick_ref, gain_ref, *outs):
    d_normed = dot(pick_sent_ref[...], dn_ref[...])
    mixed = dot(pick_ref[...], mixed_ref[...])
    grad = dot(pick_ref[...], grad_ref[...])
    centred = mixed - jnp.mean(mixed, axis=-1, keepdims=True)
    rstd = lax.rsqrt(jnp.mean(centred * centred, axis=-1, keepdims=True) + 1e-05)
    d_mixed = norm_back(d_normed, centred * rstd, rstd, grad, gain_ref[...])
    start = 0
    for out in outs:
        out[...] = d_mixed[start : start + out.shape[0]]
        start += out.shape[0]


def sums_kernel(count, *refs):
    parts, orders, refs = refs[:count], refs[count : 2 * count], refs[2 * count :]
    hbm, (left_ref, right_ref, gain_ref) = refs[:4], refs[4:7]
    out_ref, sums_ref, dn, side_l, side_r = refs[7:12]
    here, sems = refs[12:16], refs[16]
    stat_ref, mixed_ref, grad_ref, pad_ref = here
    loads = moves(list(zip(hbm, here)), sems)
    batches, rows, cols, feats = pad_ref.shape
    rows -= 2
    cells = rows * cols
    for b in range(batches):
        total = None
        for order, part in zip(orders, parts):
            size = part.shape[0] // batches
            term = dot(order[...], part[b * size : (b + 1) * size, :])
            total = term if total is None else total + term
        dn[b * cells : (b + 1) * cells, :] = total
    block = 64
    for copy in loads[:3]:
        copy.wait()

    def norm(n, gain_sum):
        at = pl.ds(pl.multiple_of(n * block, block), block)
        d_normed = dn[at, :]
        rstd = stat_ref[at, 1:2]
        nhat = (mixed_ref[at, :].astype(F32) - stat_ref[at, 0:1]) * rstd
        out_ref[at, :] = norm_back(d_normed, nhat, rstd, grad_ref[at, :], gain_ref[...])
        return gain_sum + jnp.sum((d_normed * nhat).reshape(block // 8, 8, feats), axis=0)

    gain_sum = lax.fori_loop(
        0, batches * cells // block, norm, jnp.zeros((8, feats), F32), unroll=2
    )
    sums_ref[9:10, :] = jnp.sum(gain_sum, axis=0, keepdims=True)
    sums_ref[10:, :] = jnp.zeros((sums_ref.shape[0] - 10, feats), F32)
    loads[3].wait()

    four = 4
    width = 256
    spot = lax.broadcasted_iota(jnp.int32, (cols, width), 0)
    fold = lambda v: jnp.sum(v.reshape(cols // 8, 8, width), axis=0)
    for c in range(feats // width):
        lanes = slice(c * width, (c + 1) * width)
        sums = [jnp.zeros((8, width), F32) for _ in range(9)]
        for b in range(batches):

            def step(n, sums, b=b, lanes=lanes):
                start = n * four
                x = [pad_ref[b, start + r, :, lanes].astype(F32) for r in range(four + 2)]
                sums = list(sums)
                for r in range(four):
                    h = start + r
                    at = pl.ds(pl.multiple_of((b * rows + h) * cols, cols), cols)
                    d_mixed = out_ref[at, lanes].astype(F32)
                    side_l[b, pl.ds(h, 1), lanes] = d_mixed[:1]
                    side_r[b, pl.ds(h, 1), lanes] = d_mixed[cols - 1 :]
                    moved = (
                        jnp.where(spot == cols - 1, 0.0, pltpu.roll(d_mixed, cols - 1, 0)),
                        d_mixed,
                        jnp.where(spot == 0, 0.0, pltpu.roll(d_mixed, 1, 0)),
                    )
                    for i in range(3):
                        for j in range(3):
                            sums[3 * i + j] = sums[3 * i + j] + fold(moved[j] * x[r + i])
                return tuple(sums)

            sums = lax.fori_loop(0, rows // four, step, tuple(sums))
        for n in range(9):
            sums_ref[n : n + 1, lanes] = jnp.sum(sums[n], axis=0, keepdims=True)
    for i in range(3):
        for b in range(batches):
            left, right = left_ref[b].astype(F32), right_ref[b].astype(F32)
            sums_ref[3 * i : 3 * i + 1, :] += jnp.sum(
                side_l[b] * left[i : i + rows], axis=0, keepdims=True
            )
            sums_ref[3 * i + 2 : 3 * i + 3, :] += jnp.sum(
                side_r[b] * right[i : i + rows], axis=0, keepdims=True
            )


def spread_kernel(d_ref, top_ref, bot_ref, left_ref, right_ref, dw_ref, out_ref, pad, side_l, side_r):
    batches, rows, cols, feats = pad.shape
    rows -= 2
    for b in range(batches):
        for h in range(rows):
            pad[b, h + 1] = d_ref[(b * rows + h) * cols : (b * rows + h + 1) * cols, :]
    pad[:, 0] = top_ref[...]
    pad[:, rows + 1] = bot_ref[...]
    convolve(pad, left_ref, right_ref, taps_of(dw_ref, True), side_l, side_r, out_ref)


def call(body, outs, scratch, args, micros, name, hbm_ins=(), hbm_outs=(), scalars=()):
    moved = sum(int(np.prod(o.shape)) * o.dtype.itemsize for o in (*outs, *args))
    vmem = pl.BlockSpec(memory_space=pltpu.VMEM)
    hbm = pl.BlockSpec(memory_space=pl.ANY)
    smem = pl.BlockSpec(memory_space=pltpu.SMEM)
    return pl.pallas_call(
        body,
        out_shape=outs,
        in_specs=[
            smem if n in scalars else hbm if n in hbm_ins else vmem for n in range(len(args))
        ],
        out_specs=[hbm if n in hbm_outs else vmem for n in range(len(outs))],
        scratch_shapes=scratch,
        compiler_params=pltpu.CompilerParams(vmem_limit_bytes=LIMIT),
        cost_estimate=pl.CostEstimate(
            flops=micros * 10**9, bytes_accessed=moved, transcendentals=0
        ),
        name=name,
    )(*args)


def shape(dims, dtype):
    return jax.ShapeDtypeStruct(tuple(dims), dtype)


def shifted(cells, axis, step):
    count = lax.axis_size(axis)
    return lax.ppermute(cells, axis, [(n, n + step) for n in range(count) if 0 <= n + step < count])


def halos(top, bottom, left, right):
    above = shifted(bottom, "row", 1)
    below = shifted(top, "row", -1)
    last = above.shape[1] - 1
    column = lambda own, at: jnp.concatenate(
        [above[:, at : at + 1], own, below[:, at : at + 1]], axis=1
    )
    from_left = shifted(column(right, last), "col", 1)
    from_right = shifted(column(left, 0), "col", -1)
    return above, below, from_left, from_right


def swap(x, axis, step):
    return lax.ppermute(x, axis, [(n, n ^ step) for n in range(lax.axis_size(axis))])


def total(values):
    while len(values) > 1:
        values = [a + b for a, b in zip(values[::2], values[1::2])]
    return values[0]


def scatter(blocks, sums, axis, unit, count):
    size = blocks.shape[0] // count
    sums = sums.reshape(size, -1)
    load = lambda n: jnp.concatenate([blocks[n * size : (n + 1) * size], sums], axis=1).astype(BF16)
    own = jnp.concatenate([blocks[:size], sums], axis=1)
    return [own, *(swap(load(n), axis, unit * n).astype(F32) for n in range(1, count))]


def shards(plan, latent, w_qkv, w_out, ln_gain, dw_kernel, grad_out):
    batches, rows, cols, feats = latent.shape
    row_count, col_count = lax.axis_size("row"), lax.axis_size("col")
    cells = batches * rows * cols
    parts = len(plan.rows)
    gain = ln_gain.reshape(1, feats)
    send = jnp.asarray(plan.send_all, BF16)
    back = [jnp.asarray(np.ascontiguousarray(m.T), BF16) for m in plan.send]
    sort = [jnp.asarray(m, BF16) for m in plan.sort]
    take = [jnp.asarray(m, BF16) for m in plan.take]
    chunks = [shape((n, feats), BF16) for n in plan.rows]
    trade = lambda x: lax.all_to_all(x, AXES, split_axis=0, concat_axis=0, tiled=True)
    grad_flat = grad_out.reshape(cells, feats)

    flat = shape((cells, feats), BF16)
    (grad_sent,) = call(
        functools.partial(send_kernel, batches), [flat], [], [grad_flat, send], 3, "grad_send"
    )
    grad_win = trade(grad_sent)

    above, below, left, right = halos(latent[:, 0], latent[:, -1], latent[:, :, 0], latent[:, :, -1])
    padded = (batches, rows + 2, cols, feats)
    side = pltpu.VMEM((batches, rows, feats), F32)
    stat_shape = (cells, 2)
    normed, mixed, stat, pad = call(
        mix_kernel,
        [flat, flat, shape(stat_shape, F32), shape(padded, BF16)],
        [
            pltpu.VMEM((cells, feats), BF16),
            pltpu.VMEM(stat_shape, F32),
            pltpu.VMEM(padded, BF16),
            pltpu.VMEM((cells, feats), BF16),
            side,
            side,
            pltpu.SemaphoreType.DMA((3,)),
        ],
        [latent, above, below, left, right, dw_kernel, gain, send],
        6,
        "mix",
        hbm_outs=(1, 2, 3),
    )
    normed_win = trade(normed)

    chips = col_count // 2
    ahead = call(
        functools.partial(grads_kernel, parts),
        [chunks[n // 2] for n in range(2 * parts)],
        [],
        [grad_win, w_out, *take],
        4,
        "grads",
    )
    mine = place_of(lax.axis_index("row"), lax.axis_index("col"), row_count, chips).astype(jnp.int32).reshape(1)
    half = shape((feats // 2, 4 * feats), BF16)
    d_parts, kept = [], []
    for n in range(parts):
        count = plan.rows[n]
        last = n == parts - 1
        mat = lambda width: pltpu.VMEM((count, width), BF16)
        args = [normed_win, ahead[2 * n + 1], take[n], sort[n], w_qkv]
        if last:
            outs = [chunks[n], half, half]
            args += [mine, ahead[2 * n], *kept]
            scratch = [
                mat(feats),
                pltpu.VMEM((feats, 4 * feats), BF16),
                pltpu.VMEM(half.shape, BF16),
                pltpu.VMEM(half.shape, BF16),
                pltpu.SemaphoreType.DMA((2,)),
                pltpu.SemaphoreType.DMA((1 + len(kept),)),
                *(pltpu.VMEM(x.shape, BF16) for x in kept),
            ]
        else:
            outs = [chunks[n], chunks[n], chunks[n], shape((count, 3 * feats), BF16)]
            scratch = [pltpu.SemaphoreType.DMA((3,))]
        d_chunk, *saved = call(
            functools.partial(window_kernel, (row_count, chips) if last else None, n),
            outs,
            [
                *scratch,
                pltpu.VMEM((cells, feats), BF16),
                pltpu.VMEM((feats, 3 * feats), BF16),
                mat(feats),
                mat(3 * feats),
                mat(feats),
                mat(feats),
                mat(3 * feats),
                pltpu.VMEM((4 * CELLS, 256), BF16),
                pltpu.VMEM((2 * CELLS, 256), BF16),
                pltpu.SemaphoreType.DMA((3,)),
            ],
            args,
            2 + 20 * count // sum(plan.rows),
            "windows",
            hbm_ins=(0, 1, 4, *range(6, len(args))),
            hbm_outs=tuple(range(1, len(outs))),
            scalars=(5,),
        )
        kept += [*saved, ahead[2 * n]]
        d_parts.append(trade(d_chunk))
    keep, give = saved

    tops, sides = batches * cols, batches * rows
    borders = call(
        border_kernel,
        [shape((n, feats), BF16) for n in (tops, tops, sides, sides)],
        [],
        [
            d_parts[0],
            mixed,
            grad_flat,
            jnp.asarray(plan.pick_sent, BF16),
            jnp.asarray(plan.pick, BF16),
            gain,
        ],
        3,
        "border",
    )
    d_halos = halos(*(x.reshape(batches, -1, feats) for x in borders))

    weights = (keep.astype(F32) + swap(give, "col", 1).astype(F32)).astype(BF16)
    *d_parts, above, below, from_left, from_right = lax.optimization_barrier((*d_parts, *d_halos))
    d_halos = (above, below, from_left, from_right)
    d_mixed, sums = call(
        functools.partial(sums_kernel, parts),
        [flat, shape((16, feats), F32)],
        [
            pltpu.VMEM((cells, feats), F32),
            side,
            side,
            pltpu.VMEM(stat_shape, F32),
            pltpu.VMEM((cells, feats), BF16),
            pltpu.VMEM((cells, feats), BF16),
            pltpu.VMEM(padded, BF16),
            pltpu.SemaphoreType.DMA((4,)),
        ],
        [*d_parts, *back, stat, mixed, grad_flat, pad, left, right, gain],
        7,
        "sums",
        hbm_ins=tuple(range(2 * parts, 2 * parts + 4)),
    )
    (grad_latent,) = call(
        spread_kernel,
        [flat],
        [pltpu.VMEM(padded, BF16), side, side],
        [d_mixed, *d_halos, dw_kernel],
        5,
        "spread",
    )
    wide = 4 * feats
    size = weights.shape[0] // row_count
    gives = [
        swap(weights[n * size : (n + 1) * size], "row", n).astype(F32) for n in range(1, row_count)
    ]
    weights = total([weights[:size].astype(F32), *gives])
    sums = sums + swap(sums, "col", 1)
    sums = total([sums, *(swap(sums, "row", n) for n in range(1, row_count))])
    level = scatter(weights, sums, "col", 2, chips)
    part = lambda first, last: total([x[:, first:last] for x in level])
    sums = part(wide, None).reshape(16, feats)
    return (
        grad_latent.reshape(latent.shape),
        part(0, 3 * feats),
        part(3 * feats, wide),
        sums[9],
        sums[:9].reshape(3, 3, feats),
    )


def solution(mesh):
    row_count, col_count = mesh.shape["row"], mesh.shape["col"]

    def run(latent, w_qkv, w_out, ln_gain, dw_kernel, grad_out):
        batches, rows, cols, _ = latent.shape
        plan = Plan(batches, rows // row_count, cols // col_count, row_count, col_count)
        in_specs = (P(None, "row", "col", None), P(), P(), P(), P(), P(None, "row", "col", None))
        out_specs = (
            P(None, "row", "col", None),
            P(AXES, None),
            P(AXES, None),
            P(),
            P(),
        )
        return jax.shard_map(
            functools.partial(shards, plan),
            mesh=mesh,
            in_specs=in_specs,
            out_specs=out_specs,
            check_vma=False,
        )(latent, w_qkv, w_out, ln_gain, dw_kernel, grad_out)

    return run
```

```python
import functools

import jax
import jax.numpy as jnp
import numpy as np
from jax import lax
from jax.experimental import pallas as pl
from jax.experimental.pallas import tpu as pltpu
from jax.sharding import PartitionSpec as P

HEADS = 16
HEAD = 32
GRID = 8
CELLS = GRID * GRID
AXES = ("row", "col")
F32 = jnp.float32
BF16 = jnp.bfloat16
LIMIT = 56 * 1024 * 1024
UNROLL = 2
GROUP = 16


def dot(left, right, dims=((1,), (0,))):
    return lax.dot_general(left, right, (dims, ((), ())), preferred_element_type=F32)


def moves(pairs, sems):
    copies = [pltpu.make_async_copy(a, b, sems.at[n]) for n, (a, b) in enumerate(pairs)]
    for copy in copies:
        copy.start()
    return copies


class Plan:
    def __init__(self, batches, tile_rows, tile_cols, row_count, col_count):
        devices = row_count * col_count
        high = tile_rows * row_count // GRID
        full = tile_cols * col_count // GRID
        wide = min(full, tile_cols)
        groups = full // wide
        reps_r = tile_rows // high
        reps_s = tile_cols // wide
        reps = reps_r * reps_s
        share = devices // batches
        spots = [(a, e) for a in range(high) for e in range(wide)]
        cells = tile_rows * tile_cols
        ring = [
            [(-1, w) for w in range(tile_cols)],
            [(tile_rows, w) for w in range(tile_cols)],
            [(h, -1) for h in range(-1, tile_rows + 1)],
            [(h, tile_cols) for h in range(-1, tile_rows + 1)],
        ]

        def home(h, w):
            down, right = h // tile_rows, w // tile_cols
            h, w = h % tile_rows, w % tile_cols
            return down, right, (h % high, w % wide), (h // high) * reps_s + w // wide

        wanted = {c: [] for c in spots}
        for piece, members in enumerate(ring):
            for n, cell in enumerate(members):
                wanted[home(*cell)[2]].append((piece, n))
        edge = sorted((c for c in spots if wanted[c]), key=lambda c: -len(wanted[c]))
        slots = len(spots) // share
        edge_slots = -(-len(edge) // share)
        assert edge_slots < slots
        bounds = [0, edge_slots, slots]
        place, filled, load = {}, [0] * share, [0] * share
        for c in edge:
            owner = min((n for n in range(share) if filled[n] < edge_slots), key=lambda n: load[n])
            place[c] = (owner, filled[owner])
            filled[owner] += 1
            load[owner] += len(wanted[c])
        for c in spots:
            if c not in place:
                owner = min(range(share), key=lambda n: filled[n])
                place[c] = (owner, filled[owner])
                filled[owner] += 1

        def build(first, last):
            size = (last - first) * reps
            send = np.zeros((share * size, cells), np.float32)
            for h in range(tile_rows):
                for w in range(tile_cols):
                    owner, slot = place[(h % high, w % wide)]
                    if first <= slot < last:
                        rep = (h // high) * reps_s + w // wide
                        send[owner * size + (slot - first) * reps + rep, h * tile_cols + w] = 1
            count = (last - first) * groups
            seen = np.zeros((count,), np.int64)
            where = {}
            sort = np.zeros((devices * size, devices * size), np.float32)
            for source in range(devices):
                j = source % col_count
                for slot in range(last - first):
                    for r in range(reps_r):
                        for s in range(reps_s):
                            window = slot * groups + ((j * tile_cols + s * wide) % full) // wide
                            position = int(seen[window])
                            seen[window] += 1
                            chunk, lane = divmod(position, GROUP)
                            row = chunk * GROUP * count + window * GROUP + lane
                            where[source, slot, r * reps_s + s] = window * CELLS + position
                            sort[row, source * size + slot * reps + r * reps_s + s] = 1
            step = GROUP * count
            block = sort[:step, :step]
            assert (sort == np.kron(np.eye(CELLS // GROUP), block)).all()
            return send, block, where

        self.send_all, sort_all, _ = build(0, slots)
        self.send, self.sort, self.take = [], [], []
        for first, last in zip(bounds[:-1], bounds[1:]):
            send, block, where = build(first, last)
            if first == 0:
                around = where
            self.send.append(send)
            self.sort.append(block)
            self.take.append(sort_all[first * groups * GROUP : last * groups * GROUP])
        own = edge_slots * reps
        size = own + -(-max(load) // 8) * 8
        size = -(-size // 8) * 8
        back = np.zeros((share * size, cells), np.float32)
        for n in range(share):
            back[n * size : n * size + own] = self.send[0][n * own : (n + 1) * own]
        self.send[0] = back
        self.pieces = [np.zeros((len(members), share * size), np.float32) for members in ring]
        self.index = np.full((share, 1, devices * size), -1, np.int32)
        used = [own] * share
        for source, slot, rep in around:
            self.index[:, 0, source * size + slot * reps + rep] = around[source, slot, rep]
        for c in edge:
            owner, slot = place[c]
            for piece, n in wanted[c]:
                down, right, _, rep = home(*ring[piece][n])
                self.pieces[piece][n, owner * size + used[owner]] = 1
                for i in range(row_count):
                    for j in range(col_count):
                        if 0 <= i + down < row_count and 0 <= j + right < col_count:
                            source = (i + down) * col_count + j + right
                            target = (i * col_count + j) * size + used[owner]
                            self.index[owner, 0, target] = around[source, slot, rep]
                used[owner] += 1
        self.share = share
        self.windows = [m.shape[0] // GROUP for m in self.sort]
        self.rows = [batches * m.shape[0] for m in self.send]


def send_kernel(batches, x_ref, order, out):
    cells = x_ref.shape[0] // batches
    for b in range(batches):
        at = slice(b * cells, (b + 1) * cells)
        out[at, :] = dot(order[...], x_ref[at, :]).astype(BF16)


def convolve(pad, left_ref, right_ref, kern, side_l, side_r, out_ref):
    batches, rows, cols, feats = pad.shape
    rows -= 2
    four = 4
    width = 256
    for b in range(batches):
        left, right = left_ref[b].astype(F32), right_ref[b].astype(F32)
        side_l[b] = sum(kern[i][0] * left[i : i + rows] for i in range(3))
        side_r[b] = sum(kern[i][2] * right[i : i + rows] for i in range(3))
    spot = lax.broadcasted_iota(jnp.int32, (cols, width), 0)
    for c in range(feats // width):
        at = slice(c * width, (c + 1) * width)
        taps = [[kern[i][j][:, at] for j in range(3)] for i in range(3)]
        for b in range(batches):

            def step(n, carry, b=b, at=at, taps=taps):
                first = n * four
                x = [pad[b, first + r, :, at].astype(F32) for r in range(four + 2)]
                for r in range(four):
                    low, mid, high = (
                        taps[0][j] * x[r] + taps[1][j] * x[r + 1] + taps[2][j] * x[r + 2]
                        for j in range(3)
                    )
                    h = first + r
                    low = jnp.where(spot == 0, side_l[b, pl.ds(h, 1), at], pltpu.roll(low, 1, 0))
                    high = jnp.where(
                        spot == cols - 1, side_r[b, pl.ds(h, 1), at], pltpu.roll(high, cols - 1, 0)
                    )
                    where = pl.ds(pl.multiple_of((b * rows + h) * cols, cols), cols)
                    out_ref[where, at] = (x[r + 1] + (low + mid + high)).astype(BF16)
                return carry

            lax.fori_loop(0, rows // four, step, 0)


def taps_of(dw_ref, flipped):
    side = lambda n: 2 - n if flipped else n
    return [
        [dw_ref[side(i), side(j) : side(j) + 1, :].astype(F32) for j in range(3)] for i in range(3)
    ]


def mix_kernel(lat_ref, top_ref, bot_ref, left_ref, right_ref, dw_ref, gain_ref, order, *refs):
    out, mixed_out, stat_out, pad_out = refs[:4]
    mixed_ref, stat_ref, pad_ref, normed_ref, side_l, side_r, sems = refs[4:]
    batches, rows, cols, feats = lat_ref.shape
    pad_ref[:, 1 : rows + 1] = lat_ref[...]
    pad_ref[:, 0] = top_ref[...]
    pad_ref[:, rows + 1] = bot_ref[...]
    copies = moves([(pad_ref, pad_out)], sems)
    convolve(pad_ref, left_ref, right_ref, taps_of(dw_ref, False), side_l, side_r, mixed_ref)
    copies += moves([(mixed_ref, mixed_out)], sems.at[1:2])
    block = 64

    def norm(n, carry):
        at = pl.ds(pl.multiple_of(n * block, block), block)
        mixed = mixed_ref[at, :].astype(F32)
        mean = jnp.mean(mixed, axis=-1, keepdims=True)
        centred = mixed - mean
        rstd = lax.rsqrt(jnp.mean(centred * centred, axis=-1, keepdims=True) + 1e-05)
        stat_ref[at, 0:1] = mean
        stat_ref[at, 1:2] = rstd
        normed_ref[at, :] = (centred * rstd * gain_ref[...]).astype(BF16)
        return carry

    lax.fori_loop(0, batches * rows * cols // block, norm, 0, unroll=2)
    copies += moves([(stat_ref, stat_out)], sems.at[2:3])
    send_kernel(batches, normed_ref, order, out)
    for copy in copies:
        copy.wait()


def gather_rows(source, take_ref, target):
    count = target.shape[0] // CELLS
    whole = source.shape[0] * GROUP // CELLS
    for p in range(CELLS // GROUP):
        ordered = dot(take_ref[...], source[p * whole : (p + 1) * whole, :]).astype(BF16)
        for w in range(count):
            target[w * CELLS + p * GROUP : w * CELLS + (p + 1) * GROUP, :] = ordered[
                w * GROUP : (w + 1) * GROUP
            ]


def grads_kernel(parts, g_ref, wout_ref, *refs):
    for n in range(parts):
        gw, datt = refs[parts + 2 * n : parts + 2 * n + 2]
        gather_rows(g_ref, refs[n], gw)
        rows = gw.shape[0]
        for first in range(0, rows, 256):
            at = slice(first, min(first + 256, rows))
            datt[at, :] = dot(gw[at, :], wout_ref[...], ((1,), (1,))).astype(BF16)


def window_kernel(counts, before, n_hbm, datt_hbm, take_ref, back_ref, wqkv_hbm, *refs):
    n_ref, wqkv_ref, nw, packed, datt, att, dpacked, head_mask, half_mask, in_sems = refs[-10:]
    if counts is None:
        dn_ref, *results, out_sems = refs[:5]
    else:
        mine_ref, gw_hbm, *old = refs[: 4 * before + 2]
        dn_ref, keep_hbm, give_hbm, gw, acc, keep_ref, give_ref, out_sems, old_sems, *old_refs = refs[
            4 * before + 2 : -10
        ]
        late = moves([(gw_hbm, gw), *zip(old, old_refs)], old_sems)
    loads = moves([(n_hbm, n_ref), (wqkv_hbm, wqkv_ref), (datt_hbm, datt)], in_sems)
    rows, feats = nw.shape
    count = rows // CELLS
    part = GROUP * count
    tiles = feats // 256
    scale = HEAD ** (-0.5)
    block = 256 if rows % 256 == 0 else CELLS

    head_mask[...] = (
        (lax.broadcasted_iota(jnp.int32, (4 * CELLS, 256), 1) // HEAD) % 4
        == lax.broadcasted_iota(jnp.int32, (4 * CELLS, 256), 0) // CELLS
    ).astype(F32).astype(BF16)
    half_mask[...] = (
        lax.broadcasted_iota(jnp.int32, (2 * CELLS, 256), 1) // 128
        == lax.broadcasted_iota(jnp.int32, (2 * CELLS, 256), 0) // CELLS
    ).astype(F32).astype(BF16)

    loads[0].wait()
    gather_rows(n_ref, take_ref, nw)
    loads[1].wait()

    def project(n, carry):
        at = pl.ds(pl.multiple_of(n * block, block), block)
        packed[at, :] = dot(nw[at, :], wqkv_ref[...]).astype(BF16)
        return carry

    lax.fori_loop(0, rows // block, project, 0)
    loads[2].wait()

    lane = lax.broadcasted_iota(jnp.int32, (CELLS, 256), 1)
    lane_half = lane < 128
    lane_head = (lane // HEAD) % 4

    def fold_heads(full):
        out = full[3 * CELLS :]
        for h in (2, 1, 0):
            out = jnp.where(lane_head == h, full[h * CELLS : (h + 1) * CELLS], out)
        return out

    def one(n, carry):
        at = pl.ds(pl.multiple_of(n * CELLS, CELLS), CELLS)
        for t in range(tiles):
            cols = [slice(p * feats + t * 256, p * feats + (t + 1) * 256) for p in range(3)]
            query = packed[at, cols[0]]
            key = packed[at, cols[1]]
            value = packed[at, cols[2]]
            grad = datt[at, t * 256 : (t + 1) * 256]
            key_big = jnp.concatenate([key] * 4, axis=0) * head_mask[...]
            value_big = jnp.concatenate([value] * 4, axis=0) * head_mask[...]
            query_two = jnp.concatenate([query] * 2, axis=0) * half_mask[...]
            grad_two = jnp.concatenate([grad] * 2, axis=0) * half_mask[...]
            scores = (dot(key_big, query_two, ((1,), (1,))) * scale).reshape(4, CELLS, 2 * CELLS)
            d_probs = dot(value_big, grad_two, ((1,), (1,))).reshape(4, CELLS, 2 * CELLS)
            raised = jnp.exp(scores - jnp.max(scores, axis=1, keepdims=True))
            probs = raised * (1.0 / jnp.sum(raised, axis=1, keepdims=True))
            probs_b = probs.astype(BF16).reshape(4 * CELLS, 2 * CELLS)
            inner = jnp.sum(probs * d_probs, axis=1, keepdims=True)
            d_scores = (
                (probs * (d_probs - inner) * scale).astype(BF16).reshape(4 * CELLS, 2 * CELLS)
            )
            out = dot(probs_b, value_big, ((0,), (0,)))
            att[at, t * 256 : (t + 1) * 256] = jnp.where(
                lane_half, out[:CELLS], out[CELLS:]
            ).astype(BF16)
            d_query = dot(d_scores, key_big, ((0,), (0,)))
            dpacked[at, cols[0]] = jnp.where(
                lane_half, d_query[:CELLS], d_query[CELLS:]
            ).astype(BF16)
            dpacked[at, cols[1]] = fold_heads(dot(d_scores, query_two)).astype(BF16)
            dpacked[at, cols[2]] = fold_heads(dot(probs_b, grad_two)).astype(BF16)
        return carry

    lax.fori_loop(0, count, one, 0, unroll=UNROLL)
    if counts is None:
        stores = moves(list(zip((nw, att, dpacked), results)), out_sems)
    else:
        for copy in late:
            copy.wait()
        parts = [old_refs[4 * n : 4 * n + 4] for n in range(before)] + [(nw, att, dpacked, gw)]
        weight_sums(parts, counts, mine_ref[0], acc, keep_ref, give_ref)
        stores = moves([(give_ref, give_hbm), (keep_ref, keep_hbm)], out_sems)

    def back(n, carry):
        at = pl.ds(pl.multiple_of(n * block, block), block)
        datt[at, :] = dot(dpacked[at, :], wqkv_ref[...], ((1,), (1,))).astype(BF16)
        return carry

    lax.fori_loop(0, rows // block, back, 0)
    if back_ref.shape[0] == 1:
        order = (
            lax.broadcasted_iota(jnp.int32, (rows, dn_ref.shape[0]), 0) == back_ref[...]
        ).astype(F32).astype(BF16)
        dn_ref[...] = dot(order, datt[...], ((0,), (0,))).astype(BF16)
    else:
        for p in range(CELLS // GROUP):
            ordered = jnp.concatenate(
                [
                    datt[w * CELLS + p * GROUP : w * CELLS + (p + 1) * GROUP, :]
                    for w in range(count)
                ],
                axis=0,
            )
            dn_ref[p * part : (p + 1) * part, :] = dot(
                back_ref[...], ordered, ((0,), (0,))
            ).astype(BF16)
    for copy in stores:
        copy.wait()


def place_of(i, j, row_count, chips):
    return (j % 2) * row_count * chips + i * chips + j // 2


def weight_sums(parts, counts, mine, acc, keep_ref, give_ref):
    feats = acc.shape[0]
    row_count, chips = counts
    devices = 2 * row_count * chips
    size = feats // devices
    half = devices // 2
    for left, right, start in ((0, 2, 0), (1, 3, 3 * feats)):
        turned = [part[left][...].T for part in parts]
        for t in range(parts[0][right].shape[1] // 256):
            at = slice(t * 256, (t + 1) * 256)
            acc[:, start + t * 256 : start + (t + 1) * 256] = sum(
                dot(x, part[right][:, at]) for x, part in zip(turned, parts)
            ).astype(BF16)
    if size % 16:
        source = lax.broadcasted_iota(jnp.int32, (feats, feats), 1)
        device = source // size
        place = place_of(device // (2 * chips), device % (2 * chips), row_count, chips)
        target = jnp.bitwise_xor(mine, place) * size + source % size
        order = (lax.broadcasted_iota(jnp.int32, (feats, feats), 0) == target).astype(F32).astype(BF16)
        keep_ref[...] = dot(order[: feats // 2], acc[...]).astype(BF16)
        give_ref[...] = dot(order[feats // 2 :], acc[...]).astype(BF16)
        return
    for n in range(devices):
        place = place_of(n // (2 * chips), n % (2 * chips), row_count, chips)
        block = jnp.bitwise_xor(mine, place)
        rows = acc[n * size : (n + 1) * size, :]
        at = pl.ds(pl.multiple_of((block % half) * size, size), size)

        @pl.when(block < half)
        def _(rows=rows, at=at):
            keep_ref[at, :] = rows

        @pl.when(block >= half)
        def _(rows=rows, at=at):
            give_ref[at, :] = rows


def norm_back(d_normed, nhat, rstd, grad, gain):
    scaled = d_normed * gain
    return (
        grad.astype(F32)
        + rstd
        * (
            scaled
            - jnp.mean(scaled, axis=-1, keepdims=True)
            - nhat * jnp.mean(scaled * nhat, axis=-1, keepdims=True)
        )
    ).astype(BF16)


def border_kernel(dn_ref, gain_ref, *refs):
    batches = refs[4].shape[0]
    feats = dn_ref.shape[1]
    size = dn_ref.shape[0] // batches
    for pick, pair, out in zip(refs[:4], refs[4:8], refs[8:]):
        for b in range(batches):
            d_normed = dot(pick[...], dn_ref[b * size : (b + 1) * size, :])
            mixed = pair[b, :, :feats].astype(F32)
            centred = mixed - jnp.mean(mixed, axis=-1, keepdims=True)
            rstd = lax.rsqrt(jnp.mean(centred * centred, axis=-1, keepdims=True) + 1e-05)
            out[b] = norm_back(d_normed, centred * rstd, rstd, pair[b, :, feats:], gain_ref[...])


def sums_kernel(count, *refs):
    parts, orders, refs = refs[:count], refs[count : 2 * count], refs[2 * count :]
    hbm, (left_ref, right_ref, gain_ref) = refs[:4], refs[4:7]
    out_ref, sums_ref, dn, side_l, side_r = refs[7:12]
    here, sems = refs[12:16], refs[16]
    stat_ref, mixed_ref, grad_ref, pad_ref = here
    loads = moves(list(zip(hbm, here)), sems)
    batches, rows, cols, feats = pad_ref.shape
    rows -= 2
    cells = rows * cols
    for b in range(batches):
        total = None
        for order, part in zip(orders, parts):
            size = part.shape[0] // batches
            term = dot(order[...], part[b * size : (b + 1) * size, :])
            total = term if total is None else total + term
        dn[b * cells : (b + 1) * cells, :] = total
    block = 64
    for copy in loads[:3]:
        copy.wait()

    def norm(n, gain_sum):
        at = pl.ds(pl.multiple_of(n * block, block), block)
        d_normed = dn[at, :]
        rstd = stat_ref[at, 1:2]
        nhat = (mixed_ref[at, :].astype(F32) - stat_ref[at, 0:1]) * rstd
        out_ref[at, :] = norm_back(d_normed, nhat, rstd, grad_ref[at, :], gain_ref[...])
        return gain_sum + jnp.sum((d_normed * nhat).reshape(block // 8, 8, feats), axis=0)

    gain_sum = lax.fori_loop(
        0, batches * cells // block, norm, jnp.zeros((8, feats), F32), unroll=2
    )
    sums_ref[9:10, :] = jnp.sum(gain_sum, axis=0, keepdims=True)
    sums_ref[10:, :] = jnp.zeros((sums_ref.shape[0] - 10, feats), F32)
    loads[3].wait()

    four = 4
    width = 256
    spot = lax.broadcasted_iota(jnp.int32, (cols, width), 0)
    fold = lambda v: jnp.sum(v.reshape(cols // 8, 8, width), axis=0)
    for c in range(feats // width):
        lanes = slice(c * width, (c + 1) * width)
        sums = [jnp.zeros((8, width), F32) for _ in range(9)]
        for b in range(batches):

            def step(n, sums, b=b, lanes=lanes):
                start = n * four
                x = [pad_ref[b, start + r, :, lanes].astype(F32) for r in range(four + 2)]
                sums = list(sums)
                for r in range(four):
                    h = start + r
                    at = pl.ds(pl.multiple_of((b * rows + h) * cols, cols), cols)
                    d_mixed = out_ref[at, lanes].astype(F32)
                    side_l[b, pl.ds(h, 1), lanes] = d_mixed[:1]
                    side_r[b, pl.ds(h, 1), lanes] = d_mixed[cols - 1 :]
                    moved = (
                        jnp.where(spot == cols - 1, 0.0, pltpu.roll(d_mixed, cols - 1, 0)),
                        d_mixed,
                        jnp.where(spot == 0, 0.0, pltpu.roll(d_mixed, 1, 0)),
                    )
                    for i in range(3):
                        for j in range(3):
                            sums[3 * i + j] = sums[3 * i + j] + fold(moved[j] * x[r + i])
                return tuple(sums)

            sums = lax.fori_loop(0, rows // four, step, tuple(sums))
        for n in range(9):
            sums_ref[n : n + 1, lanes] = jnp.sum(sums[n], axis=0, keepdims=True)
    for i in range(3):
        for b in range(batches):
            left, right = left_ref[b].astype(F32), right_ref[b].astype(F32)
            sums_ref[3 * i : 3 * i + 1, :] += jnp.sum(
                side_l[b] * left[i : i + rows], axis=0, keepdims=True
            )
            sums_ref[3 * i + 2 : 3 * i + 3, :] += jnp.sum(
                side_r[b] * right[i : i + rows], axis=0, keepdims=True
            )


def spread_kernel(d_ref, top_ref, bot_ref, left_ref, right_ref, dw_ref, out_ref, pad, side_l, side_r):
    batches, rows, cols, feats = pad.shape
    rows -= 2
    for b in range(batches):
        for h in range(rows):
            pad[b, h + 1] = d_ref[(b * rows + h) * cols : (b * rows + h + 1) * cols, :]
    pad[:, 0] = top_ref[...]
    pad[:, rows + 1] = bot_ref[...]
    convolve(pad, left_ref, right_ref, taps_of(dw_ref, True), side_l, side_r, out_ref)


def call(body, outs, scratch, args, micros, name, hbm_ins=(), hbm_outs=(), scalars=()):
    moved = sum(int(np.prod(o.shape)) * o.dtype.itemsize for o in (*outs, *args))
    vmem = pl.BlockSpec(memory_space=pltpu.VMEM)
    hbm = pl.BlockSpec(memory_space=pl.ANY)
    smem = pl.BlockSpec(memory_space=pltpu.SMEM)
    return pl.pallas_call(
        body,
        out_shape=outs,
        in_specs=[
            smem if n in scalars else hbm if n in hbm_ins else vmem for n in range(len(args))
        ],
        out_specs=[hbm if n in hbm_outs else vmem for n in range(len(outs))],
        scratch_shapes=scratch,
        compiler_params=pltpu.CompilerParams(vmem_limit_bytes=LIMIT),
        cost_estimate=pl.CostEstimate(
            flops=micros * 10**9, bytes_accessed=moved, transcendentals=0
        ),
        name=name,
    )(*args)


def shape(dims, dtype):
    return jax.ShapeDtypeStruct(tuple(dims), dtype)


def shifted(cells, axis, step):
    count = lax.axis_size(axis)
    return lax.ppermute(cells, axis, [(n, n + step) for n in range(count) if 0 <= n + step < count])


def halos(top, bottom, left, right):
    above = shifted(bottom, "row", 1)
    below = shifted(top, "row", -1)
    last = above.shape[1] - 1
    column = lambda own, at: jnp.concatenate(
        [above[:, at : at + 1], own, below[:, at : at + 1]], axis=1
    )
    from_left = shifted(column(right, last), "col", 1)
    from_right = shifted(column(left, 0), "col", -1)
    return above, below, from_left, from_right


def swap(x, axis, step):
    return lax.ppermute(x, axis, [(n, n ^ step) for n in range(lax.axis_size(axis))])


def total(values):
    while len(values) > 1:
        values = [a + b for a, b in zip(values[::2], values[1::2])]
    return values[0]


def scatter(blocks, sums, axis, unit, count):
    size = blocks.shape[0] // count
    sums = sums.reshape(size, -1)
    load = lambda n: jnp.concatenate([blocks[n * size : (n + 1) * size], sums], axis=1).astype(BF16)
    own = jnp.concatenate([blocks[:size], sums], axis=1)
    return [own, *(swap(load(n), axis, unit * n).astype(F32) for n in range(1, count))]


def shards(plan, latent, w_qkv, w_out, ln_gain, dw_kernel, grad_out):
    batches, rows, cols, feats = latent.shape
    row_count, col_count = lax.axis_size("row"), lax.axis_size("col")
    cells = batches * rows * cols
    parts = len(plan.rows)
    gain = ln_gain.reshape(1, feats)
    send = jnp.asarray(plan.send_all, BF16)
    owner = lax.axis_index("row") * col_count + lax.axis_index("col")
    index = lax.dynamic_index_in_dim(jnp.asarray(plan.index), owner % plan.share, keepdims=False)
    back = [jnp.asarray(np.ascontiguousarray(m.T), BF16) for m in plan.send]
    sort = [index, *(jnp.asarray(m, BF16) for m in plan.sort[1:])]
    grouped = [shape((n * CELLS, feats), BF16) for n in plan.windows]
    take = [jnp.asarray(m, BF16) for m in plan.take]
    chunks = [shape((n, feats), BF16) for n in plan.rows]
    trade = lambda x: lax.all_to_all(x, AXES, split_axis=0, concat_axis=0, tiled=True)
    grad_flat = grad_out.reshape(cells, feats)

    flat = shape((cells, feats), BF16)
    (grad_sent,) = call(
        functools.partial(send_kernel, batches), [flat], [], [grad_flat, send], 3, "grad_send"
    )
    grad_win = trade(grad_sent)

    above, below, left, right = halos(latent[:, 0], latent[:, -1], latent[:, :, 0], latent[:, :, -1])
    padded = (batches, rows + 2, cols, feats)
    side = pltpu.VMEM((batches, rows, feats), F32)
    stat_shape = (cells, 2)
    normed, mixed, stat, pad = call(
        mix_kernel,
        [flat, flat, shape(stat_shape, F32), shape(padded, BF16)],
        [
            pltpu.VMEM((cells, feats), BF16),
            pltpu.VMEM(stat_shape, F32),
            pltpu.VMEM(padded, BF16),
            pltpu.VMEM((cells, feats), BF16),
            side,
            side,
            pltpu.SemaphoreType.DMA((3,)),
        ],
        [latent, above, below, left, right, dw_kernel, gain, send],
        6,
        "mix",
        hbm_outs=(1, 2, 3),
    )
    normed_win = trade(normed)
    pair = lambda pick: jnp.concatenate([pick(mixed.reshape(latent.shape)), pick(grad_out)], axis=-1)
    pairs = halos(
        pair(lambda x: x[:, 0]),
        pair(lambda x: x[:, -1]),
        pair(lambda x: x[:, :, 0]),
        pair(lambda x: x[:, :, -1]),
    )
    normed_win, *pairs = lax.optimization_barrier((normed_win, *pairs))

    chips = col_count // 2
    ahead = call(
        functools.partial(grads_kernel, parts),
        [grouped[n // 2] for n in range(2 * parts)],
        [],
        [grad_win, w_out, *take],
        4,
        "grads",
    )
    mine = place_of(lax.axis_index("row"), lax.axis_index("col"), row_count, chips).astype(jnp.int32).reshape(1)
    half = shape((feats // 2, 4 * feats), BF16)
    d_parts, kept = [], []
    for n in range(parts):
        count = plan.windows[n] * CELLS
        last = n == parts - 1
        mat = lambda width: pltpu.VMEM((count, width), BF16)
        args = [normed_win, ahead[2 * n + 1], take[n], sort[n], w_qkv]
        if last:
            outs = [chunks[n], half, half]
            args += [mine, ahead[2 * n], *kept]
            scratch = [
                mat(feats),
                pltpu.VMEM((feats, 4 * feats), BF16),
                pltpu.VMEM(half.shape, BF16),
                pltpu.VMEM(half.shape, BF16),
                pltpu.SemaphoreType.DMA((2,)),
                pltpu.SemaphoreType.DMA((1 + len(kept),)),
                *(pltpu.VMEM(x.shape, BF16) for x in kept),
            ]
        else:
            outs = [chunks[n], grouped[n], grouped[n], shape((count, 3 * feats), BF16)]
            scratch = [pltpu.SemaphoreType.DMA((3,))]
        d_chunk, *saved = call(
            functools.partial(window_kernel, (row_count, chips) if last else None, n),
            outs,
            [
                *scratch,
                pltpu.VMEM((cells, feats), BF16),
                pltpu.VMEM((feats, 3 * feats), BF16),
                mat(feats),
                mat(3 * feats),
                mat(feats),
                mat(feats),
                mat(3 * feats),
                pltpu.VMEM((4 * CELLS, 256), BF16),
                pltpu.VMEM((2 * CELLS, 256), BF16),
                pltpu.SemaphoreType.DMA((3,)),
            ],
            args,
            2 + 20 * count // cells,
            "windows",
            hbm_ins=(0, 1, 4, *range(6, len(args))),
            hbm_outs=tuple(range(1, len(outs))),
            scalars=(5,),
        )
        kept += [*saved, ahead[2 * n]]
        d_parts.append(trade(d_chunk))
    keep, give = saved

    d_halos = call(
        border_kernel,
        [shape((*x.shape[:2], feats), BF16) for x in pairs],
        [],
        [d_parts[0], gain, *(jnp.asarray(m, BF16) for m in plan.pieces), *pairs],
        3,
        "border",
    )
    weights = (keep.astype(F32) + swap(give, "col", 1).astype(F32)).astype(BF16)
    d_mixed, sums = call(
        functools.partial(sums_kernel, parts),
        [flat, shape((16, feats), F32)],
        [
            pltpu.VMEM((cells, feats), F32),
            side,
            side,
            pltpu.VMEM(stat_shape, F32),
            pltpu.VMEM((cells, feats), BF16),
            pltpu.VMEM((cells, feats), BF16),
            pltpu.VMEM(padded, BF16),
            pltpu.SemaphoreType.DMA((4,)),
        ],
        [*d_parts, *back, stat, mixed, grad_flat, pad, left, right, gain],
        7,
        "sums",
        hbm_ins=tuple(range(2 * parts, 2 * parts + 4)),
    )
    (grad_latent,) = call(
        spread_kernel,
        [flat],
        [pltpu.VMEM(padded, BF16), side, side],
        [d_mixed, *d_halos, dw_kernel],
        5,
        "spread",
    )
    wide = 4 * feats
    size = weights.shape[0] // row_count
    gives = [
        swap(weights[n * size : (n + 1) * size], "row", n).astype(F32) for n in range(1, row_count)
    ]
    weights = total([weights[:size].astype(F32), *gives])
    sums = sums + swap(sums, "col", 1)
    sums = total([sums, *(swap(sums, "row", n) for n in range(1, row_count))])
    level = scatter(weights, sums, "col", 2, chips)
    part = lambda first, last: total([x[:, first:last] for x in level])
    sums = part(wide, None).reshape(16, feats)
    return (
        grad_latent.reshape(latent.shape),
        part(0, 3 * feats),
        part(3 * feats, wide),
        sums[9],
        sums[:9].reshape(3, 3, feats),
    )


def solution(mesh):
    row_count, col_count = mesh.shape["row"], mesh.shape["col"]

    def run(latent, w_qkv, w_out, ln_gain, dw_kernel, grad_out):
        batches, rows, cols, _ = latent.shape
        plan = Plan(batches, rows // row_count, cols // col_count, row_count, col_count)
        in_specs = (P(None, "row", "col", None), P(), P(), P(), P(), P(None, "row", "col", None))
        out_specs = (
            P(None, "row", "col", None),
            P(AXES, None),
            P(AXES, None),
            P(),
            P(),
        )
        return jax.shard_map(
            functools.partial(shards, plan),
            mesh=mesh,
            in_specs=in_specs,
            out_specs=out_specs,
            check_vma=False,
        )(latent, w_qkv, w_out, ln_gain, dw_kernel, grad_out)

    return run
```

```python
import functools

import jax
import jax.numpy as jnp
import numpy as np
from jax import lax
from jax.experimental import pallas as pl
from jax.experimental.pallas import tpu as pltpu
from jax.sharding import PartitionSpec as P

HEADS = 16
HEAD = 32
GRID = 8
CELLS = GRID * GRID
AXES = ("row", "col")
F32 = jnp.float32
BF16 = jnp.bfloat16
LIMIT = 56 * 1024 * 1024
UNROLL = 4
GROUP = 16


def dot(left, right, dims=((1,), (0,))):
    return lax.dot_general(left, right, (dims, ((), ())), preferred_element_type=F32)


def moves(pairs, sems):
    copies = [pltpu.make_async_copy(a, b, sems.at[n]) for n, (a, b) in enumerate(pairs)]
    for copy in copies:
        copy.start()
    return copies


class Plan:
    def __init__(self, batches, tile_rows, tile_cols, row_count, col_count):
        devices = row_count * col_count
        high = tile_rows * row_count // GRID
        full = tile_cols * col_count // GRID
        wide = min(full, tile_cols)
        groups = full // wide
        reps_r = tile_rows // high
        reps_s = tile_cols // wide
        reps = reps_r * reps_s
        share = devices // batches
        spots = [(a, e) for a in range(high) for e in range(wide)]
        cells = tile_rows * tile_cols
        ring = [
            [(-1, w) for w in range(tile_cols)],
            [(tile_rows, w) for w in range(tile_cols)],
            [(h, -1) for h in range(-1, tile_rows + 1)],
            [(h, tile_cols) for h in range(-1, tile_rows + 1)],
        ]

        def home(h, w):
            down, right = h // tile_rows, w // tile_cols
            h, w = h % tile_rows, w % tile_cols
            return down, right, (h % high, w % wide), (h // high) * reps_s + w // wide

        wanted = {c: [] for c in spots}
        for piece, members in enumerate(ring):
            for n, cell in enumerate(members):
                wanted[home(*cell)[2]].append((piece, n))
        edge = sorted((c for c in spots if wanted[c]), key=lambda c: -len(wanted[c]))
        slots = len(spots) // share
        edge_slots = -(-len(edge) // share)
        assert edge_slots < slots
        bounds = [0, edge_slots, slots]
        place, filled, load = {}, [0] * share, [0] * share
        for c in edge:
            owner = min((n for n in range(share) if filled[n] < edge_slots), key=lambda n: load[n])
            place[c] = (owner, filled[owner])
            filled[owner] += 1
            load[owner] += len(wanted[c])
        for c in spots:
            if c not in place:
                owner = min(range(share), key=lambda n: filled[n])
                place[c] = (owner, filled[owner])
                filled[owner] += 1

        def build(first, last):
            size = (last - first) * reps
            send = np.zeros((share * size, cells), np.float32)
            for h in range(tile_rows):
                for w in range(tile_cols):
                    owner, slot = place[(h % high, w % wide)]
                    if first <= slot < last:
                        rep = (h // high) * reps_s + w // wide
                        send[owner * size + (slot - first) * reps + rep, h * tile_cols + w] = 1
            count = (last - first) * groups
            seen = np.zeros((count,), np.int64)
            where = {}
            sort = np.zeros((devices * size, devices * size), np.float32)
            for source in range(devices):
                j = source % col_count
                for slot in range(last - first):
                    for r in range(reps_r):
                        for s in range(reps_s):
                            window = slot * groups + ((j * tile_cols + s * wide) % full) // wide
                            position = int(seen[window])
                            seen[window] += 1
                            chunk, lane = divmod(position, GROUP)
                            row = chunk * GROUP * count + window * GROUP + lane
                            where[source, slot, r * reps_s + s] = window * CELLS + position
                            sort[row, source * size + slot * reps + r * reps_s + s] = 1
            step = GROUP * count
            block = sort[:step, :step]
            assert (sort == np.kron(np.eye(CELLS // GROUP), block)).all()
            return send, block, where

        self.send_all, sort_all, _ = build(0, slots)
        self.send, self.sort, self.take = [], [], []
        for first, last in zip(bounds[:-1], bounds[1:]):
            send, block, where = build(first, last)
            if first == 0:
                around = where
            self.send.append(send)
            self.sort.append(block)
            self.take.append(sort_all[first * groups * GROUP : last * groups * GROUP])
        own = edge_slots * reps
        size = own + -(-max(load) // 8) * 8
        size = -(-size // 8) * 8
        back = np.zeros((share * size, cells), np.float32)
        for n in range(share):
            back[n * size : n * size + own] = self.send[0][n * own : (n + 1) * own]
        self.send[0] = back
        self.pieces = [np.zeros((len(members), share * size), np.float32) for members in ring]
        self.index = np.full((share, 1, devices * size), -1, np.int32)
        used = [own] * share
        for source, slot, rep in around:
            self.index[:, 0, source * size + slot * reps + rep] = around[source, slot, rep]
        for c in edge:
            owner, slot = place[c]
            for piece, n in wanted[c]:
                down, right, _, rep = home(*ring[piece][n])
                self.pieces[piece][n, owner * size + used[owner]] = 1
                for i in range(row_count):
                    for j in range(col_count):
                        if 0 <= i + down < row_count and 0 <= j + right < col_count:
                            source = (i + down) * col_count + j + right
                            target = (i * col_count + j) * size + used[owner]
                            self.index[owner, 0, target] = around[source, slot, rep]
                used[owner] += 1
        self.share = share
        self.windows = [m.shape[0] // GROUP for m in self.sort]
        self.rows = [batches * m.shape[0] for m in self.send]


def send_kernel(batches, x_ref, order, out):
    cells = x_ref.shape[0] // batches
    for b in range(batches):
        at = slice(b * cells, (b + 1) * cells)
        out[at, :] = dot(order[...], x_ref[at, :]).astype(BF16)


def convolve(pad, left_ref, right_ref, kern, side_l, side_r, out_ref):
    batches, rows, cols, feats = pad.shape
    rows -= 2
    four = 4
    width = 256
    for b in range(batches):
        left, right = left_ref[b].astype(F32), right_ref[b].astype(F32)
        side_l[b] = sum(kern[i][0] * left[i : i + rows] for i in range(3))
        side_r[b] = sum(kern[i][2] * right[i : i + rows] for i in range(3))
    spot = lax.broadcasted_iota(jnp.int32, (cols, width), 0)
    for c in range(feats // width):
        at = slice(c * width, (c + 1) * width)
        taps = [[kern[i][j][:, at] for j in range(3)] for i in range(3)]
        for b in range(batches):

            def step(n, carry, b=b, at=at, taps=taps):
                first = n * four
                x = [pad[b, first + r, :, at].astype(F32) for r in range(four + 2)]
                for r in range(four):
                    low, mid, high = (
                        taps[0][j] * x[r] + taps[1][j] * x[r + 1] + taps[2][j] * x[r + 2]
                        for j in range(3)
                    )
                    h = first + r
                    low = jnp.where(spot == 0, side_l[b, pl.ds(h, 1), at], pltpu.roll(low, 1, 0))
                    high = jnp.where(
                        spot == cols - 1, side_r[b, pl.ds(h, 1), at], pltpu.roll(high, cols - 1, 0)
                    )
                    where = pl.ds(pl.multiple_of((b * rows + h) * cols, cols), cols)
                    out_ref[where, at] = (x[r + 1] + (low + mid + high)).astype(BF16)
                return carry

            lax.fori_loop(0, rows // four, step, 0)


def taps_of(dw_ref, flipped):
    side = lambda n: 2 - n if flipped else n
    return [
        [dw_ref[side(i), side(j) : side(j) + 1, :].astype(F32) for j in range(3)] for i in range(3)
    ]


def mix_kernel(lat_ref, top_ref, bot_ref, left_ref, right_ref, dw_ref, gain_ref, order, *refs):
    out, mixed_out, stat_out, pad_out = refs[:4]
    mixed_ref, stat_ref, pad_ref, normed_ref, side_l, side_r, sems = refs[4:]
    batches, rows, cols, feats = lat_ref.shape
    pad_ref[:, 1 : rows + 1] = lat_ref[...]
    pad_ref[:, 0] = top_ref[...]
    pad_ref[:, rows + 1] = bot_ref[...]
    copies = moves([(pad_ref, pad_out)], sems)
    convolve(pad_ref, left_ref, right_ref, taps_of(dw_ref, False), side_l, side_r, mixed_ref)
    copies += moves([(mixed_ref, mixed_out)], sems.at[1:2])
    block = 64

    def norm(n, carry):
        at = pl.ds(pl.multiple_of(n * block, block), block)
        mixed = mixed_ref[at, :].astype(F32)
        mean = jnp.mean(mixed, axis=-1, keepdims=True)
        centred = mixed - mean
        rstd = lax.rsqrt(jnp.mean(centred * centred, axis=-1, keepdims=True) + 1e-05)
        stat_ref[at, 0:1] = mean
        stat_ref[at, 1:2] = rstd
        normed_ref[at, :] = (centred * rstd * gain_ref[...]).astype(BF16)
        return carry

    lax.fori_loop(0, batches * rows * cols // block, norm, 0, unroll=2)
    copies += moves([(stat_ref, stat_out)], sems.at[2:3])
    send_kernel(batches, normed_ref, order, out)
    for copy in copies:
        copy.wait()


def gather_rows(source, take_ref, target):
    count = target.shape[0] // CELLS
    whole = source.shape[0] * GROUP // CELLS
    for p in range(CELLS // GROUP):
        ordered = dot(take_ref[...], source[p * whole : (p + 1) * whole, :]).astype(BF16)
        for w in range(count):
            target[w * CELLS + p * GROUP : w * CELLS + (p + 1) * GROUP, :] = ordered[
                w * GROUP : (w + 1) * GROUP
            ]


def grads_kernel(parts, g_ref, wout_ref, *refs):
    for n in range(parts):
        gw, datt = refs[parts + 2 * n : parts + 2 * n + 2]
        gather_rows(g_ref, refs[n], gw)
        rows = gw.shape[0]
        for first in range(0, rows, 256):
            at = slice(first, min(first + 256, rows))
            datt[at, :] = dot(gw[at, :], wout_ref[...], ((1,), (1,))).astype(BF16)


def window_kernel(counts, before, n_hbm, datt_hbm, take_ref, back_ref, wqkv_hbm, *refs):
    n_ref, wqkv_ref, nw, packed, datt, att, dpacked, head_mask, half_mask, in_sems = refs[-10:]
    if counts is None:
        dn_ref, *results, out_sems = refs[:5]
    else:
        mine_ref, gw_hbm, *old = refs[: 4 * before + 2]
        dn_ref, keep_hbm, give_hbm, gw, acc, keep_ref, give_ref, out_sems, old_sems, *old_refs = refs[
            4 * before + 2 : -10
        ]
        late = moves([(gw_hbm, gw), *zip(old, old_refs)], old_sems)
    loads = moves([(n_hbm, n_ref), (wqkv_hbm, wqkv_ref), (datt_hbm, datt)], in_sems)
    rows, feats = nw.shape
    count = rows // CELLS
    part = GROUP * count
    tiles = feats // 256
    scale = HEAD ** (-0.5)
    block = 256 if rows % 256 == 0 else CELLS

    head_mask[...] = (
        (lax.broadcasted_iota(jnp.int32, (4 * CELLS, 256), 1) // HEAD) % 4
        == lax.broadcasted_iota(jnp.int32, (4 * CELLS, 256), 0) // CELLS
    ).astype(F32).astype(BF16)
    half_mask[...] = (
        lax.broadcasted_iota(jnp.int32, (2 * CELLS, 256), 1) // 128
        == lax.broadcasted_iota(jnp.int32, (2 * CELLS, 256), 0) // CELLS
    ).astype(F32).astype(BF16)

    loads[0].wait()
    gather_rows(n_ref, take_ref, nw)
    loads[1].wait()

    def project(n, carry):
        at = pl.ds(pl.multiple_of(n * block, block), block)
        packed[at, :] = dot(nw[at, :], wqkv_ref[...]).astype(BF16)
        return carry

    lax.fori_loop(0, rows // block, project, 0)
    loads[2].wait()

    lane = lax.broadcasted_iota(jnp.int32, (CELLS, 256), 1)
    lane_half = lane < 128
    lane_head = (lane // HEAD) % 4

    def fold_heads(full):
        out = full[3 * CELLS :]
        for h in (2, 1, 0):
            out = jnp.where(lane_head == h, full[h * CELLS : (h + 1) * CELLS], out)
        return out

    def one(n, carry):
        at = pl.ds(pl.multiple_of(n * CELLS, CELLS), CELLS)
        for t in range(tiles):
            cols = [slice(p * feats + t * 256, p * feats + (t + 1) * 256) for p in range(3)]
            query = packed[at, cols[0]]
            key = packed[at, cols[1]]
            value = packed[at, cols[2]]
            grad = datt[at, t * 256 : (t + 1) * 256]
            key_big = jnp.concatenate([key] * 4, axis=0) * head_mask[...]
            value_big = jnp.concatenate([value] * 4, axis=0) * head_mask[...]
            query_two = jnp.concatenate([query] * 2, axis=0) * half_mask[...]
            grad_two = jnp.concatenate([grad] * 2, axis=0) * half_mask[...]
            scores = (dot(key_big, query_two, ((1,), (1,))) * scale).reshape(4, CELLS, 2 * CELLS)
            d_probs = dot(value_big, grad_two, ((1,), (1,))).reshape(4, CELLS, 2 * CELLS)
            raised = jnp.exp(scores - jnp.max(scores, axis=1, keepdims=True))
            probs = raised * (1.0 / jnp.sum(raised, axis=1, keepdims=True))
            probs_b = probs.astype(BF16).reshape(4 * CELLS, 2 * CELLS)
            inner = jnp.sum(probs * d_probs, axis=1, keepdims=True)
            d_scores = (
                (probs * (d_probs - inner) * scale).astype(BF16).reshape(4 * CELLS, 2 * CELLS)
            )
            out = dot(probs_b, value_big, ((0,), (0,)))
            att[at, t * 256 : (t + 1) * 256] = jnp.where(
                lane_half, out[:CELLS], out[CELLS:]
            ).astype(BF16)
            d_query = dot(d_scores, key_big, ((0,), (0,)))
            dpacked[at, cols[0]] = jnp.where(
                lane_half, d_query[:CELLS], d_query[CELLS:]
            ).astype(BF16)
            dpacked[at, cols[1]] = fold_heads(dot(d_scores, query_two)).astype(BF16)
            dpacked[at, cols[2]] = fold_heads(dot(probs_b, grad_two)).astype(BF16)
        return carry

    lax.fori_loop(0, count, one, 0, unroll=UNROLL)
    if counts is None:
        stores = moves(list(zip((nw, att, dpacked), results)), out_sems)
    else:
        for copy in late:
            copy.wait()
        parts = [old_refs[4 * n : 4 * n + 4] for n in range(before)] + [(nw, att, dpacked, gw)]
        weight_sums(parts, counts, mine_ref[0], acc, keep_ref, give_ref)
        stores = moves([(give_ref, give_hbm), (keep_ref, keep_hbm)], out_sems)

    def back(n, carry):
        at = pl.ds(pl.multiple_of(n * block, block), block)
        datt[at, :] = dot(dpacked[at, :], wqkv_ref[...], ((1,), (1,))).astype(BF16)
        return carry

    lax.fori_loop(0, rows // block, back, 0)
    if back_ref.shape[0] == 1:
        order = (
            lax.broadcasted_iota(jnp.int32, (rows, dn_ref.shape[0]), 0) == back_ref[...]
        ).astype(F32).astype(BF16)
        dn_ref[...] = dot(order, datt[...], ((0,), (0,))).astype(BF16)
    else:
        for p in range(CELLS // GROUP):
            ordered = jnp.concatenate(
                [
                    datt[w * CELLS + p * GROUP : w * CELLS + (p + 1) * GROUP, :]
                    for w in range(count)
                ],
                axis=0,
            )
            dn_ref[p * part : (p + 1) * part, :] = dot(
                back_ref[...], ordered, ((0,), (0,))
            ).astype(BF16)
    for copy in stores:
        copy.wait()


def place_of(i, j, row_count, chips):
    return (j % 2) * row_count * chips + i * chips + j // 2


def weight_sums(parts, counts, mine, acc, keep_ref, give_ref):
    feats = acc.shape[0]
    row_count, chips = counts
    devices = 2 * row_count * chips
    size = feats // devices
    half = devices // 2
    for left, right, start in ((0, 2, 0), (1, 3, 3 * feats)):
        turned = [part[left][...].T for part in parts]
        for t in range(parts[0][right].shape[1] // 256):
            at = slice(t * 256, (t + 1) * 256)
            acc[:, start + t * 256 : start + (t + 1) * 256] = sum(
                dot(x, part[right][:, at]) for x, part in zip(turned, parts)
            ).astype(BF16)
    if size % 16:
        source = lax.broadcasted_iota(jnp.int32, (feats, feats), 1)
        device = source // size
        place = place_of(device // (2 * chips), device % (2 * chips), row_count, chips)
        target = jnp.bitwise_xor(mine, place) * size + source % size
        order = (lax.broadcasted_iota(jnp.int32, (feats, feats), 0) == target).astype(F32).astype(BF16)
        keep_ref[...] = dot(order[: feats // 2], acc[...]).astype(BF16)
        give_ref[...] = dot(order[feats // 2 :], acc[...]).astype(BF16)
        return
    for n in range(devices):
        place = place_of(n // (2 * chips), n % (2 * chips), row_count, chips)
        block = jnp.bitwise_xor(mine, place)
        rows = acc[n * size : (n + 1) * size, :]
        at = pl.ds(pl.multiple_of((block % half) * size, size), size)

        @pl.when(block < half)
        def _(rows=rows, at=at):
            keep_ref[at, :] = rows

        @pl.when(block >= half)
        def _(rows=rows, at=at):
            give_ref[at, :] = rows


def norm_back(d_normed, nhat, rstd, grad, gain):
    scaled = d_normed * gain
    return (
        grad.astype(F32)
        + rstd
        * (
            scaled
            - jnp.mean(scaled, axis=-1, keepdims=True)
            - nhat * jnp.mean(scaled * nhat, axis=-1, keepdims=True)
        )
    ).astype(BF16)


def border_kernel(dn_ref, gain_ref, *refs):
    batches = refs[4].shape[0]
    feats = dn_ref.shape[1]
    size = dn_ref.shape[0] // batches
    for pick, pair, out in zip(refs[:4], refs[4:8], refs[8:]):
        for b in range(batches):
            d_normed = dot(pick[...], dn_ref[b * size : (b + 1) * size, :])
            mixed = pair[b, :, :feats].astype(F32)
            centred = mixed - jnp.mean(mixed, axis=-1, keepdims=True)
            rstd = lax.rsqrt(jnp.mean(centred * centred, axis=-1, keepdims=True) + 1e-05)
            out[b] = norm_back(d_normed, centred * rstd, rstd, pair[b, :, feats:], gain_ref[...])


def sums_kernel(count, *refs):
    orders, refs = refs[:count], refs[count:]
    hbm, refs = refs[:count], refs[count:]
    hbm, (left_ref, right_ref, gain_ref) = hbm + refs[:4], refs[4:7]
    out_ref, sums_ref, dn, side_l, side_r = refs[7:12]
    here, sems = refs[12:-1], refs[-1]
    parts = here[:count]
    stat_ref, mixed_ref, grad_ref, pad_ref = here[count:]
    loads = moves(list(zip(hbm, here)), sems)
    batches, rows, cols, feats = pad_ref.shape
    rows -= 2
    cells = rows * cols
    for copy in loads[:count]:
        copy.wait()
    for b in range(batches):
        total = None
        for order, part in zip(orders, parts):
            size = part.shape[0] // batches
            term = dot(order[...], part[b * size : (b + 1) * size, :])
            total = term if total is None else total + term
        dn[b * cells : (b + 1) * cells, :] = total
    block = 64
    for copy in loads[count : count + 3]:
        copy.wait()

    def norm(n, gain_sum):
        at = pl.ds(pl.multiple_of(n * block, block), block)
        d_normed = dn[at, :]
        rstd = stat_ref[at, 1:2]
        nhat = (mixed_ref[at, :].astype(F32) - stat_ref[at, 0:1]) * rstd
        out_ref[at, :] = norm_back(d_normed, nhat, rstd, grad_ref[at, :], gain_ref[...])
        return gain_sum + jnp.sum((d_normed * nhat).reshape(block // 8, 8, feats), axis=0)

    gain_sum = lax.fori_loop(
        0, batches * cells // block, norm, jnp.zeros((8, feats), F32), unroll=2
    )
    sums_ref[9:10, :] = jnp.sum(gain_sum, axis=0, keepdims=True)
    sums_ref[10:, :] = jnp.zeros((sums_ref.shape[0] - 10, feats), F32)
    loads[count + 3].wait()

    four = 4
    width = 256
    spot = lax.broadcasted_iota(jnp.int32, (cols, width), 0)
    fold = lambda v: jnp.sum(v.reshape(cols // 8, 8, width), axis=0)
    for c in range(feats // width):
        lanes = slice(c * width, (c + 1) * width)
        sums = [jnp.zeros((8, width), F32) for _ in range(9)]
        for b in range(batches):

            def step(n, sums, b=b, lanes=lanes):
                start = n * four
                x = [pad_ref[b, start + r, :, lanes].astype(F32) for r in range(four + 2)]
                sums = list(sums)
                for r in range(four):
                    h = start + r
                    at = pl.ds(pl.multiple_of((b * rows + h) * cols, cols), cols)
                    d_mixed = out_ref[at, lanes].astype(F32)
                    side_l[b, pl.ds(h, 1), lanes] = d_mixed[:1]
                    side_r[b, pl.ds(h, 1), lanes] = d_mixed[cols - 1 :]
                    moved = (
                        jnp.where(spot == cols - 1, 0.0, pltpu.roll(d_mixed, cols - 1, 0)),
                        d_mixed,
                        jnp.where(spot == 0, 0.0, pltpu.roll(d_mixed, 1, 0)),
                    )
                    for i in range(3):
                        for j in range(3):
                            sums[3 * i + j] = sums[3 * i + j] + fold(moved[j] * x[r + i])
                return tuple(sums)

            sums = lax.fori_loop(0, rows // four, step, tuple(sums))
        for n in range(9):
            sums_ref[n : n + 1, lanes] = jnp.sum(sums[n], axis=0, keepdims=True)
    for i in range(3):
        for b in range(batches):
            left, right = left_ref[b].astype(F32), right_ref[b].astype(F32)
            sums_ref[3 * i : 3 * i + 1, :] += jnp.sum(
                side_l[b] * left[i : i + rows], axis=0, keepdims=True
            )
            sums_ref[3 * i + 2 : 3 * i + 3, :] += jnp.sum(
                side_r[b] * right[i : i + rows], axis=0, keepdims=True
            )


def spread_kernel(d_ref, top_ref, bot_ref, left_ref, right_ref, dw_ref, out_ref, pad, side_l, side_r):
    batches, rows, cols, feats = pad.shape
    rows -= 2
    for b in range(batches):
        for h in range(rows):
            pad[b, h + 1] = d_ref[(b * rows + h) * cols : (b * rows + h + 1) * cols, :]
    pad[:, 0] = top_ref[...]
    pad[:, rows + 1] = bot_ref[...]
    convolve(pad, left_ref, right_ref, taps_of(dw_ref, True), side_l, side_r, out_ref)


def finish_kernel(*refs):
    *parts, qkv_ref, wout_ref, gain_ref, kernel_ref = refs
    feats = wout_ref.shape[1]
    level = total([part[...].astype(F32) for part in parts])
    qkv_ref[...] = level[:, : 3 * feats]
    wout_ref[...] = level[:, 3 * feats : 4 * feats]
    sums = level[:, 4 * feats :]
    gain_ref[...] = sums[9:10]
    for i in range(3):
        kernel_ref[i] = sums[3 * i : 3 * i + 3]


def call(body, outs, scratch, args, micros, name, hbm_ins=(), hbm_outs=(), scalars=(), limit=56 << 20):
    moved = sum(int(np.prod(o.shape)) * o.dtype.itemsize for o in (*outs, *args))
    vmem = pl.BlockSpec(memory_space=pltpu.VMEM)
    hbm = pl.BlockSpec(memory_space=pltpu.HBM)
    smem = pl.BlockSpec(memory_space=pltpu.SMEM)
    return pl.pallas_call(
        body,
        out_shape=outs,
        in_specs=[
            smem if n in scalars else hbm if n in hbm_ins else vmem for n in range(len(args))
        ],
        out_specs=[hbm if n in hbm_outs else vmem for n in range(len(outs))],
        scratch_shapes=scratch,
        compiler_params=pltpu.CompilerParams(vmem_limit_bytes=limit),
        cost_estimate=pl.CostEstimate(
            flops=micros * 10**9, bytes_accessed=moved, transcendentals=0
        ),
        name=name,
    )(*args)


def shape(dims, dtype):
    return jax.ShapeDtypeStruct(tuple(dims), dtype)


def shifted(cells, axis, step):
    count = lax.axis_size(axis)
    return lax.ppermute(cells, axis, [(n, n + step) for n in range(count) if 0 <= n + step < count])


def halos(top, bottom, left, right):
    above = shifted(bottom, "row", 1)
    below = shifted(top, "row", -1)
    last = above.shape[1] - 1
    column = lambda own, at: jnp.concatenate(
        [above[:, at : at + 1], own, below[:, at : at + 1]], axis=1
    )
    from_left = shifted(column(right, last), "col", 1)
    from_right = shifted(column(left, 0), "col", -1)
    return above, below, from_left, from_right


def swap(x, axis, step):
    return lax.ppermute(x, axis, [(n, n ^ step) for n in range(lax.axis_size(axis))])


def total(values):
    while len(values) > 1:
        values = [a + b for a, b in zip(values[::2], values[1::2])]
    return values[0]


def scatter(blocks, sums, axis, unit, count):
    size = blocks.shape[0] // count
    sums = sums.reshape(size, -1)
    load = lambda n: jnp.concatenate([blocks[n * size : (n + 1) * size], sums], axis=1).astype(BF16)
    own = jnp.concatenate([blocks[:size], sums], axis=1)
    return [own, *(swap(load(n), axis, unit * n) for n in range(1, count))]


def shards(plan, latent, w_qkv, w_out, ln_gain, dw_kernel, grad_out):
    batches, rows, cols, feats = latent.shape
    row_count, col_count = lax.axis_size("row"), lax.axis_size("col")
    cells = batches * rows * cols
    parts = len(plan.rows)
    gain = ln_gain.reshape(1, feats)
    send = jnp.asarray(plan.send_all, BF16)
    owner = lax.axis_index("row") * col_count + lax.axis_index("col")
    index = lax.dynamic_index_in_dim(jnp.asarray(plan.index), owner % plan.share, keepdims=False)
    back = [jnp.asarray(np.ascontiguousarray(m.T), BF16) for m in plan.send]
    sort = [index, *(jnp.asarray(m, BF16) for m in plan.sort[1:])]
    grouped = [shape((n * CELLS, feats), BF16) for n in plan.windows]
    take = [jnp.asarray(m, BF16) for m in plan.take]
    chunks = [shape((n, feats), BF16) for n in plan.rows]
    trade = lambda x: lax.all_to_all(x, AXES, split_axis=0, concat_axis=0, tiled=True)
    grad_flat = grad_out.reshape(cells, feats)

    flat = shape((cells, feats), BF16)
    (grad_sent,) = call(
        functools.partial(send_kernel, batches), [flat], [], [grad_flat, send], 3, "grad_send"
    )
    grad_win = trade(grad_sent)

    above, below, left, right = halos(latent[:, 0], latent[:, -1], latent[:, :, 0], latent[:, :, -1])
    padded = (batches, rows + 2, cols, feats)
    side = pltpu.VMEM((batches, rows, feats), F32)
    stat_shape = (cells, 2)
    normed, mixed, stat, pad = call(
        mix_kernel,
        [flat, flat, shape(stat_shape, F32), shape(padded, BF16)],
        [
            pltpu.VMEM((cells, feats), BF16),
            pltpu.VMEM(stat_shape, F32),
            pltpu.VMEM(padded, BF16),
            pltpu.VMEM((cells, feats), BF16),
            side,
            side,
            pltpu.SemaphoreType.DMA((3,)),
        ],
        [latent, above, below, left, right, dw_kernel, gain, send],
        6,
        "mix",
        limit=50 << 20,
        hbm_outs=(1, 2, 3),
    )
    normed_win = trade(normed)
    pair = lambda pick: jnp.concatenate([pick(mixed.reshape(latent.shape)), pick(grad_out)], axis=-1)
    pairs = halos(
        pair(lambda x: x[:, 0]),
        pair(lambda x: x[:, -1]),
        pair(lambda x: x[:, :, 0]),
        pair(lambda x: x[:, :, -1]),
    )
    normed_win, *pairs = lax.optimization_barrier((normed_win, *pairs))

    chips = col_count // 2
    ahead = call(
        functools.partial(grads_kernel, parts),
        [grouped[n // 2] for n in range(2 * parts)],
        [],
        [grad_win, w_out, *take],
        4,
        "grads",
        limit=50 << 20,
    )
    mine = place_of(lax.axis_index("row"), lax.axis_index("col"), row_count, chips).astype(jnp.int32).reshape(1)
    half = shape((feats // 2, 4 * feats), BF16)
    d_parts, kept = [], []
    for n in range(parts):
        count = plan.windows[n] * CELLS
        last = n == parts - 1
        mat = lambda width: pltpu.VMEM((count, width), BF16)
        args = [normed_win, ahead[2 * n + 1], take[n], sort[n], w_qkv]
        if last:
            outs = [chunks[n], half, half]
            args += [mine, ahead[2 * n], *kept]
            scratch = [
                mat(feats),
                pltpu.VMEM((feats, 4 * feats), BF16),
                pltpu.VMEM(half.shape, BF16),
                pltpu.VMEM(half.shape, BF16),
                pltpu.SemaphoreType.DMA((2,)),
                pltpu.SemaphoreType.DMA((1 + len(kept),)),
                *(pltpu.VMEM(x.shape, BF16) for x in kept),
            ]
        else:
            outs = [chunks[n], grouped[n], grouped[n], shape((count, 3 * feats), BF16)]
            scratch = [pltpu.SemaphoreType.DMA((3,))]
        d_chunk, *saved = call(
            functools.partial(window_kernel, (row_count, chips) if last else None, n),
            outs,
            [
                *scratch,
                pltpu.VMEM((cells, feats), BF16),
                pltpu.VMEM((feats, 3 * feats), BF16),
                mat(feats),
                mat(3 * feats),
                mat(feats),
                mat(feats),
                mat(3 * feats),
                pltpu.VMEM((4 * CELLS, 256), BF16),
                pltpu.VMEM((2 * CELLS, 256), BF16),
                pltpu.SemaphoreType.DMA((3,)),
            ],
            args,
            2 + 20 * count // cells,
            "windows",
        limit=56 << 20,
            hbm_ins=(0, 1, 4, *range(6, len(args))),
            hbm_outs=tuple(range(1, len(outs))),
            scalars=(5,),
        )
        kept += [*saved, ahead[2 * n]]
        d_parts.append(trade(d_chunk))
    keep, give = saved

    d_halos = call(
        border_kernel,
        [shape((*x.shape[:2], feats), BF16) for x in pairs],
        [],
        [d_parts[0], gain, *(jnp.asarray(m, BF16) for m in plan.pieces), *pairs],
        3,
        "border",
        limit=50 << 20,
    )
    weights = (keep.astype(F32) + swap(give, "col", 1).astype(F32)).astype(BF16)
    d_mixed, sums = call(
        functools.partial(sums_kernel, parts),
        [flat, shape((16, feats), F32)],
        [
            pltpu.VMEM((cells, feats), F32),
            side,
            side,
            *(pltpu.VMEM((n, feats), BF16) for n in plan.rows),
            pltpu.VMEM(stat_shape, F32),
            pltpu.VMEM((cells, feats), BF16),
            pltpu.VMEM((cells, feats), BF16),
            pltpu.VMEM(padded, BF16),
            pltpu.SemaphoreType.DMA((parts + 4,)),
        ],
        [*back, *d_parts, stat, mixed, grad_flat, pad, left, right, gain],
        7,
        "sums",
        limit=50 << 20,
        hbm_ins=tuple(range(parts, 2 * parts + 4)),
    )
    wide = 4 * feats
    size = weights.shape[0] // row_count
    gives = [
        swap(weights[n * size : (n + 1) * size], "row", n) for n in range(1, row_count)
    ]
    sums, weights, *gives = lax.optimization_barrier((sums, weights, *gives))
    weights = total([x.astype(F32) for x in (weights[:size], *gives)])
    sums = sums + swap(sums, "col", 1)
    sums = total([sums, *(swap(sums, "row", n) for n in range(1, row_count))])
    sums, d_mixed = lax.optimization_barrier((sums, d_mixed))
    (grad_latent,) = call(
        spread_kernel,
        [flat],
        [pltpu.VMEM(padded, BF16), side, side],
        [d_mixed, *d_halos, dw_kernel],
        5,
        "spread",
        limit=50 << 20,
    )
    level = scatter(weights, sums, "col", 2, chips)
    grad_latent = grad_latent.reshape(latent.shape)
    size = level[0].shape[0]
    if size == 16:
        qkv, wout, gain_sum, kernel_sum = call(
            finish_kernel,
            [
                shape((size, 3 * feats), F32),
                shape((size, feats), F32),
                shape((1, feats), F32),
                shape((3, 3, feats), F32),
            ],
            [],
            level,
            1,
            "finish",
            limit=50 << 20,
        )
        return grad_latent, qkv, wout, gain_sum.reshape(feats), kernel_sum
    level = total([x.astype(F32) for x in level])
    sums = level[:, wide:].reshape(16, feats)
    return (
        grad_latent,
        level[:, : 3 * feats],
        level[:, 3 * feats : wide],
        sums[9],
        sums[:9].reshape(3, 3, feats),
    )


def solution(mesh):
    row_count, col_count = mesh.shape["row"], mesh.shape["col"]

    def run(latent, w_qkv, w_out, ln_gain, dw_kernel, grad_out):
        batches, rows, cols, _ = latent.shape
        plan = Plan(batches, rows // row_count, cols // col_count, row_count, col_count)
        in_specs = (P(None, "row", "col", None), P(), P(), P(), P(), P(None, "row", "col", None))
        out_specs = (
            P(None, "row", "col", None),
            P(AXES, None),
            P(AXES, None),
            P(),
            P(),
        )
        return jax.shard_map(
            functools.partial(shards, plan),
            mesh=mesh,
            in_specs=in_specs,
            out_specs=out_specs,
            check_vma=False,
        )(latent, w_qkv, w_out, ln_gain, dw_kernel, grad_out)

    return run
```

```python
import functools

import jax
import jax.numpy as jnp
import numpy as np
from jax import lax
from jax.experimental import pallas as pl
from jax.experimental.pallas import tpu as pltpu
from jax.sharding import PartitionSpec as P

HEADS = 16
HEAD = 32
GRID = 8
CELLS = GRID * GRID
AXES = ("row", "col")
F32 = jnp.float32
BF16 = jnp.bfloat16
LIMIT = 56 * 1024 * 1024
UNROLL = 4
GROUP = 16


def dot(left, right, dims=((1,), (0,))):
    return lax.dot_general(left, right, (dims, ((), ())), preferred_element_type=F32)


def moves(pairs, sems):
    copies = [pltpu.make_async_copy(a, b, sems.at[n]) for n, (a, b) in enumerate(pairs)]
    for copy in copies:
        copy.start()
    return copies


class Plan:
    def __init__(self, batches, tile_rows, tile_cols, row_count, col_count):
        devices = row_count * col_count
        high = tile_rows * row_count // GRID
        full = tile_cols * col_count // GRID
        wide = min(full, tile_cols)
        groups = full // wide
        reps_r = tile_rows // high
        reps_s = tile_cols // wide
        reps = reps_r * reps_s
        share = devices // batches
        spots = [(a, e) for a in range(high) for e in range(wide)]
        cells = tile_rows * tile_cols
        ring = [
            [(-1, w) for w in range(tile_cols)],
            [(tile_rows, w) for w in range(tile_cols)],
            [(h, -1) for h in range(-1, tile_rows + 1)],
            [(h, tile_cols) for h in range(-1, tile_rows + 1)],
        ]

        def home(h, w):
            down, right = h // tile_rows, w // tile_cols
            h, w = h % tile_rows, w % tile_cols
            return down, right, (h % high, w % wide), (h // high) * reps_s + w // wide

        wanted = {c: [] for c in spots}
        for piece, members in enumerate(ring):
            for n, cell in enumerate(members):
                wanted[home(*cell)[2]].append((piece, n))
        edge = sorted((c for c in spots if wanted[c]), key=lambda c: -len(wanted[c]))
        slots = len(spots) // share
        edge_slots = -(-len(edge) // share)
        assert edge_slots < slots
        bounds = [0, edge_slots, slots]
        place, filled, load = {}, [0] * share, [0] * share
        for c in edge:
            owner = min((n for n in range(share) if filled[n] < edge_slots), key=lambda n: load[n])
            place[c] = (owner, filled[owner])
            filled[owner] += 1
            load[owner] += len(wanted[c])
        for c in spots:
            if c not in place:
                owner = min(range(share), key=lambda n: filled[n])
                place[c] = (owner, filled[owner])
                filled[owner] += 1

        def build(first, last):
            size = (last - first) * reps
            send = np.zeros((share * size, cells), np.float32)
            for h in range(tile_rows):
                for w in range(tile_cols):
                    owner, slot = place[(h % high, w % wide)]
                    if first <= slot < last:
                        rep = (h // high) * reps_s + w // wide
                        send[owner * size + (slot - first) * reps + rep, h * tile_cols + w] = 1
            count = (last - first) * groups
            seen = np.zeros((count,), np.int64)
            where = {}
            sort = np.zeros((devices * size, devices * size), np.float32)
            for source in range(devices):
                j = source % col_count
                for slot in range(last - first):
                    for r in range(reps_r):
                        for s in range(reps_s):
                            window = slot * groups + ((j * tile_cols + s * wide) % full) // wide
                            position = int(seen[window])
                            seen[window] += 1
                            chunk, lane = divmod(position, GROUP)
                            row = chunk * GROUP * count + window * GROUP + lane
                            where[source, slot, r * reps_s + s] = window * CELLS + position
                            sort[row, source * size + slot * reps + r * reps_s + s] = 1
            step = GROUP * count
            block = sort[:step, :step]
            assert (sort == np.kron(np.eye(CELLS // GROUP), block)).all()
            return send, block, where

        self.send_all, sort_all, _ = build(0, slots)
        self.send, self.sort, self.take = [], [], []
        for first, last in zip(bounds[:-1], bounds[1:]):
            send, block, where = build(first, last)
            if first == 0:
                around = where
            self.send.append(send)
            self.sort.append(block)
            self.take.append(sort_all[first * groups * GROUP : last * groups * GROUP])
        own = edge_slots * reps
        size = own + -(-max(load) // 8) * 8
        size = -(-size // 8) * 8
        back = np.zeros((share * size, cells), np.float32)
        for n in range(share):
            back[n * size : n * size + own] = self.send[0][n * own : (n + 1) * own]
        self.send[0] = back
        self.pieces = [np.zeros((len(members), share * size), np.float32) for members in ring]
        self.index = np.full((share, 1, devices * size), -1, np.int32)
        used = [own] * share
        for source, slot, rep in around:
            self.index[:, 0, source * size + slot * reps + rep] = around[source, slot, rep]
        for c in edge:
            owner, slot = place[c]
            for piece, n in wanted[c]:
                down, right, _, rep = home(*ring[piece][n])
                self.pieces[piece][n, owner * size + used[owner]] = 1
                for i in range(row_count):
                    for j in range(col_count):
                        if 0 <= i + down < row_count and 0 <= j + right < col_count:
                            source = (i + down) * col_count + j + right
                            target = (i * col_count + j) * size + used[owner]
                            self.index[owner, 0, target] = around[source, slot, rep]
                used[owner] += 1
        border = [(h, w) for h in (0, tile_rows - 1) for w in range(tile_cols)]
        border += [(h, w) for w in (0, tile_cols - 1) for h in range(tile_rows)]
        self.unpick = np.zeros((cells, len(border)), np.float32)
        for n, (h, w) in enumerate(border):
            if n < 2 * tile_cols or h not in (0, tile_rows - 1):
                self.unpick[h * tile_cols + w, n] = 1
        self.send_border = self.send_all @ self.unpick
        self.send_inner = self.send_all * (1 - self.unpick.sum(1))[None]
        self.columns = np.zeros((4 * tile_rows, cells), np.float32)
        for n, w in enumerate((0, 1, tile_cols - 2, tile_cols - 1)):
            for h in range(tile_rows):
                self.columns[n * tile_rows + h, h * tile_cols + w] = 1
        self.share = share
        self.windows = [m.shape[0] // GROUP for m in self.sort]
        self.rows = [batches * m.shape[0] for m in self.send]


def send_kernel(batches, x_ref, order, out):
    cells = x_ref.shape[0] // batches
    for b in range(batches):
        at = slice(b * cells, (b + 1) * cells)
        out[at, :] = dot(order[...], x_ref[at, :]).astype(BF16)


def convolve(pad, left_ref, right_ref, kern, side_l, side_r, out_ref):
    batches, rows, cols, feats = pad.shape
    rows -= 2
    four = 4
    width = 256
    for b in range(batches):
        if left_ref is None:
            side_l[b] = jnp.zeros(side_l.shape[1:], F32)
            side_r[b] = jnp.zeros(side_r.shape[1:], F32)
            continue
        left, right = left_ref[b].astype(F32), right_ref[b].astype(F32)
        side_l[b] = sum(kern[i][0] * left[i : i + rows] for i in range(3))
        side_r[b] = sum(kern[i][2] * right[i : i + rows] for i in range(3))
    spot = lax.broadcasted_iota(jnp.int32, (cols, width), 0)
    for c in range(feats // width):
        at = slice(c * width, (c + 1) * width)
        taps = [[kern[i][j][:, at] for j in range(3)] for i in range(3)]
        for b in range(batches):

            def step(n, carry, b=b, at=at, taps=taps):
                first = n * four
                x = [pad[b, first + r, :, at].astype(F32) for r in range(four + 2)]
                for r in range(four):
                    low, mid, high = (
                        taps[0][j] * x[r] + taps[1][j] * x[r + 1] + taps[2][j] * x[r + 2]
                        for j in range(3)
                    )
                    h = first + r
                    low = jnp.where(spot == 0, side_l[b, pl.ds(h, 1), at], pltpu.roll(low, 1, 0))
                    high = jnp.where(
                        spot == cols - 1, side_r[b, pl.ds(h, 1), at], pltpu.roll(high, cols - 1, 0)
                    )
                    where = pl.ds(pl.multiple_of((b * rows + h) * cols, cols), cols)
                    out_ref[where, at] = (x[r + 1] + (low + mid + high)).astype(BF16)
                return carry

            lax.fori_loop(0, rows // four, step, 0)


def taps_of(dw_ref, flipped):
    side = lambda n: 2 - n if flipped else n
    return [
        [dw_ref[side(i), side(j) : side(j) + 1, :].astype(F32) for j in range(3)] for i in range(3)
    ]


def norm(mixed, gain):
    mixed = mixed.astype(F32)
    mean = jnp.mean(mixed, axis=-1, keepdims=True)
    centred = mixed - mean
    rstd = lax.rsqrt(jnp.mean(centred * centred, axis=-1, keepdims=True) + 1e-05)
    return mean, rstd, (centred * rstd * gain).astype(BF16)


def inner_kernel(lat_ref, dw_ref, gain_ref, order, columns_ref, *refs):
    out, mixed_out, rows_ref, cols_ref, mixed_ref, pad_ref, normed_ref, side_l, side_r, sems = refs
    batches, rows, cols, feats = lat_ref.shape
    cells = rows * cols
    pad_ref[:, 1 : rows + 1] = lat_ref[...]
    pad_ref[:, 0] = jnp.zeros((batches, cols, feats), BF16)
    pad_ref[:, rows + 1] = jnp.zeros((batches, cols, feats), BF16)
    for b in range(batches):
        rows_ref[b, :2] = lat_ref[b, :2]
        rows_ref[b, 2:] = lat_ref[b, rows - 2 :]
        for h in range(rows):
            normed_ref[b * cells + h * cols : b * cells + (h + 1) * cols, :] = lat_ref[b, h]
        cols_ref[b] = dot(columns_ref[...], normed_ref[b * cells : (b + 1) * cells, :]).astype(BF16)
    convolve(pad_ref, None, None, taps_of(dw_ref, False), side_l, side_r, mixed_ref)
    copies = moves([(mixed_ref, mixed_out)], sems)
    block = 64

    def step(n, carry):
        at = pl.ds(pl.multiple_of(n * block, block), block)
        normed_ref[at, :] = norm(mixed_ref[at, :], gain_ref[...])[2]
        return carry

    lax.fori_loop(0, batches * cells // block, step, 0, unroll=2)
    send_kernel(batches, normed_ref, order, out)
    for copy in copies:
        copy.wait()


def edge_kernel(
    inner_ref, rows_ref, cols_ref, top_ref, bot_ref, left_ref, right_ref, dw_ref, gain_ref, order, out, mixed_ref
):
    batches, _, cols, feats = rows_ref.shape
    rows = cols_ref.shape[1] // 4
    size = out.shape[0] // batches
    taps = taps_of(dw_ref, False)
    spot = lax.broadcasted_iota(jnp.int32, (cols, feats), 0)

    def row(x, left, right):
        low, mid, high = (sum(taps[i][j] * x[i] for i in range(3)) for j in range(3))
        low = jnp.where(spot == 0, sum(taps[i][0] * left[i : i + 1] for i in range(3)), pltpu.roll(low, 1, 0))
        high = jnp.where(
            spot == cols - 1,
            sum(taps[i][2] * right[i : i + 1] for i in range(3)),
            pltpu.roll(high, cols - 1, 0),
        )
        return (x[1] + (low + mid + high)).astype(BF16)

    def column(x):
        low, mid, high = (sum(taps[i][j] * x[j][i : i + rows] for i in range(3)) for j in range(3))
        return (x[1][1 : rows + 1] + (low + mid + high)).astype(BF16)

    for b in range(batches):
        top, bot = top_ref[b].astype(F32), bot_ref[b].astype(F32)
        left, right = left_ref[b].astype(F32), right_ref[b].astype(F32)
        near = [rows_ref[b, n].astype(F32) for n in range(4)]
        both = cols_ref[b].astype(F32)
        longer = [
            jnp.concatenate([top[w : w + 1], both[n * rows : (n + 1) * rows], bot[w : w + 1]], axis=0)
            for n, w in enumerate((0, 1, cols - 2, cols - 1))
        ]
        mixed_ref[b] = jnp.concatenate(
            [
                row([top, near[0], near[1]], left[:3], right[:3]),
                row([near[2], near[3], bot], left[rows - 1 :], right[rows - 1 :]),
                column([left, longer[0], longer[1]]),
                column([longer[2], longer[3], right]),
            ],
            axis=0,
        )
        normed = norm(mixed_ref[b], gain_ref[...])[2]
        at = slice(b * size, (b + 1) * size)
        out[at, :] = inner_ref[at, :] + dot(order[...], normed).astype(BF16)


def patch_kernel(inner_ref, border_ref, unpick_ref, lat_ref, top_ref, bot_ref, *refs):
    mixed_out, stat_out, pad_out, mixed_ref, stat_ref, pad_ref, sems = refs
    batches, rows, cols, feats = lat_ref.shape
    cells = rows * cols
    pad_ref[:, 1 : rows + 1] = lat_ref[...]
    pad_ref[:, 0] = top_ref[...]
    pad_ref[:, rows + 1] = bot_ref[...]
    copies = moves([(pad_ref, pad_out)], sems.at[0:1])
    cell = lax.broadcasted_iota(jnp.int32, (cells, feats), 0)
    h, w = cell // cols, cell % cols
    inside = (h > 0) & (h < rows - 1) & (w > 0) & (w < cols - 1)
    for b in range(batches):
        at = slice(b * cells, (b + 1) * cells)
        patch = dot(unpick_ref[...], border_ref[b])
        mixed_ref[at, :] = jnp.where(inside, inner_ref[at, :].astype(F32), patch).astype(BF16)
    copies += moves([(mixed_ref, mixed_out)], sems.at[1:2])
    block = 64

    def step(n, carry):
        at = pl.ds(pl.multiple_of(n * block, block), block)
        mean, rstd, _ = norm(mixed_ref[at, :], 1.0)
        stat_ref[at, 0:1] = mean
        stat_ref[at, 1:2] = rstd
        return carry

    lax.fori_loop(0, batches * cells // block, step, 0, unroll=2)
    copies += moves([(stat_ref, stat_out)], sems.at[2:3])
    for copy in copies:
        copy.wait()


def gather_rows(source, take_ref, target):
    count = target.shape[0] // CELLS
    whole = source.shape[0] * GROUP // CELLS
    for p in range(CELLS // GROUP):
        ordered = dot(take_ref[...], source[p * whole : (p + 1) * whole, :]).astype(BF16)
        for w in range(count):
            target[w * CELLS + p * GROUP : w * CELLS + (p + 1) * GROUP, :] = ordered[
                w * GROUP : (w + 1) * GROUP
            ]


def grads_kernel(parts, g_ref, wout_ref, *refs):
    for n in range(parts):
        gw, datt = refs[parts + 2 * n : parts + 2 * n + 2]
        gather_rows(g_ref, refs[n], gw)
        rows = gw.shape[0]
        for first in range(0, rows, 256):
            at = slice(first, min(first + 256, rows))
            datt[at, :] = dot(gw[at, :], wout_ref[...], ((1,), (1,))).astype(BF16)


def window_kernel(counts, before, n_hbm, datt_hbm, take_ref, back_ref, wqkv_hbm, *refs):
    n_ref, wqkv_ref, nw, packed, datt, att, dpacked, head_mask, half_mask, in_sems = refs[-10:]
    if counts is None:
        dn_ref, *results, out_sems = refs[:5]
    else:
        mine_ref, gw_hbm, *old = refs[: 4 * before + 2]
        dn_ref, keep_hbm, give_hbm, gw, acc, keep_ref, give_ref, out_sems, old_sems, *old_refs = refs[
            4 * before + 2 : -10
        ]
        late = moves([(gw_hbm, gw), *zip(old, old_refs)], old_sems)
    loads = moves([(n_hbm, n_ref), (wqkv_hbm, wqkv_ref), (datt_hbm, datt)], in_sems)
    rows, feats = nw.shape
    count = rows // CELLS
    part = GROUP * count
    tiles = feats // 256
    scale = HEAD ** (-0.5)
    block = 256 if rows % 256 == 0 else CELLS

    head_mask[...] = (
        (lax.broadcasted_iota(jnp.int32, (4 * CELLS, 256), 1) // HEAD) % 4
        == lax.broadcasted_iota(jnp.int32, (4 * CELLS, 256), 0) // CELLS
    ).astype(F32).astype(BF16)
    half_mask[...] = (
        lax.broadcasted_iota(jnp.int32, (2 * CELLS, 256), 1) // 128
        == lax.broadcasted_iota(jnp.int32, (2 * CELLS, 256), 0) // CELLS
    ).astype(F32).astype(BF16)

    loads[0].wait()
    gather_rows(n_ref, take_ref, nw)
    loads[1].wait()

    def project(n, carry):
        at = pl.ds(pl.multiple_of(n * block, block), block)
        packed[at, :] = dot(nw[at, :], wqkv_ref[...]).astype(BF16)
        return carry

    lax.fori_loop(0, rows // block, project, 0)
    loads[2].wait()

    lane = lax.broadcasted_iota(jnp.int32, (CELLS, 256), 1)
    lane_half = lane < 128
    lane_head = (lane // HEAD) % 4

    def fold_heads(full):
        out = full[3 * CELLS :]
        for h in (2, 1, 0):
            out = jnp.where(lane_head == h, full[h * CELLS : (h + 1) * CELLS], out)
        return out

    def one(n, carry):
        at = pl.ds(pl.multiple_of(n * CELLS, CELLS), CELLS)
        for t in range(tiles):
            cols = [slice(p * feats + t * 256, p * feats + (t + 1) * 256) for p in range(3)]
            query = packed[at, cols[0]]
            key = packed[at, cols[1]]
            value = packed[at, cols[2]]
            grad = datt[at, t * 256 : (t + 1) * 256]
            key_big = jnp.concatenate([key] * 4, axis=0) * head_mask[...]
            value_big = jnp.concatenate([value] * 4, axis=0) * head_mask[...]
            query_two = jnp.concatenate([query] * 2, axis=0) * half_mask[...]
            grad_two = jnp.concatenate([grad] * 2, axis=0) * half_mask[...]
            scores = (dot(key_big, query_two, ((1,), (1,))) * scale).reshape(4, CELLS, 2 * CELLS)
            d_probs = dot(value_big, grad_two, ((1,), (1,))).reshape(4, CELLS, 2 * CELLS)
            raised = jnp.exp(scores - jnp.max(scores, axis=1, keepdims=True))
            probs = raised * (1.0 / jnp.sum(raised, axis=1, keepdims=True))
            probs_b = probs.astype(BF16).reshape(4 * CELLS, 2 * CELLS)
            inner = jnp.sum(probs * d_probs, axis=1, keepdims=True)
            d_scores = (
                (probs * (d_probs - inner) * scale).astype(BF16).reshape(4 * CELLS, 2 * CELLS)
            )
            out = dot(probs_b, value_big, ((0,), (0,)))
            att[at, t * 256 : (t + 1) * 256] = jnp.where(
                lane_half, out[:CELLS], out[CELLS:]
            ).astype(BF16)
            d_query = dot(d_scores, key_big, ((0,), (0,)))
            dpacked[at, cols[0]] = jnp.where(
                lane_half, d_query[:CELLS], d_query[CELLS:]
            ).astype(BF16)
            dpacked[at, cols[1]] = fold_heads(dot(d_scores, query_two)).astype(BF16)
            dpacked[at, cols[2]] = fold_heads(dot(probs_b, grad_two)).astype(BF16)
        return carry

    lax.fori_loop(0, count, one, 0, unroll=UNROLL)
    if counts is None:
        stores = moves(list(zip((nw, att, dpacked), results)), out_sems)
    else:
        for copy in late:
            copy.wait()
        parts = [old_refs[4 * n : 4 * n + 4] for n in range(before)] + [(nw, att, dpacked, gw)]
        weight_sums(parts, counts, mine_ref[0], acc, keep_ref, give_ref)
        stores = moves([(give_ref, give_hbm), (keep_ref, keep_hbm)], out_sems)

    def back(n, carry):
        at = pl.ds(pl.multiple_of(n * block, block), block)
        datt[at, :] = dot(dpacked[at, :], wqkv_ref[...], ((1,), (1,))).astype(BF16)
        return carry

    lax.fori_loop(0, rows // block, back, 0)
    if back_ref.shape[0] == 1:
        order = (
            lax.broadcasted_iota(jnp.int32, (rows, dn_ref.shape[0]), 0) == back_ref[...]
        ).astype(F32).astype(BF16)
        dn_ref[...] = dot(order, datt[...], ((0,), (0,))).astype(BF16)
    else:
        for p in range(CELLS // GROUP):
            ordered = jnp.concatenate(
                [
                    datt[w * CELLS + p * GROUP : w * CELLS + (p + 1) * GROUP, :]
                    for w in range(count)
                ],
                axis=0,
            )
            dn_ref[p * part : (p + 1) * part, :] = dot(
                back_ref[...], ordered, ((0,), (0,))
            ).astype(BF16)
    for copy in stores:
        copy.wait()


def place_of(i, j, row_count, chips):
    return (j % 2) * row_count * chips + i * chips + j // 2


def weight_sums(parts, counts, mine, acc, keep_ref, give_ref):
    feats = acc.shape[0]
    row_count, chips = counts
    devices = 2 * row_count * chips
    size = feats // devices
    half = devices // 2
    for left, right, start in ((0, 2, 0), (1, 3, 3 * feats)):
        turned = [part[left][...].T for part in parts]
        for t in range(parts[0][right].shape[1] // 256):
            at = slice(t * 256, (t + 1) * 256)
            acc[:, start + t * 256 : start + (t + 1) * 256] = sum(
                dot(x, part[right][:, at]) for x, part in zip(turned, parts)
            ).astype(BF16)
    if size % 16:
        source = lax.broadcasted_iota(jnp.int32, (feats, feats), 1)
        device = source // size
        place = place_of(device // (2 * chips), device % (2 * chips), row_count, chips)
        target = jnp.bitwise_xor(mine, place) * size + source % size
        order = (lax.broadcasted_iota(jnp.int32, (feats, feats), 0) == target).astype(F32).astype(BF16)
        keep_ref[...] = dot(order[: feats // 2], acc[...]).astype(BF16)
        give_ref[...] = dot(order[feats // 2 :], acc[...]).astype(BF16)
        return
    for n in range(devices):
        place = place_of(n // (2 * chips), n % (2 * chips), row_count, chips)
        block = jnp.bitwise_xor(mine, place)
        rows = acc[n * size : (n + 1) * size, :]
        at = pl.ds(pl.multiple_of((block % half) * size, size), size)

        @pl.when(block < half)
        def _(rows=rows, at=at):
            keep_ref[at, :] = rows

        @pl.when(block >= half)
        def _(rows=rows, at=at):
            give_ref[at, :] = rows


def norm_back(d_normed, nhat, rstd, grad, gain):
    scaled = d_normed * gain
    return (
        grad.astype(F32)
        + rstd
        * (
            scaled
            - jnp.mean(scaled, axis=-1, keepdims=True)
            - nhat * jnp.mean(scaled * nhat, axis=-1, keepdims=True)
        )
    ).astype(BF16)


def border_kernel(dn_ref, gain_ref, *refs):
    batches = refs[4].shape[0]
    feats = dn_ref.shape[1]
    size = dn_ref.shape[0] // batches
    for pick, pair, out in zip(refs[:4], refs[4:8], refs[8:]):
        for b in range(batches):
            d_normed = dot(pick[...], dn_ref[b * size : (b + 1) * size, :])
            mixed = pair[b, :, :feats].astype(F32)
            centred = mixed - jnp.mean(mixed, axis=-1, keepdims=True)
            rstd = lax.rsqrt(jnp.mean(centred * centred, axis=-1, keepdims=True) + 1e-05)
            out[b] = norm_back(d_normed, centred * rstd, rstd, pair[b, :, feats:], gain_ref[...])


def sums_kernel(count, *refs):
    orders, refs = refs[:count], refs[count:]
    hbm, refs = refs[:count], refs[count:]
    hbm, (left_ref, right_ref, gain_ref) = hbm + refs[:4], refs[4:7]
    out_ref, sums_ref, dn, side_l, side_r = refs[7:12]
    here, sems = refs[12:-1], refs[-1]
    parts = here[:count]
    stat_ref, mixed_ref, grad_ref, pad_ref = here[count:]
    loads = moves(list(zip(hbm, here)), sems)
    batches, rows, cols, feats = pad_ref.shape
    rows -= 2
    cells = rows * cols
    for copy in loads[:count]:
        copy.wait()
    for b in range(batches):
        total = None
        for order, part in zip(orders, parts):
            size = part.shape[0] // batches
            term = dot(order[...], part[b * size : (b + 1) * size, :])
            total = term if total is None else total + term
        dn[b * cells : (b + 1) * cells, :] = total
    block = 64
    for copy in loads[count : count + 3]:
        copy.wait()

    def norm(n, gain_sum):
        at = pl.ds(pl.multiple_of(n * block, block), block)
        d_normed = dn[at, :]
        rstd = stat_ref[at, 1:2]
        nhat = (mixed_ref[at, :].astype(F32) - stat_ref[at, 0:1]) * rstd
        out_ref[at, :] = norm_back(d_normed, nhat, rstd, grad_ref[at, :], gain_ref[...])
        return gain_sum + jnp.sum((d_normed * nhat).reshape(block // 8, 8, feats), axis=0)

    gain_sum = lax.fori_loop(
        0, batches * cells // block, norm, jnp.zeros((8, feats), F32), unroll=2
    )
    sums_ref[9:10, :] = jnp.sum(gain_sum, axis=0, keepdims=True)
    sums_ref[10:, :] = jnp.zeros((sums_ref.shape[0] - 10, feats), F32)
    loads[count + 3].wait()

    four = 4
    width = 256
    spot = lax.broadcasted_iota(jnp.int32, (cols, width), 0)
    fold = lambda v: jnp.sum(v.reshape(cols // 8, 8, width), axis=0)
    for c in range(feats // width):
        lanes = slice(c * width, (c + 1) * width)
        sums = [jnp.zeros((8, width), F32) for _ in range(9)]
        for b in range(batches):

            def step(n, sums, b=b, lanes=lanes):
                start = n * four
                x = [pad_ref[b, start + r, :, lanes].astype(F32) for r in range(four + 2)]
                sums = list(sums)
                for r in range(four):
                    h = start + r
                    at = pl.ds(pl.multiple_of((b * rows + h) * cols, cols), cols)
                    d_mixed = out_ref[at, lanes].astype(F32)
                    side_l[b, pl.ds(h, 1), lanes] = d_mixed[:1]
                    side_r[b, pl.ds(h, 1), lanes] = d_mixed[cols - 1 :]
                    moved = (
                        jnp.where(spot == cols - 1, 0.0, pltpu.roll(d_mixed, cols - 1, 0)),
                        d_mixed,
                        jnp.where(spot == 0, 0.0, pltpu.roll(d_mixed, 1, 0)),
                    )
                    for i in range(3):
                        for j in range(3):
                            sums[3 * i + j] = sums[3 * i + j] + fold(moved[j] * x[r + i])
                return tuple(sums)

            sums = lax.fori_loop(0, rows // four, step, tuple(sums))
        for n in range(9):
            sums_ref[n : n + 1, lanes] = jnp.sum(sums[n], axis=0, keepdims=True)
    for i in range(3):
        for b in range(batches):
            left, right = left_ref[b].astype(F32), right_ref[b].astype(F32)
            sums_ref[3 * i : 3 * i + 1, :] += jnp.sum(
                side_l[b] * left[i : i + rows], axis=0, keepdims=True
            )
            sums_ref[3 * i + 2 : 3 * i + 3, :] += jnp.sum(
                side_r[b] * right[i : i + rows], axis=0, keepdims=True
            )


def spread_kernel(d_ref, top_ref, bot_ref, left_ref, right_ref, dw_ref, out_ref, pad, side_l, side_r):
    batches, rows, cols, feats = pad.shape
    rows -= 2
    for b in range(batches):
        for h in range(rows):
            pad[b, h + 1] = d_ref[(b * rows + h) * cols : (b * rows + h + 1) * cols, :]
    pad[:, 0] = top_ref[...]
    pad[:, rows + 1] = bot_ref[...]
    convolve(pad, left_ref, right_ref, taps_of(dw_ref, True), side_l, side_r, out_ref)


def finish_kernel(*refs):
    *parts, qkv_ref, wout_ref, gain_ref, kernel_ref = refs
    feats = wout_ref.shape[1]
    level = total([part[...].astype(F32) for part in parts])
    qkv_ref[...] = level[:, : 3 * feats]
    wout_ref[...] = level[:, 3 * feats : 4 * feats]
    sums = level[:, 4 * feats :]
    gain_ref[...] = sums[9:10]
    for i in range(3):
        kernel_ref[i] = sums[3 * i : 3 * i + 3]


def call(body, outs, scratch, args, micros, name, hbm_ins=(), hbm_outs=(), scalars=(), limit=56 << 20):
    moved = sum(int(np.prod(o.shape)) * o.dtype.itemsize for o in (*outs, *args))
    vmem = pl.BlockSpec(memory_space=pltpu.VMEM)
    hbm = pl.BlockSpec(memory_space=pltpu.HBM)
    smem = pl.BlockSpec(memory_space=pltpu.SMEM)
    return pl.pallas_call(
        body,
        out_shape=outs,
        in_specs=[
            smem if n in scalars else hbm if n in hbm_ins else vmem for n in range(len(args))
        ],
        out_specs=[hbm if n in hbm_outs else vmem for n in range(len(outs))],
        scratch_shapes=scratch,
        compiler_params=pltpu.CompilerParams(vmem_limit_bytes=limit),
        cost_estimate=pl.CostEstimate(
            flops=micros * 10**9, bytes_accessed=moved, transcendentals=0
        ),
        name=name,
    )(*args)


def shape(dims, dtype):
    return jax.ShapeDtypeStruct(tuple(dims), dtype)


def shifted(cells, axis, step):
    count = lax.axis_size(axis)
    return lax.ppermute(cells, axis, [(n, n + step) for n in range(count) if 0 <= n + step < count])


def halos(top, bottom, left, right):
    above = shifted(bottom, "row", 1)
    below = shifted(top, "row", -1)
    last = above.shape[1] - 1
    column = lambda own, at: jnp.concatenate(
        [above[:, at : at + 1], own, below[:, at : at + 1]], axis=1
    )
    from_left = shifted(column(right, last), "col", 1)
    from_right = shifted(column(left, 0), "col", -1)
    return above, below, from_left, from_right


def swap(x, axis, step):
    return lax.ppermute(x, axis, [(n, n ^ step) for n in range(lax.axis_size(axis))])


def total(values):
    while len(values) > 1:
        values = [a + b for a, b in zip(values[::2], values[1::2])]
    return values[0]


def scatter(blocks, sums, axis, unit, count):
    size = blocks.shape[0] // count
    sums = sums.reshape(size, -1)
    load = lambda n: jnp.concatenate([blocks[n * size : (n + 1) * size], sums], axis=1).astype(BF16)
    own = jnp.concatenate([blocks[:size], sums], axis=1)
    return [own, *(swap(load(n), axis, unit * n) for n in range(1, count))]


def shards(plan, latent, w_qkv, w_out, ln_gain, dw_kernel, grad_out):
    batches, rows, cols, feats = latent.shape
    row_count, col_count = lax.axis_size("row"), lax.axis_size("col")
    cells = batches * rows * cols
    parts = len(plan.rows)
    gain = ln_gain.reshape(1, feats)
    send = jnp.asarray(plan.send_all, BF16)
    owner = lax.axis_index("row") * col_count + lax.axis_index("col")
    index = lax.dynamic_index_in_dim(jnp.asarray(plan.index), owner % plan.share, keepdims=False)
    back = [jnp.asarray(np.ascontiguousarray(m.T), BF16) for m in plan.send]
    sort = [index, *(jnp.asarray(m, BF16) for m in plan.sort[1:])]
    grouped = [shape((n * CELLS, feats), BF16) for n in plan.windows]
    take = [jnp.asarray(m, BF16) for m in plan.take]
    chunks = [shape((n, feats), BF16) for n in plan.rows]
    trade = lambda x: lax.all_to_all(x, AXES, split_axis=0, concat_axis=0, tiled=True)
    grad_flat = grad_out.reshape(cells, feats)

    flat = shape((cells, feats), BF16)
    (grad_sent,) = call(
        functools.partial(send_kernel, batches), [flat], [], [grad_flat, send], 3, "grad_send"
    )
    grad_win = trade(grad_sent)

    above, below, left, right = halos(latent[:, 0], latent[:, -1], latent[:, :, 0], latent[:, :, -1])
    padded = (batches, rows + 2, cols, feats)
    side = pltpu.VMEM((batches, rows, feats), F32)
    stat_shape = (cells, 2)
    const = lambda m: jnp.asarray(m, BF16)
    sent, mixed_inner, own_rows, own_cols = call(
        inner_kernel,
        [
            flat,
            flat,
            shape((batches, 4, cols, feats), BF16),
            shape((batches, 4 * rows, feats), BF16),
        ],
        [
            pltpu.VMEM((cells, feats), BF16),
            pltpu.VMEM(padded, BF16),
            pltpu.VMEM((cells, feats), BF16),
            side,
            side,
            pltpu.SemaphoreType.DMA((1,)),
        ],
        [latent, dw_kernel, gain, const(plan.send_inner), const(plan.columns)],
        6,
        "inner",
        limit=50 << 20,
        hbm_outs=(1,),
    )
    normed, mixed_border = call(
        edge_kernel,
        [flat, shape((batches, plan.unpick.shape[1], feats), BF16)],
        [],
        [sent, own_rows, own_cols, above, below, left, right, dw_kernel, gain, const(plan.send_border)],
        3,
        "edge",
        limit=50 << 20,
    )
    normed_win = trade(normed)
    ends = (0, cols, 2 * cols, 2 * cols + rows, 2 * cols + 2 * rows)
    grad_ends = (grad_out[:, 0], grad_out[:, -1], grad_out[:, :, 0], grad_out[:, :, -1])
    pairs = halos(
        *(
            jnp.concatenate([mixed_border[:, first:last], x], axis=-1)
            for first, last, x in zip(ends[:-1], ends[1:], grad_ends)
        )
    )
    mixed, stat, pad = call(
        patch_kernel,
        [flat, shape(stat_shape, F32), shape(padded, BF16)],
        [
            pltpu.VMEM((cells, feats), BF16),
            pltpu.VMEM(stat_shape, F32),
            pltpu.VMEM(padded, BF16),
            pltpu.SemaphoreType.DMA((3,)),
        ],
        [mixed_inner, mixed_border, const(plan.unpick), latent, above, below],
        4,
        "patch",
        limit=50 << 20,
        hbm_outs=(0, 1, 2),
    )
    normed_win, *pairs = lax.optimization_barrier((normed_win, *pairs))

    chips = col_count // 2
    ahead = call(
        functools.partial(grads_kernel, parts),
        [grouped[n // 2] for n in range(2 * parts)],
        [],
        [grad_win, w_out, *take],
        4,
        "grads",
        limit=50 << 20,
    )
    mine = place_of(lax.axis_index("row"), lax.axis_index("col"), row_count, chips).astype(jnp.int32).reshape(1)
    half = shape((feats // 2, 4 * feats), BF16)
    d_parts, kept = [], []
    for n in range(parts):
        count = plan.windows[n] * CELLS
        last = n == parts - 1
        mat = lambda width: pltpu.VMEM((count, width), BF16)
        args = [normed_win, ahead[2 * n + 1], take[n], sort[n], w_qkv]
        if last:
            outs = [chunks[n], half, half]
            args += [mine, ahead[2 * n], *kept]
            scratch = [
                mat(feats),
                pltpu.VMEM((feats, 4 * feats), BF16),
                pltpu.VMEM(half.shape, BF16),
                pltpu.VMEM(half.shape, BF16),
                pltpu.SemaphoreType.DMA((2,)),
                pltpu.SemaphoreType.DMA((1 + len(kept),)),
                *(pltpu.VMEM(x.shape, BF16) for x in kept),
            ]
        else:
            outs = [chunks[n], grouped[n], grouped[n], shape((count, 3 * feats), BF16)]
            scratch = [pltpu.SemaphoreType.DMA((3,))]
        d_chunk, *saved = call(
            functools.partial(window_kernel, (row_count, chips) if last else None, n),
            outs,
            [
                *scratch,
                pltpu.VMEM((cells, feats), BF16),
                pltpu.VMEM((feats, 3 * feats), BF16),
                mat(feats),
                mat(3 * feats),
                mat(feats),
                mat(feats),
                mat(3 * feats),
                pltpu.VMEM((4 * CELLS, 256), BF16),
                pltpu.VMEM((2 * CELLS, 256), BF16),
                pltpu.SemaphoreType.DMA((3,)),
            ],
            args,
            2 + 20 * count // cells,
            "windows",
        limit=56 << 20,
            hbm_ins=(0, 1, 4, *range(6, len(args))),
            hbm_outs=tuple(range(1, len(outs))),
            scalars=(5,),
        )
        kept += [*saved, ahead[2 * n]]
        d_parts.append(trade(d_chunk))
    keep, give = saved

    d_halos = call(
        border_kernel,
        [shape((*x.shape[:2], feats), BF16) for x in pairs],
        [],
        [d_parts[0], gain, *(jnp.asarray(m, BF16) for m in plan.pieces), *pairs],
        3,
        "border",
        limit=50 << 20,
    )
    weights = (keep.astype(F32) + swap(give, "col", 1).astype(F32)).astype(BF16)
    d_mixed, sums = call(
        functools.partial(sums_kernel, parts),
        [flat, shape((16, feats), F32)],
        [
            pltpu.VMEM((cells, feats), F32),
            side,
            side,
            *(pltpu.VMEM((n, feats), BF16) for n in plan.rows),
            pltpu.VMEM(stat_shape, F32),
            pltpu.VMEM((cells, feats), BF16),
            pltpu.VMEM((cells, feats), BF16),
            pltpu.VMEM(padded, BF16),
            pltpu.SemaphoreType.DMA((parts + 4,)),
        ],
        [*back, *d_parts, stat, mixed, grad_flat, pad, left, right, gain],
        7,
        "sums",
        limit=50 << 20,
        hbm_ins=tuple(range(parts, 2 * parts + 4)),
    )
    wide = 4 * feats
    size = weights.shape[0] // row_count
    gives = [
        swap(weights[n * size : (n + 1) * size], "row", n) for n in range(1, row_count)
    ]
    sums, weights, *gives = lax.optimization_barrier((sums, weights, *gives))
    weights = total([x.astype(F32) for x in (weights[:size], *gives)])
    sums = sums + swap(sums, "col", 1)
    sums = total([sums, *(swap(sums, "row", n) for n in range(1, row_count))])
    sums, d_mixed = lax.optimization_barrier((sums, d_mixed))
    (grad_latent,) = call(
        spread_kernel,
        [flat],
        [pltpu.VMEM(padded, BF16), side, side],
        [d_mixed, *d_halos, dw_kernel],
        5,
        "spread",
        limit=50 << 20,
    )
    level = scatter(weights, sums, "col", 2, chips)
    grad_latent = grad_latent.reshape(latent.shape)
    size = level[0].shape[0]
    if size == 16:
        qkv, wout, gain_sum, kernel_sum = call(
            finish_kernel,
            [
                shape((size, 3 * feats), F32),
                shape((size, feats), F32),
                shape((1, feats), F32),
                shape((3, 3, feats), F32),
            ],
            [],
            level,
            1,
            "finish",
            limit=50 << 20,
        )
        return grad_latent, qkv, wout, gain_sum.reshape(feats), kernel_sum
    level = total([x.astype(F32) for x in level])
    sums = level[:, wide:].reshape(16, feats)
    return (
        grad_latent,
        level[:, : 3 * feats],
        level[:, 3 * feats : wide],
        sums[9],
        sums[:9].reshape(3, 3, feats),
    )


def solution(mesh):
    row_count, col_count = mesh.shape["row"], mesh.shape["col"]

    def run(latent, w_qkv, w_out, ln_gain, dw_kernel, grad_out):
        batches, rows, cols, _ = latent.shape
        plan = Plan(batches, rows // row_count, cols // col_count, row_count, col_count)
        in_specs = (P(None, "row", "col", None), P(), P(), P(), P(), P(None, "row", "col", None))
        out_specs = (
            P(None, "row", "col", None),
            P(AXES, None),
            P(AXES, None),
            P(),
            P(),
        )
        return jax.shard_map(
            functools.partial(shards, plan),
            mesh=mesh,
            in_specs=in_specs,
            out_specs=out_specs,
            check_vma=False,
        )(latent, w_qkv, w_out, ln_gain, dw_kernel, grad_out)

    return run
```

```python
import functools

import jax
import jax.numpy as jnp
import numpy as np
from jax import lax
from jax.experimental import pallas as pl
from jax.experimental.pallas import tpu as pltpu
from jax.sharding import PartitionSpec as P

HEADS = 16
HEAD = 32
GRID = 8
CELLS = GRID * GRID
AXES = ("row", "col")
F32 = jnp.float32
BF16 = jnp.bfloat16
LIMIT = 56 * 1024 * 1024
UNROLL = 4
GROUP = 16


def dot(left, right, dims=((1,), (0,))):
    return lax.dot_general(left, right, (dims, ((), ())), preferred_element_type=F32)


def moves(pairs, sems):
    copies = [pltpu.make_async_copy(a, b, sems.at[n]) for n, (a, b) in enumerate(pairs)]
    for copy in copies:
        copy.start()
    return copies


class Plan:
    def __init__(self, batches, tile_rows, tile_cols, row_count, col_count):
        devices = row_count * col_count
        high = tile_rows * row_count // GRID
        full = tile_cols * col_count // GRID
        wide = min(full, tile_cols)
        groups = full // wide
        reps_r = tile_rows // high
        reps_s = tile_cols // wide
        reps = reps_r * reps_s
        share = devices // batches
        spots = [(a, e) for a in range(high) for e in range(wide)]
        cells = tile_rows * tile_cols
        ring = [
            [(-1, w) for w in range(tile_cols)],
            [(tile_rows, w) for w in range(tile_cols)],
            [(h, -1) for h in range(-1, tile_rows + 1)],
            [(h, tile_cols) for h in range(-1, tile_rows + 1)],
        ]

        def home(h, w):
            down, right = h // tile_rows, w // tile_cols
            h, w = h % tile_rows, w % tile_cols
            return down, right, (h % high, w % wide), (h // high) * reps_s + w // wide

        wanted = {c: [] for c in spots}
        for piece, members in enumerate(ring):
            for n, cell in enumerate(members):
                wanted[home(*cell)[2]].append((piece, n))
        edge = sorted((c for c in spots if wanted[c]), key=lambda c: -len(wanted[c]))
        slots = len(spots) // share
        edge_slots = -(-len(edge) // share)
        assert edge_slots < slots
        bounds = [0, edge_slots, slots]
        place, filled, load = {}, [0] * share, [0] * share
        for c in edge:
            owner = min((n for n in range(share) if filled[n] < edge_slots), key=lambda n: load[n])
            place[c] = (owner, filled[owner])
            filled[owner] += 1
            load[owner] += len(wanted[c])
        for c in spots:
            if c not in place:
                owner = min(range(share), key=lambda n: filled[n])
                place[c] = (owner, filled[owner])
                filled[owner] += 1

        def build(first, last):
            size = (last - first) * reps
            send = np.zeros((share * size, cells), np.float32)
            for h in range(tile_rows):
                for w in range(tile_cols):
                    owner, slot = place[(h % high, w % wide)]
                    if first <= slot < last:
                        rep = (h // high) * reps_s + w // wide
                        send[owner * size + (slot - first) * reps + rep, h * tile_cols + w] = 1
            count = (last - first) * groups
            seen = np.zeros((count,), np.int64)
            where = {}
            sort = np.zeros((devices * size, devices * size), np.float32)
            for source in range(devices):
                j = source % col_count
                for slot in range(last - first):
                    for r in range(reps_r):
                        for s in range(reps_s):
                            window = slot * groups + ((j * tile_cols + s * wide) % full) // wide
                            position = int(seen[window])
                            seen[window] += 1
                            chunk, lane = divmod(position, GROUP)
                            row = chunk * GROUP * count + window * GROUP + lane
                            where[source, slot, r * reps_s + s] = window * CELLS + position
                            sort[row, source * size + slot * reps + r * reps_s + s] = 1
            step = GROUP * count
            block = sort[:step, :step]
            assert (sort == np.kron(np.eye(CELLS // GROUP), block)).all()
            return send, block, where

        self.send_all, sort_all, _ = build(0, slots)
        self.send, self.sort, self.take = [], [], []
        for first, last in zip(bounds[:-1], bounds[1:]):
            send, block, where = build(first, last)
            if first == 0:
                around = where
            self.send.append(send)
            self.sort.append(block)
            self.take.append(sort_all[first * groups * GROUP : last * groups * GROUP])
        own = edge_slots * reps
        size = own + -(-max(load) // 8) * 8
        size = -(-size // 8) * 8
        back = np.zeros((share * size, cells), np.float32)
        for n in range(share):
            back[n * size : n * size + own] = self.send[0][n * own : (n + 1) * own]
        self.send[0] = back
        self.pieces = [np.zeros((len(members), share * size), np.float32) for members in ring]
        self.index = np.full((share, 1, devices * size), -1, np.int32)
        used = [own] * share
        for source, slot, rep in around:
            self.index[:, 0, source * size + slot * reps + rep] = around[source, slot, rep]
        for c in edge:
            owner, slot = place[c]
            for piece, n in wanted[c]:
                down, right, _, rep = home(*ring[piece][n])
                self.pieces[piece][n, owner * size + used[owner]] = 1
                for i in range(row_count):
                    for j in range(col_count):
                        if 0 <= i + down < row_count and 0 <= j + right < col_count:
                            source = (i + down) * col_count + j + right
                            target = (i * col_count + j) * size + used[owner]
                            self.index[owner, 0, target] = around[source, slot, rep]
                used[owner] += 1
        border = [(h, w) for h in (0, tile_rows - 1) for w in range(tile_cols)]
        border += [(h, w) for w in (0, tile_cols - 1) for h in range(tile_rows)]
        self.unpick = np.zeros((cells, len(border)), np.float32)
        for n, (h, w) in enumerate(border):
            if n < 2 * tile_cols or h not in (0, tile_rows - 1):
                self.unpick[h * tile_cols + w, n] = 1
        self.send_border = self.send_all @ self.unpick
        self.send_inner = self.send_all * (1 - self.unpick.sum(1))[None]
        self.columns = np.zeros((4 * tile_rows, cells), np.float32)
        for n, w in enumerate((0, 1, tile_cols - 2, tile_cols - 1)):
            for h in range(tile_rows):
                self.columns[n * tile_rows + h, h * tile_cols + w] = 1
        self.share = share
        self.windows = [m.shape[0] // GROUP for m in self.sort]
        self.rows = [batches * m.shape[0] for m in self.send]


def send_kernel(batches, x_ref, order, out):
    cells = x_ref.shape[0] // batches
    for b in range(batches):
        at = slice(b * cells, (b + 1) * cells)
        out[at, :] = dot(order[...], x_ref[at, :]).astype(BF16)


def grad_kernel(batches, x_hbm, order_hbm, out_hbm, x_ref, order_ref, out_ref, sems):
    cells = x_ref.shape[0] // batches
    at = [pl.ds(b * cells, cells) for b in range(batches)]
    loads = moves([(order_hbm, order_ref), *((x_hbm.at[a], x_ref.at[a]) for a in at)], sems)
    stores = []
    loads[0].wait()
    for b, a in enumerate(at):
        loads[1 + b].wait()
        out_ref[a, :] = dot(order_ref[...], x_ref[a, :]).astype(BF16)
        stores += moves([(out_ref.at[a], out_hbm.at[a])], sems.at[1 + batches + b : 2 + batches + b])
    for copy in stores:
        copy.wait()


def convolve(pad, left_ref, right_ref, kern, side_l, side_r, out_ref):
    batches, rows, cols, feats = pad.shape
    rows -= 2
    four = 4
    width = 256
    for b in range(batches):
        if left_ref is None:
            side_l[b] = jnp.zeros(side_l.shape[1:], F32)
            side_r[b] = jnp.zeros(side_r.shape[1:], F32)
            continue
        left, right = left_ref[b].astype(F32), right_ref[b].astype(F32)
        side_l[b] = sum(kern[i][0] * left[i : i + rows] for i in range(3))
        side_r[b] = sum(kern[i][2] * right[i : i + rows] for i in range(3))
    spot = lax.broadcasted_iota(jnp.int32, (cols, width), 0)
    for c in range(feats // width):
        at = slice(c * width, (c + 1) * width)
        taps = [[kern[i][j][:, at] for j in range(3)] for i in range(3)]
        for b in range(batches):

            def step(n, carry, b=b, at=at, taps=taps):
                first = n * four
                x = [pad[b, first + r, :, at].astype(F32) for r in range(four + 2)]
                for r in range(four):
                    low, mid, high = (
                        taps[0][j] * x[r] + taps[1][j] * x[r + 1] + taps[2][j] * x[r + 2]
                        for j in range(3)
                    )
                    h = first + r
                    low = jnp.where(spot == 0, side_l[b, pl.ds(h, 1), at], pltpu.roll(low, 1, 0))
                    high = jnp.where(
                        spot == cols - 1, side_r[b, pl.ds(h, 1), at], pltpu.roll(high, cols - 1, 0)
                    )
                    where = pl.ds(pl.multiple_of((b * rows + h) * cols, cols), cols)
                    out_ref[where, at] = (x[r + 1] + (low + mid + high)).astype(BF16)
                return carry

            lax.fori_loop(0, rows // four, step, 0)


def taps_of(dw_ref, flipped):
    side = lambda n: 2 - n if flipped else n
    return [
        [dw_ref[side(i), side(j) : side(j) + 1, :].astype(F32) for j in range(3)] for i in range(3)
    ]


def norm(mixed, gain):
    mixed = mixed.astype(F32)
    mean = jnp.mean(mixed, axis=-1, keepdims=True)
    centred = mixed - mean
    rstd = lax.rsqrt(jnp.mean(centred * centred, axis=-1, keepdims=True) + 1e-05)
    return mean, rstd, (centred * rstd * gain).astype(BF16)


def inner_kernel(lat_ref, dw_ref, gain_ref, order, columns_ref, *refs):
    out, mixed_out, rows_ref, cols_ref, mixed_ref, pad_ref, normed_ref, side_l, side_r, sems = refs
    batches, rows, cols, feats = lat_ref.shape
    cells = rows * cols
    pad_ref[:, 1 : rows + 1] = lat_ref[...]
    pad_ref[:, 0] = jnp.zeros((batches, cols, feats), BF16)
    pad_ref[:, rows + 1] = jnp.zeros((batches, cols, feats), BF16)
    for b in range(batches):
        rows_ref[b, :2] = lat_ref[b, :2]
        rows_ref[b, 2:] = lat_ref[b, rows - 2 :]
        for h in range(rows):
            normed_ref[b * cells + h * cols : b * cells + (h + 1) * cols, :] = lat_ref[b, h]
        cols_ref[b] = dot(columns_ref[...], normed_ref[b * cells : (b + 1) * cells, :]).astype(BF16)
    convolve(pad_ref, None, None, taps_of(dw_ref, False), side_l, side_r, mixed_ref)
    copies = moves([(mixed_ref, mixed_out)], sems)
    block = 64

    def step(n, carry):
        at = pl.ds(pl.multiple_of(n * block, block), block)
        normed_ref[at, :] = norm(mixed_ref[at, :], gain_ref[...])[2]
        return carry

    lax.fori_loop(0, batches * cells // block, step, 0, unroll=2)
    send_kernel(batches, normed_ref, order, out)
    for copy in copies:
        copy.wait()


def edge_kernel(
    inner_ref, rows_ref, cols_ref, top_ref, bot_ref, left_ref, right_ref, dw_ref, gain_ref, order, out, mixed_ref
):
    batches, _, cols, feats = rows_ref.shape
    rows = cols_ref.shape[1] // 4
    size = out.shape[0] // batches
    taps = taps_of(dw_ref, False)
    spot = lax.broadcasted_iota(jnp.int32, (cols, feats), 0)

    def row(x, left, right):
        low, mid, high = (sum(taps[i][j] * x[i] for i in range(3)) for j in range(3))
        low = jnp.where(spot == 0, sum(taps[i][0] * left[i : i + 1] for i in range(3)), pltpu.roll(low, 1, 0))
        high = jnp.where(
            spot == cols - 1,
            sum(taps[i][2] * right[i : i + 1] for i in range(3)),
            pltpu.roll(high, cols - 1, 0),
        )
        return (x[1] + (low + mid + high)).astype(BF16)

    def column(x):
        low, mid, high = (sum(taps[i][j] * x[j][i : i + rows] for i in range(3)) for j in range(3))
        return (x[1][1 : rows + 1] + (low + mid + high)).astype(BF16)

    for b in range(batches):
        top, bot = top_ref[b].astype(F32), bot_ref[b].astype(F32)
        left, right = left_ref[b].astype(F32), right_ref[b].astype(F32)
        near = [rows_ref[b, n].astype(F32) for n in range(4)]
        both = cols_ref[b].astype(F32)
        longer = [
            jnp.concatenate([top[w : w + 1], both[n * rows : (n + 1) * rows], bot[w : w + 1]], axis=0)
            for n, w in enumerate((0, 1, cols - 2, cols - 1))
        ]
        mixed_ref[b] = jnp.concatenate(
            [
                row([top, near[0], near[1]], left[:3], right[:3]),
                row([near[2], near[3], bot], left[rows - 1 :], right[rows - 1 :]),
                column([left, longer[0], longer[1]]),
                column([longer[2], longer[3], right]),
            ],
            axis=0,
        )
        normed = norm(mixed_ref[b], gain_ref[...])[2]
        at = slice(b * size, (b + 1) * size)
        out[at, :] = inner_ref[at, :] + dot(order[...], normed).astype(BF16)


def patch_kernel(inner_ref, border_ref, unpick_ref, lat_ref, top_ref, bot_ref, *refs):
    mixed_out, stat_out, pad_out, mixed_ref, stat_ref, pad_ref, sems = refs
    batches, rows, cols, feats = lat_ref.shape
    cells = rows * cols
    pad_ref[:, 1 : rows + 1] = lat_ref[...]
    pad_ref[:, 0] = top_ref[...]
    pad_ref[:, rows + 1] = bot_ref[...]
    copies = moves([(pad_ref, pad_out)], sems.at[0:1])
    cell = lax.broadcasted_iota(jnp.int32, (cells, feats), 0)
    h, w = cell // cols, cell % cols
    inside = (h > 0) & (h < rows - 1) & (w > 0) & (w < cols - 1)
    for b in range(batches):
        at = slice(b * cells, (b + 1) * cells)
        patch = dot(unpick_ref[...], border_ref[b])
        mixed_ref[at, :] = jnp.where(inside, inner_ref[at, :].astype(F32), patch).astype(BF16)
    copies += moves([(mixed_ref, mixed_out)], sems.at[1:2])
    block = 64

    def step(n, carry):
        at = pl.ds(pl.multiple_of(n * block, block), block)
        mean, rstd, _ = norm(mixed_ref[at, :], 1.0)
        stat_ref[at, 0:1] = mean
        stat_ref[at, 1:2] = rstd
        return carry

    lax.fori_loop(0, batches * cells // block, step, 0, unroll=2)
    copies += moves([(stat_ref, stat_out)], sems.at[2:3])
    for copy in copies:
        copy.wait()


def gather_rows(source, take_ref, target):
    count = target.shape[0] // CELLS
    whole = source.shape[0] * GROUP // CELLS
    for p in range(CELLS // GROUP):
        ordered = dot(take_ref[...], source[p * whole : (p + 1) * whole, :]).astype(BF16)
        for w in range(count):
            target[w * CELLS + p * GROUP : w * CELLS + (p + 1) * GROUP, :] = ordered[
                w * GROUP : (w + 1) * GROUP
            ]


def grads_kernel(parts, g_ref, wout_ref, *refs):
    for n in range(parts):
        gw, datt = refs[parts + 2 * n : parts + 2 * n + 2]
        gather_rows(g_ref, refs[n], gw)
        rows = gw.shape[0]
        for first in range(0, rows, 256):
            at = slice(first, min(first + 256, rows))
            datt[at, :] = dot(gw[at, :], wout_ref[...], ((1,), (1,))).astype(BF16)


def window_kernel(counts, before, n_hbm, datt_hbm, take_ref, back_ref, wqkv_hbm, *refs):
    n_ref, wqkv_ref, nw, packed, datt, att, dpacked, head_mask, half_mask, in_sems = refs[-10:]
    if counts is None:
        dn_ref, *results, out_sems = refs[:5]
    else:
        mine_ref, gw_hbm, *old = refs[: 4 * before + 2]
        dn_ref, keep_hbm, give_hbm, gw, acc, out_sems, old_sems, *old_refs = refs[
            4 * before + 2 : -10
        ]
        late = moves([(gw_hbm, gw), *zip(old, old_refs)], old_sems)
    loads = moves([(n_hbm, n_ref), (wqkv_hbm, wqkv_ref), (datt_hbm, datt)], in_sems)
    rows, feats = nw.shape
    count = rows // CELLS
    part = GROUP * count
    tiles = feats // 256
    scale = HEAD ** (-0.5)
    block = 256 if rows % 256 == 0 else CELLS

    head_mask[...] = (
        (lax.broadcasted_iota(jnp.int32, (4 * CELLS, 256), 1) // HEAD) % 4
        == lax.broadcasted_iota(jnp.int32, (4 * CELLS, 256), 0) // CELLS
    ).astype(F32).astype(BF16)
    half_mask[...] = (
        lax.broadcasted_iota(jnp.int32, (2 * CELLS, 256), 1) // 128
        == lax.broadcasted_iota(jnp.int32, (2 * CELLS, 256), 0) // CELLS
    ).astype(F32).astype(BF16)

    loads[0].wait()
    gather_rows(n_ref, take_ref, nw)
    loads[1].wait()

    def project(n, carry):
        at = pl.ds(pl.multiple_of(n * block, block), block)
        packed[at, :] = dot(nw[at, :], wqkv_ref[...]).astype(BF16)
        return carry

    lax.fori_loop(0, rows // block, project, 0)
    loads[2].wait()

    lane = lax.broadcasted_iota(jnp.int32, (CELLS, 256), 1)
    lane_half = lane < 128
    lane_head = (lane // HEAD) % 4

    def fold_heads(full):
        out = full[3 * CELLS :]
        for h in (2, 1, 0):
            out = jnp.where(lane_head == h, full[h * CELLS : (h + 1) * CELLS], out)
        return out

    def one(n, carry):
        at = pl.ds(pl.multiple_of(n * CELLS, CELLS), CELLS)
        for t in range(tiles):
            cols = [slice(p * feats + t * 256, p * feats + (t + 1) * 256) for p in range(3)]
            query = packed[at, cols[0]]
            key = packed[at, cols[1]]
            value = packed[at, cols[2]]
            grad = datt[at, t * 256 : (t + 1) * 256]
            key_big = jnp.concatenate([key] * 4, axis=0) * head_mask[...]
            value_big = jnp.concatenate([value] * 4, axis=0) * head_mask[...]
            query_two = jnp.concatenate([query] * 2, axis=0) * half_mask[...]
            grad_two = jnp.concatenate([grad] * 2, axis=0) * half_mask[...]
            scores = (dot(key_big, query_two, ((1,), (1,))) * scale).reshape(4, CELLS, 2 * CELLS)
            d_probs = dot(value_big, grad_two, ((1,), (1,))).reshape(4, CELLS, 2 * CELLS)
            raised = jnp.exp(scores - jnp.max(scores, axis=1, keepdims=True))
            probs = raised * (1.0 / jnp.sum(raised, axis=1, keepdims=True))
            probs_b = probs.astype(BF16).reshape(4 * CELLS, 2 * CELLS)
            inner = jnp.sum(probs * d_probs, axis=1, keepdims=True)
            d_scores = (
                (probs * (d_probs - inner) * scale).astype(BF16).reshape(4 * CELLS, 2 * CELLS)
            )
            out = dot(probs_b, value_big, ((0,), (0,)))
            att[at, t * 256 : (t + 1) * 256] = jnp.where(
                lane_half, out[:CELLS], out[CELLS:]
            ).astype(BF16)
            d_query = dot(d_scores, key_big, ((0,), (0,)))
            dpacked[at, cols[0]] = jnp.where(
                lane_half, d_query[:CELLS], d_query[CELLS:]
            ).astype(BF16)
            dpacked[at, cols[1]] = fold_heads(dot(d_scores, query_two)).astype(BF16)
            dpacked[at, cols[2]] = fold_heads(dot(probs_b, grad_two)).astype(BF16)
        return carry

    lax.fori_loop(0, count, one, 0, unroll=6 if count % 6 == 0 else UNROLL)
    if counts is None:
        stores = moves(list(zip((nw, att, dpacked), results)), out_sems)
    else:
        for copy in late:
            copy.wait()
        parts = [old_refs[4 * n : 4 * n + 4] for n in range(before)] + [(nw, att, dpacked, gw)]
        weight_sums(parts, counts, mine_ref[0], acc)
        half = feats // 2
        stores = moves([(acc.at[half:], give_hbm), (acc.at[:half], keep_hbm)], out_sems)

    def back(n, carry):
        at = pl.ds(pl.multiple_of(n * block, block), block)
        datt[at, :] = dot(dpacked[at, :], wqkv_ref[...], ((1,), (1,))).astype(BF16)
        return carry

    lax.fori_loop(0, rows // block, back, 0)
    if back_ref.shape[0] == 1:
        order = (
            lax.broadcasted_iota(jnp.int32, (rows, dn_ref.shape[0]), 0) == back_ref[...]
        ).astype(F32).astype(BF16)
        dn_ref[...] = dot(order, datt[...], ((0,), (0,))).astype(BF16)
    else:
        for p in range(CELLS // GROUP):
            ordered = jnp.concatenate(
                [
                    datt[w * CELLS + p * GROUP : w * CELLS + (p + 1) * GROUP, :]
                    for w in range(count)
                ],
                axis=0,
            )
            dn_ref[p * part : (p + 1) * part, :] = dot(
                back_ref[...], ordered, ((0,), (0,))
            ).astype(BF16)
    for copy in stores:
        copy.wait()


def place_of(i, j, row_count, chips):
    return (j % 2) * row_count * chips + i * chips + j // 2


def weight_sums(parts, counts, mine, acc):
    feats = acc.shape[0]
    row_count, chips = counts
    devices = 2 * row_count * chips
    size = feats // devices
    if size % 16:
        source = lax.broadcasted_iota(jnp.int32, (feats, feats), 1)
        device = source // size
        place = place_of(device // (2 * chips), device % (2 * chips), row_count, chips)
        target = jnp.bitwise_xor(mine, place) * size + source % size
        order = (lax.broadcasted_iota(jnp.int32, (feats, feats), 0) == target).astype(F32).astype(BF16)
    for left, right, start in ((0, 2, 0), (1, 3, 3 * feats)):
        turned = [part[left][...].T for part in parts]
        for t in range(parts[0][right].shape[1] // 256):
            at = slice(t * 256, (t + 1) * 256)
            to = slice(start + t * 256, start + (t + 1) * 256)
            sums = sum(dot(x, part[right][:, at]) for x, part in zip(turned, parts)).astype(BF16)
            if size % 16:
                acc[:, to] = dot(order, sums).astype(BF16)
                continue
            for n in range(devices):
                place = place_of(n // (2 * chips), n % (2 * chips), row_count, chips)
                block = jnp.bitwise_xor(mine, place)
                acc[pl.ds(pl.multiple_of(block * size, size), size), to] = sums[n * size : (n + 1) * size]


def norm_back(d_normed, nhat, rstd, grad, gain):
    scaled = d_normed * gain
    return (
        grad.astype(F32)
        + rstd
        * (
            scaled
            - jnp.mean(scaled, axis=-1, keepdims=True)
            - nhat * jnp.mean(scaled * nhat, axis=-1, keepdims=True)
        )
    ).astype(BF16)


def border_kernel(dn_ref, gain_ref, *refs):
    batches = refs[4].shape[0]
    feats = dn_ref.shape[1]
    size = dn_ref.shape[0] // batches
    for pick, pair, out in zip(refs[:4], refs[4:8], refs[8:]):
        for b in range(batches):
            d_normed = dot(pick[...], dn_ref[b * size : (b + 1) * size, :])
            mixed = pair[b, :, :feats].astype(F32)
            centred = mixed - jnp.mean(mixed, axis=-1, keepdims=True)
            rstd = lax.rsqrt(jnp.mean(centred * centred, axis=-1, keepdims=True) + 1e-05)
            out[b] = norm_back(d_normed, centred * rstd, rstd, pair[b, :, feats:], gain_ref[...])


def sums_kernel(count, *refs):
    orders, refs = refs[:count], refs[count:]
    hbm, refs = refs[:count], refs[count:]
    hbm, (left_ref, right_ref, gain_ref) = hbm + refs[:4], refs[4:7]
    out_ref, sums_ref, dn, side_l, side_r = refs[7:12]
    here, sems = refs[12:-1], refs[-1]
    parts = here[:count]
    stat_ref, mixed_ref, grad_ref, pad_ref = here[count:]
    loads = moves(list(zip(hbm, here)), sems)
    batches, rows, cols, feats = pad_ref.shape
    rows -= 2
    cells = rows * cols
    for copy in loads[:count]:
        copy.wait()
    for b in range(batches):
        total = None
        for order, part in zip(orders, parts):
            size = part.shape[0] // batches
            term = dot(order[...], part[b * size : (b + 1) * size, :])
            total = term if total is None else total + term
        dn[b * cells : (b + 1) * cells, :] = total
    block = 64
    for copy in loads[count : count + 3]:
        copy.wait()

    def norm(n, gain_sum):
        at = pl.ds(pl.multiple_of(n * block, block), block)
        d_normed = dn[at, :]
        rstd = stat_ref[at, 1:2]
        nhat = (mixed_ref[at, :].astype(F32) - stat_ref[at, 0:1]) * rstd
        out_ref[at, :] = norm_back(d_normed, nhat, rstd, grad_ref[at, :], gain_ref[...])
        return gain_sum + jnp.sum((d_normed * nhat).reshape(block // 8, 8, feats), axis=0)

    gain_sum = lax.fori_loop(
        0, batches * cells // block, norm, jnp.zeros((8, feats), F32), unroll=2
    )
    sums_ref[9:10, :] = jnp.sum(gain_sum, axis=0, keepdims=True)
    sums_ref[10:, :] = jnp.zeros((sums_ref.shape[0] - 10, feats), F32)
    loads[count + 3].wait()

    four = 4
    width = 256
    spot = lax.broadcasted_iota(jnp.int32, (cols, width), 0)
    fold = lambda v: jnp.sum(v.reshape(cols // 8, 8, width), axis=0)
    for c in range(feats // width):
        lanes = slice(c * width, (c + 1) * width)
        sums = [jnp.zeros((8, width), F32) for _ in range(9)]
        for b in range(batches):

            def step(n, sums, b=b, lanes=lanes):
                start = n * four
                x = [pad_ref[b, start + r, :, lanes].astype(F32) for r in range(four + 2)]
                sums = list(sums)
                for r in range(four):
                    h = start + r
                    at = pl.ds(pl.multiple_of((b * rows + h) * cols, cols), cols)
                    d_mixed = out_ref[at, lanes].astype(F32)
                    side_l[b, pl.ds(h, 1), lanes] = d_mixed[:1]
                    side_r[b, pl.ds(h, 1), lanes] = d_mixed[cols - 1 :]
                    moved = (
                        jnp.where(spot == cols - 1, 0.0, pltpu.roll(d_mixed, cols - 1, 0)),
                        d_mixed,
                        jnp.where(spot == 0, 0.0, pltpu.roll(d_mixed, 1, 0)),
                    )
                    for i in range(3):
                        for j in range(3):
                            sums[3 * i + j] = sums[3 * i + j] + fold(moved[j] * x[r + i])
                return tuple(sums)

            sums = lax.fori_loop(0, rows // four, step, tuple(sums))
        for n in range(9):
            sums_ref[n : n + 1, lanes] = jnp.sum(sums[n], axis=0, keepdims=True)
    for i in range(3):
        for b in range(batches):
            left, right = left_ref[b].astype(F32), right_ref[b].astype(F32)
            sums_ref[3 * i : 3 * i + 1, :] += jnp.sum(
                side_l[b] * left[i : i + rows], axis=0, keepdims=True
            )
            sums_ref[3 * i + 2 : 3 * i + 3, :] += jnp.sum(
                side_r[b] * right[i : i + rows], axis=0, keepdims=True
            )


def spread_kernel(d_ref, top_ref, bot_ref, left_ref, right_ref, dw_ref, out_ref, pad, side_l, side_r):
    batches, rows, cols, feats = pad.shape
    rows -= 2
    for b in range(batches):
        for h in range(rows):
            pad[b, h + 1] = d_ref[(b * rows + h) * cols : (b * rows + h + 1) * cols, :]
    pad[:, 0] = top_ref[...]
    pad[:, rows + 1] = bot_ref[...]
    convolve(pad, left_ref, right_ref, taps_of(dw_ref, True), side_l, side_r, out_ref)


def finish_kernel(*refs):
    *parts, qkv_ref, wout_ref, gain_ref, kernel_ref = refs
    feats = wout_ref.shape[1]
    level = total([part[...].astype(F32) for part in parts])
    qkv_ref[...] = level[:, : 3 * feats]
    wout_ref[...] = level[:, 3 * feats : 4 * feats]
    sums = level[:, 4 * feats :]
    gain_ref[...] = sums[9:10]
    for i in range(3):
        kernel_ref[i] = sums[3 * i : 3 * i + 3]


def call(body, outs, scratch, args, micros, name, hbm_ins=(), hbm_outs=(), scalars=(), limit=56 << 20):
    moved = sum(int(np.prod(o.shape)) * o.dtype.itemsize for o in (*outs, *args))
    vmem = pl.BlockSpec(memory_space=pltpu.VMEM)
    hbm = pl.BlockSpec(memory_space=pltpu.HBM)
    smem = pl.BlockSpec(memory_space=pltpu.SMEM)
    return pl.pallas_call(
        body,
        out_shape=outs,
        in_specs=[
            smem if n in scalars else hbm if n in hbm_ins else vmem for n in range(len(args))
        ],
        out_specs=[hbm if n in hbm_outs else vmem for n in range(len(outs))],
        scratch_shapes=scratch,
        compiler_params=pltpu.CompilerParams(vmem_limit_bytes=limit),
        cost_estimate=pl.CostEstimate(
            flops=micros * 10**9, bytes_accessed=moved, transcendentals=0
        ),
        name=name,
    )(*args)


def shape(dims, dtype):
    return jax.ShapeDtypeStruct(tuple(dims), dtype)


def shifted(cells, axis, step):
    count = lax.axis_size(axis)
    return lax.ppermute(cells, axis, [(n, n + step) for n in range(count) if 0 <= n + step < count])


def halos(top, bottom, left, right):
    above = shifted(bottom, "row", 1)
    below = shifted(top, "row", -1)
    last = above.shape[1] - 1
    column = lambda own, at: jnp.concatenate(
        [above[:, at : at + 1], own, below[:, at : at + 1]], axis=1
    )
    from_left = shifted(column(right, last), "col", 1)
    from_right = shifted(column(left, 0), "col", -1)
    return above, below, from_left, from_right


def swap(x, axis, step):
    return lax.ppermute(x, axis, [(n, n ^ step) for n in range(lax.axis_size(axis))])


def total(values):
    while len(values) > 1:
        values = [a + b for a, b in zip(values[::2], values[1::2])]
    return values[0]


def scatter(blocks, sums, axis, unit, count):
    size = blocks.shape[0] // count
    sums = sums.reshape(size, -1)
    load = lambda n: jnp.concatenate([blocks[n * size : (n + 1) * size], sums], axis=1).astype(BF16)
    own = jnp.concatenate([blocks[:size], sums], axis=1)
    return [own, *(swap(load(n), axis, unit * n) for n in range(1, count))]


def shards(plan, latent, w_qkv, w_out, ln_gain, dw_kernel, grad_out):
    batches, rows, cols, feats = latent.shape
    row_count, col_count = lax.axis_size("row"), lax.axis_size("col")
    cells = batches * rows * cols
    parts = len(plan.rows)
    gain = ln_gain.reshape(1, feats)
    send = jnp.asarray(plan.send_all, BF16)
    owner = lax.axis_index("row") * col_count + lax.axis_index("col")
    index = lax.dynamic_index_in_dim(jnp.asarray(plan.index), owner % plan.share, keepdims=False)
    back = [jnp.asarray(np.ascontiguousarray(m.T), BF16) for m in plan.send]
    sort = [index, *(jnp.asarray(m, BF16) for m in plan.sort[1:])]
    grouped = [shape((n * CELLS, feats), BF16) for n in plan.windows]
    take = [jnp.asarray(m, BF16) for m in plan.take]
    chunks = [shape((n, feats), BF16) for n in plan.rows]
    trade = lambda x: lax.all_to_all(x, AXES, split_axis=0, concat_axis=0, tiled=True)
    grad_flat = grad_out.reshape(cells, feats)

    flat = shape((cells, feats), BF16)
    (grad_sent,) = call(
        functools.partial(grad_kernel, batches),
        [flat],
        [
            pltpu.VMEM((cells, feats), BF16),
            pltpu.VMEM(send.shape, BF16),
            pltpu.VMEM((cells, feats), BF16),
            pltpu.SemaphoreType.DMA((1 + 2 * batches,)),
        ],
        [grad_flat, send],
        3,
        "grad_send",
        hbm_ins=(0, 1),
        hbm_outs=(0,),
    )
    grad_sent, latent = lax.optimization_barrier((grad_sent, latent))
    grad_win = trade(grad_sent)

    above, below, left, right = halos(latent[:, 0], latent[:, -1], latent[:, :, 0], latent[:, :, -1])
    padded = (batches, rows + 2, cols, feats)
    side = pltpu.VMEM((batches, rows, feats), F32)
    stat_shape = (cells, 2)
    const = lambda m: jnp.asarray(m, BF16)
    sent, mixed_inner, own_rows, own_cols = call(
        inner_kernel,
        [
            flat,
            flat,
            shape((batches, 4, cols, feats), BF16),
            shape((batches, 4 * rows, feats), BF16),
        ],
        [
            pltpu.VMEM((cells, feats), BF16),
            pltpu.VMEM(padded, BF16),
            pltpu.VMEM((cells, feats), BF16),
            side,
            side,
            pltpu.SemaphoreType.DMA((1,)),
        ],
        [latent, dw_kernel, gain, const(plan.send_inner), const(plan.columns)],
        6,
        "inner",
        limit=50 << 20,
        hbm_outs=(1,),
    )
    normed, mixed_border = call(
        edge_kernel,
        [flat, shape((batches, plan.unpick.shape[1], feats), BF16)],
        [],
        [sent, own_rows, own_cols, above, below, left, right, dw_kernel, gain, const(plan.send_border)],
        3,
        "edge",
        limit=50 << 20,
    )
    normed_win = trade(normed)
    ends = (0, cols, 2 * cols, 2 * cols + rows, 2 * cols + 2 * rows)
    grad_ends = (grad_out[:, 0], grad_out[:, -1], grad_out[:, :, 0], grad_out[:, :, -1])
    pairs = halos(
        *(
            jnp.concatenate([mixed_border[:, first:last], x], axis=-1)
            for first, last, x in zip(ends[:-1], ends[1:], grad_ends)
        )
    )
    mixed, stat, pad = call(
        patch_kernel,
        [flat, shape(stat_shape, F32), shape(padded, BF16)],
        [
            pltpu.VMEM((cells, feats), BF16),
            pltpu.VMEM(stat_shape, F32),
            pltpu.VMEM(padded, BF16),
            pltpu.SemaphoreType.DMA((3,)),
        ],
        [mixed_inner, mixed_border, const(plan.unpick), latent, above, below],
        4,
        "patch",
        limit=50 << 20,
        hbm_outs=(0, 1, 2),
    )

    chips = col_count // 2
    normed_win, mixed, stat, pad, *pairs = lax.optimization_barrier(
        (normed_win, mixed, stat, pad, *pairs)
    )
    ahead = call(
        functools.partial(grads_kernel, parts),
        [grouped[n // 2] for n in range(2 * parts)],
        [],
        [grad_win, w_out, *take],
        4,
        "grads",
        limit=50 << 20,
    )
    mine = place_of(lax.axis_index("row"), lax.axis_index("col"), row_count, chips).astype(jnp.int32).reshape(1)
    half = shape((feats // 2, 4 * feats), BF16)
    d_parts, kept = [], []
    for n in range(parts):
        count = plan.windows[n] * CELLS
        last = n == parts - 1
        mat = lambda width: pltpu.VMEM((count, width), BF16)
        args = [normed_win, ahead[2 * n + 1], take[n], sort[n], w_qkv]
        if last:
            outs = [chunks[n], half, half]
            args += [mine, ahead[2 * n], *kept]
            scratch = [
                mat(feats),
                pltpu.VMEM((feats, 4 * feats), BF16),
                pltpu.SemaphoreType.DMA((2,)),
                pltpu.SemaphoreType.DMA((1 + len(kept),)),
                *(pltpu.VMEM(x.shape, BF16) for x in kept),
            ]
        else:
            outs = [chunks[n], grouped[n], grouped[n], shape((count, 3 * feats), BF16)]
            scratch = [pltpu.SemaphoreType.DMA((3,))]
        d_chunk, *saved = call(
            functools.partial(window_kernel, (row_count, chips) if last else None, n),
            outs,
            [
                *scratch,
                pltpu.VMEM((cells, feats), BF16),
                pltpu.VMEM((feats, 3 * feats), BF16),
                mat(feats),
                mat(3 * feats),
                mat(feats),
                mat(feats),
                mat(3 * feats),
                pltpu.VMEM((4 * CELLS, 256), BF16),
                pltpu.VMEM((2 * CELLS, 256), BF16),
                pltpu.SemaphoreType.DMA((3,)),
            ],
            args,
            2 + 20 * count // cells,
            "windows",
        limit=56 << 20,
            hbm_ins=(0, 1, 4, *range(6, len(args))),
            hbm_outs=tuple(range(1, len(outs))),
            scalars=(5,),
        )
        kept += [*saved, ahead[2 * n]]
        d_parts.append(trade(d_chunk))
    keep, give = saved

    d_halos = call(
        border_kernel,
        [shape((*x.shape[:2], feats), BF16) for x in pairs],
        [],
        [d_parts[0], gain, *(jnp.asarray(m, BF16) for m in plan.pieces), *pairs],
        3,
        "border",
        limit=50 << 20,
    )
    weights = (keep.astype(F32) + swap(give, "col", 1).astype(F32)).astype(BF16)
    d_mixed, sums = call(
        functools.partial(sums_kernel, parts),
        [flat, shape((16, feats), F32)],
        [
            pltpu.VMEM((cells, feats), F32),
            side,
            side,
            *(pltpu.VMEM((n, feats), BF16) for n in plan.rows),
            pltpu.VMEM(stat_shape, F32),
            pltpu.VMEM((cells, feats), BF16),
            pltpu.VMEM((cells, feats), BF16),
            pltpu.VMEM(padded, BF16),
            pltpu.SemaphoreType.DMA((parts + 4,)),
        ],
        [*back, *d_parts, stat, mixed, grad_flat, pad, left, right, gain],
        7,
        "sums",
        limit=50 << 20,
        hbm_ins=tuple(range(parts, 2 * parts + 4)),
    )
    wide = 4 * feats
    size = weights.shape[0] // row_count
    gives = [
        swap(weights[n * size : (n + 1) * size], "row", n) for n in range(1, row_count)
    ]
    sums, weights, *gives = lax.optimization_barrier((sums, weights, *gives))
    weights = total([x.astype(F32) for x in (weights[:size], *gives)])
    sums = sums + swap(sums, "col", 1)
    sums = total([sums, *(swap(sums, "row", n) for n in range(1, row_count))])
    sums, d_mixed = lax.optimization_barrier((sums, d_mixed))
    (grad_latent,) = call(
        spread_kernel,
        [flat],
        [pltpu.VMEM(padded, BF16), side, side],
        [d_mixed, *d_halos, dw_kernel],
        5,
        "spread",
        limit=50 << 20,
    )
    level = scatter(weights, sums, "col", 2, chips)
    grad_latent = grad_latent.reshape(latent.shape)
    size = level[0].shape[0]
    if size == 16:
        qkv, wout, gain_sum, kernel_sum = call(
            finish_kernel,
            [
                shape((size, 3 * feats), F32),
                shape((size, feats), F32),
                shape((1, feats), F32),
                shape((3, 3, feats), F32),
            ],
            [],
            level,
            1,
            "finish",
            limit=50 << 20,
        )
        return grad_latent, qkv, wout, gain_sum.reshape(feats), kernel_sum
    level = total([x.astype(F32) for x in level])
    sums = level[:, wide:].reshape(16, feats)
    return (
        grad_latent,
        level[:, : 3 * feats],
        level[:, 3 * feats : wide],
        sums[9],
        sums[:9].reshape(3, 3, feats),
    )


def solution(mesh):
    row_count, col_count = mesh.shape["row"], mesh.shape["col"]

    def run(latent, w_qkv, w_out, ln_gain, dw_kernel, grad_out):
        batches, rows, cols, _ = latent.shape
        plan = Plan(batches, rows // row_count, cols // col_count, row_count, col_count)
        in_specs = (P(None, "row", "col", None), P(), P(), P(), P(), P(None, "row", "col", None))
        out_specs = (
            P(None, "row", "col", None),
            P(AXES, None),
            P(AXES, None),
            P(),
            P(),
        )
        return jax.shard_map(
            functools.partial(shards, plan),
            mesh=mesh,
            in_specs=in_specs,
            out_specs=out_specs,
            check_vma=False,
        )(latent, w_qkv, w_out, ln_gain, dw_kernel, grad_out)

    return run
```

```python
import functools

import jax
import jax.numpy as jnp
import numpy as np
from jax import lax
from jax.experimental import pallas as pl
from jax.experimental.pallas import tpu as pltpu
from jax.sharding import PartitionSpec as P

HEADS = 16
HEAD = 32
GRID = 8
CELLS = GRID * GRID
AXES = ("row", "col")
F32 = jnp.float32
BF16 = jnp.bfloat16
LIMIT = 54 * 1024 * 1024
UNROLL = 4
GROUP = 16


def dot(left, right, dims=((1,), (0,))):
    return lax.dot_general(left, right, (dims, ((), ())), preferred_element_type=F32)


def moves(pairs, sems):
    copies = [pltpu.make_async_copy(a, b, sems.at[n]) for n, (a, b) in enumerate(pairs)]
    for copy in copies:
        copy.start()
    return copies


class Plan:
    def __init__(self, batches, tile_rows, tile_cols, row_count, col_count):
        devices = row_count * col_count
        high = tile_rows * row_count // GRID
        full = tile_cols * col_count // GRID
        wide = min(full, tile_cols)
        groups = full // wide
        reps_r = tile_rows // high
        reps_s = tile_cols // wide
        reps = reps_r * reps_s
        share = devices // batches
        spots = [(a, e) for a in range(high) for e in range(wide)]
        cells = tile_rows * tile_cols
        ring = [
            [(-1, w) for w in range(tile_cols)],
            [(tile_rows, w) for w in range(tile_cols)],
            [(h, -1) for h in range(-1, tile_rows + 1)],
            [(h, tile_cols) for h in range(-1, tile_rows + 1)],
        ]

        def home(h, w):
            down, right = h // tile_rows, w // tile_cols
            h, w = h % tile_rows, w % tile_cols
            return down, right, (h % high, w % wide), (h // high) * reps_s + w // wide

        wanted = {c: [] for c in spots}
        for piece, members in enumerate(ring):
            for n, cell in enumerate(members):
                wanted[home(*cell)[2]].append((piece, n))
        edge = sorted((c for c in spots if wanted[c]), key=lambda c: -len(wanted[c]))
        slots = len(spots) // share
        edge_slots = -(-len(edge) // share)
        assert edge_slots < slots
        bounds = [0, edge_slots, slots]
        place, filled, load = {}, [0] * share, [0] * share
        for c in edge:
            owner = min((n for n in range(share) if filled[n] < edge_slots), key=lambda n: load[n])
            place[c] = (owner, filled[owner])
            filled[owner] += 1
            load[owner] += len(wanted[c])
        for c in spots:
            if c not in place:
                owner = min(range(share), key=lambda n: filled[n])
                place[c] = (owner, filled[owner])
                filled[owner] += 1

        def build(first, last):
            size = (last - first) * reps
            send = np.zeros((share * size, cells), np.float32)
            for h in range(tile_rows):
                for w in range(tile_cols):
                    owner, slot = place[(h % high, w % wide)]
                    if first <= slot < last:
                        rep = (h // high) * reps_s + w // wide
                        send[owner * size + (slot - first) * reps + rep, h * tile_cols + w] = 1
            count = (last - first) * groups
            seen = np.zeros((count,), np.int64)
            where = {}
            sort = np.zeros((devices * size, devices * size), np.float32)
            for source in range(devices):
                j = source % col_count
                for slot in range(last - first):
                    for r in range(reps_r):
                        for s in range(reps_s):
                            window = slot * groups + ((j * tile_cols + s * wide) % full) // wide
                            position = int(seen[window])
                            seen[window] += 1
                            chunk, lane = divmod(position, GROUP)
                            row = chunk * GROUP * count + window * GROUP + lane
                            where[source, slot, r * reps_s + s] = window * CELLS + position
                            sort[row, source * size + slot * reps + r * reps_s + s] = 1
            step = GROUP * count
            block = sort[:step, :step]
            assert (sort == np.kron(np.eye(CELLS // GROUP), block)).all()
            return send, block, where

        self.send_all, sort_all, _ = build(0, slots)
        self.send, self.sort, self.take = [], [], []
        for first, last in zip(bounds[:-1], bounds[1:]):
            send, block, where = build(first, last)
            if first == 0:
                around = where
            self.send.append(send)
            self.sort.append(block)
            self.take.append(sort_all[first * groups * GROUP : last * groups * GROUP])
        own = edge_slots * reps
        size = own + -(-max(load) // 8) * 8
        size = -(-size // 8) * 8
        back = np.zeros((share * size, cells), np.float32)
        for n in range(share):
            back[n * size : n * size + own] = self.send[0][n * own : (n + 1) * own]
        self.send[0] = back
        self.pieces = [np.zeros((len(members), share * size), np.float32) for members in ring]
        self.index = np.full((share, 1, devices * size), -1, np.int32)
        used = [own] * share
        for source, slot, rep in around:
            self.index[:, 0, source * size + slot * reps + rep] = around[source, slot, rep]
        for c in edge:
            owner, slot = place[c]
            for piece, n in wanted[c]:
                down, right, _, rep = home(*ring[piece][n])
                self.pieces[piece][n, owner * size + used[owner]] = 1
                for i in range(row_count):
                    for j in range(col_count):
                        if 0 <= i + down < row_count and 0 <= j + right < col_count:
                            source = (i + down) * col_count + j + right
                            target = (i * col_count + j) * size + used[owner]
                            self.index[owner, 0, target] = around[source, slot, rep]
                used[owner] += 1
        border = [(h, w) for h in (0, tile_rows - 1) for w in range(tile_cols)]
        border += [(h, w) for w in (0, tile_cols - 1) for h in range(tile_rows)]
        self.unpick = np.zeros((cells, len(border)), np.float32)
        for n, (h, w) in enumerate(border):
            if n < 2 * tile_cols or h not in (0, tile_rows - 1):
                self.unpick[h * tile_cols + w, n] = 1
        self.send_border = self.send_all @ self.unpick
        self.send_inner = self.send_all * (1 - self.unpick.sum(1))[None]
        self.columns = np.zeros((4 * tile_rows, cells), np.float32)
        for n, w in enumerate((0, 1, tile_cols - 2, tile_cols - 1)):
            for h in range(tile_rows):
                self.columns[n * tile_rows + h, h * tile_cols + w] = 1
        self.share = share
        self.windows = [m.shape[0] // GROUP for m in self.sort]
        self.rows = [batches * m.shape[0] for m in self.send]


def send_kernel(batches, x_ref, order, out):
    cells = x_ref.shape[0] // batches
    for b in range(batches):
        at = slice(b * cells, (b + 1) * cells)
        out[at, :] = dot(order[...], x_ref[at, :]).astype(BF16)


def grad_kernel(batches, x_hbm, order_hbm, out_hbm, x_ref, order_ref, out_ref, sems):
    cells = x_ref.shape[0] // batches
    at = [pl.ds(b * cells, cells) for b in range(batches)]
    loads = moves([(order_hbm, order_ref), *((x_hbm.at[a], x_ref.at[a]) for a in at)], sems)
    stores = []
    loads[0].wait()
    for b, a in enumerate(at):
        loads[1 + b].wait()
        out_ref[a, :] = dot(order_ref[...], x_ref[a, :]).astype(BF16)
        stores += moves([(out_ref.at[a], out_hbm.at[a])], sems.at[1 + batches + b : 2 + batches + b])
    for copy in stores:
        copy.wait()


def convolve(pad, left_ref, right_ref, kern, side_l, side_r, out_ref):
    batches, rows, cols, feats = pad.shape
    rows -= 2
    four = 4
    width = 256
    for b in range(batches):
        if left_ref is None:
            side_l[b] = jnp.zeros(side_l.shape[1:], F32)
            side_r[b] = jnp.zeros(side_r.shape[1:], F32)
            continue
        left, right = left_ref[b].astype(F32), right_ref[b].astype(F32)
        side_l[b] = sum(kern[i][0] * left[i : i + rows] for i in range(3))
        side_r[b] = sum(kern[i][2] * right[i : i + rows] for i in range(3))
    spot = lax.broadcasted_iota(jnp.int32, (cols, width), 0)
    for c in range(feats // width):
        at = slice(c * width, (c + 1) * width)
        taps = [[kern[i][j][:, at] for j in range(3)] for i in range(3)]
        for b in range(batches):

            def step(n, carry, b=b, at=at, taps=taps):
                first = n * four
                x = [pad[b, first + r, :, at].astype(F32) for r in range(four + 2)]
                for r in range(four):
                    low, mid, high = (
                        taps[0][j] * x[r] + taps[1][j] * x[r + 1] + taps[2][j] * x[r + 2]
                        for j in range(3)
                    )
                    h = first + r
                    low = jnp.where(spot == 0, side_l[b, pl.ds(h, 1), at], pltpu.roll(low, 1, 0))
                    high = jnp.where(
                        spot == cols - 1, side_r[b, pl.ds(h, 1), at], pltpu.roll(high, cols - 1, 0)
                    )
                    where = pl.ds(pl.multiple_of((b * rows + h) * cols, cols), cols)
                    out_ref[where, at] = (x[r + 1] + (low + mid + high)).astype(BF16)
                return carry

            lax.fori_loop(0, rows // four, step, 0)


def taps_of(dw_ref, flipped):
    side = lambda n: 2 - n if flipped else n
    return [
        [dw_ref[side(i), side(j) : side(j) + 1, :].astype(F32) for j in range(3)] for i in range(3)
    ]


def norm(mixed, gain):
    mixed = mixed.astype(F32)
    mean = jnp.mean(mixed, axis=-1, keepdims=True)
    centred = mixed - mean
    rstd = lax.rsqrt(jnp.mean(centred * centred, axis=-1, keepdims=True) + 1e-05)
    return mean, rstd, (centred * rstd * gain).astype(BF16)


def inner_kernel(lat_ref, dw_ref, gain_ref, order, columns_ref, *refs):
    out, mixed_out, rows_ref, cols_ref, mixed_ref, pad_ref, normed_ref, side_l, side_r, sems = refs
    batches, rows, cols, feats = lat_ref.shape
    cells = rows * cols
    pad_ref[:, 1 : rows + 1] = lat_ref[...]
    pad_ref[:, 0] = jnp.zeros((batches, cols, feats), BF16)
    pad_ref[:, rows + 1] = jnp.zeros((batches, cols, feats), BF16)
    for b in range(batches):
        rows_ref[b, :2] = lat_ref[b, :2]
        rows_ref[b, 2:] = lat_ref[b, rows - 2 :]
        for h in range(rows):
            normed_ref[b * cells + h * cols : b * cells + (h + 1) * cols, :] = lat_ref[b, h]
        cols_ref[b] = dot(columns_ref[...], normed_ref[b * cells : (b + 1) * cells, :]).astype(BF16)
    convolve(pad_ref, None, None, taps_of(dw_ref, False), side_l, side_r, mixed_ref)
    copies = moves([(mixed_ref, mixed_out)], sems)
    block = 64

    def step(n, carry):
        at = pl.ds(pl.multiple_of(n * block, block), block)
        normed_ref[at, :] = norm(mixed_ref[at, :], gain_ref[...])[2]
        return carry

    lax.fori_loop(0, batches * cells // block, step, 0, unroll=2)
    send_kernel(batches, normed_ref, order, out)
    for copy in copies:
        copy.wait()


def edge_kernel(
    inner_ref, rows_ref, cols_ref, top_ref, bot_ref, left_ref, right_ref, dw_ref, gain_ref, order, out, mixed_ref
):
    batches, _, cols, feats = rows_ref.shape
    rows = cols_ref.shape[1] // 4
    size = out.shape[0] // batches
    taps = taps_of(dw_ref, False)
    spot = lax.broadcasted_iota(jnp.int32, (cols, feats), 0)

    def row(x, left, right):
        low, mid, high = (sum(taps[i][j] * x[i] for i in range(3)) for j in range(3))
        low = jnp.where(spot == 0, sum(taps[i][0] * left[i : i + 1] for i in range(3)), pltpu.roll(low, 1, 0))
        high = jnp.where(
            spot == cols - 1,
            sum(taps[i][2] * right[i : i + 1] for i in range(3)),
            pltpu.roll(high, cols - 1, 0),
        )
        return (x[1] + (low + mid + high)).astype(BF16)

    def column(x):
        low, mid, high = (sum(taps[i][j] * x[j][i : i + rows] for i in range(3)) for j in range(3))
        return (x[1][1 : rows + 1] + (low + mid + high)).astype(BF16)

    for b in range(batches):
        top, bot = top_ref[b].astype(F32), bot_ref[b].astype(F32)
        left, right = left_ref[b].astype(F32), right_ref[b].astype(F32)
        near = [rows_ref[b, n].astype(F32) for n in range(4)]
        both = cols_ref[b].astype(F32)
        longer = [
            jnp.concatenate([top[w : w + 1], both[n * rows : (n + 1) * rows], bot[w : w + 1]], axis=0)
            for n, w in enumerate((0, 1, cols - 2, cols - 1))
        ]
        mixed_ref[b] = jnp.concatenate(
            [
                row([top, near[0], near[1]], left[:3], right[:3]),
                row([near[2], near[3], bot], left[rows - 1 :], right[rows - 1 :]),
                column([left, longer[0], longer[1]]),
                column([longer[2], longer[3], right]),
            ],
            axis=0,
        )
        normed = norm(mixed_ref[b], gain_ref[...])[2]
        at = slice(b * size, (b + 1) * size)
        out[at, :] = inner_ref[at, :] + dot(order[...], normed).astype(BF16)


def patch_kernel(inner_ref, border_ref, unpick_ref, lat_ref, top_ref, bot_ref, *refs):
    mixed_out, stat_out, pad_out, mixed_ref, stat_ref, pad_ref, sems = refs
    batches, rows, cols, feats = lat_ref.shape
    cells = rows * cols
    pad_ref[:, 1 : rows + 1] = lat_ref[...]
    pad_ref[:, 0] = top_ref[...]
    pad_ref[:, rows + 1] = bot_ref[...]
    copies = moves([(pad_ref, pad_out)], sems.at[0:1])
    cell = lax.broadcasted_iota(jnp.int32, (cells, feats), 0)
    h, w = cell // cols, cell % cols
    inside = (h > 0) & (h < rows - 1) & (w > 0) & (w < cols - 1)
    for b in range(batches):
        at = slice(b * cells, (b + 1) * cells)
        patch = dot(unpick_ref[...], border_ref[b])
        mixed_ref[at, :] = jnp.where(inside, inner_ref[at, :].astype(F32), patch).astype(BF16)
    copies += moves([(mixed_ref, mixed_out)], sems.at[1:2])
    block = 64

    def step(n, carry):
        at = pl.ds(pl.multiple_of(n * block, block), block)
        mean, rstd, _ = norm(mixed_ref[at, :], 1.0)
        stat_ref[at, 0:1] = mean
        stat_ref[at, 1:2] = rstd
        return carry

    lax.fori_loop(0, batches * cells // block, step, 0, unroll=2)
    copies += moves([(stat_ref, stat_out)], sems.at[2:3])
    for copy in copies:
        copy.wait()


def gather_rows(source, take_ref, target):
    count = target.shape[0] // CELLS
    whole = source.shape[0] * GROUP // CELLS
    for p in range(CELLS // GROUP):
        ordered = dot(take_ref[...], source[p * whole : (p + 1) * whole, :]).astype(BF16)
        for w in range(count):
            target[w * CELLS + p * GROUP : w * CELLS + (p + 1) * GROUP, :] = ordered[
                w * GROUP : (w + 1) * GROUP
            ]


def grads_kernel(parts, g_ref, wout_ref, *refs):
    for n in range(parts):
        gw, datt = refs[parts + 2 * n : parts + 2 * n + 2]
        gather_rows(g_ref, refs[n], gw)
        rows = gw.shape[0]
        for first in range(0, rows, 256):
            at = slice(first, min(first + 256, rows))
            datt[at, :] = dot(gw[at, :], wout_ref[...], ((1,), (1,))).astype(BF16)


def window_kernel(counts, before, n_hbm, datt_hbm, take_ref, back_ref, wqkv_hbm, *refs):
    n_ref, wqkv_ref, nw, packed, datt, att, dpacked, head_mask, half_mask, in_sems = refs[-10:]
    if counts is None:
        dn_ref, *results, out_sems = refs[:5]
    else:
        mine_ref, gw_hbm, *old = refs[: 4 * before + 2]
        dn_ref, keep_hbm, give_hbm, gw, acc, out_sems, old_sems, *old_refs = refs[
            4 * before + 2 : -10
        ]
        late = moves([(gw_hbm, gw), *zip(old, old_refs)], old_sems)
    loads = moves([(n_hbm, n_ref), (wqkv_hbm, wqkv_ref), (datt_hbm, datt)], in_sems)
    rows, feats = nw.shape
    count = rows // CELLS
    part = GROUP * count
    tiles = feats // 256
    scale = HEAD ** (-0.5)
    block = 256 if rows % 256 == 0 else CELLS

    head_mask[...] = (
        (lax.broadcasted_iota(jnp.int32, (4 * CELLS, 256), 1) // HEAD) % 4
        == lax.broadcasted_iota(jnp.int32, (4 * CELLS, 256), 0) // CELLS
    ).astype(F32).astype(BF16)
    half_mask[...] = (
        lax.broadcasted_iota(jnp.int32, (2 * CELLS, 256), 1) // 128
        == lax.broadcasted_iota(jnp.int32, (2 * CELLS, 256), 0) // CELLS
    ).astype(F32).astype(BF16)

    loads[0].wait()
    gather_rows(n_ref, take_ref, nw)
    loads[1].wait()

    def project(n, carry):
        at = pl.ds(pl.multiple_of(n * block, block), block)
        packed[at, :] = dot(nw[at, :], wqkv_ref[...]).astype(BF16)
        return carry

    lax.fori_loop(0, rows // block, project, 0)
    loads[2].wait()

    lane = lax.broadcasted_iota(jnp.int32, (CELLS, 256), 1)
    lane_half = lane < 128
    lane_head = (lane // HEAD) % 4

    def fold_heads(full):
        out = full[3 * CELLS :]
        for h in (2, 1, 0):
            out = jnp.where(lane_head == h, full[h * CELLS : (h + 1) * CELLS], out)
        return out

    def one(n, carry):
        at = pl.ds(pl.multiple_of(n * CELLS, CELLS), CELLS)
        for t in range(tiles):
            cols = [slice(p * feats + t * 256, p * feats + (t + 1) * 256) for p in range(3)]
            query = packed[at, cols[0]]
            key = packed[at, cols[1]]
            value = packed[at, cols[2]]
            grad = datt[at, t * 256 : (t + 1) * 256]
            key_big = jnp.concatenate([key] * 4, axis=0) * head_mask[...]
            value_big = jnp.concatenate([value] * 4, axis=0) * head_mask[...]
            query_two = jnp.concatenate([query] * 2, axis=0) * half_mask[...]
            grad_two = jnp.concatenate([grad] * 2, axis=0) * half_mask[...]
            scores = (dot(key_big, query_two, ((1,), (1,))) * scale).reshape(4, CELLS, 2 * CELLS)
            d_probs = dot(value_big, grad_two, ((1,), (1,))).reshape(4, CELLS, 2 * CELLS)
            raised = jnp.exp(scores - jnp.max(scores, axis=1, keepdims=True))
            probs = raised * (1.0 / jnp.sum(raised, axis=1, keepdims=True))
            probs_b = probs.astype(BF16).reshape(4 * CELLS, 2 * CELLS)
            inner = jnp.sum(probs * d_probs, axis=1, keepdims=True)
            d_scores = (
                (probs * (d_probs - inner) * scale).astype(BF16).reshape(4 * CELLS, 2 * CELLS)
            )
            out = dot(probs_b, value_big, ((0,), (0,)))
            att[at, t * 256 : (t + 1) * 256] = jnp.where(
                lane_half, out[:CELLS], out[CELLS:]
            ).astype(BF16)
            d_query = dot(d_scores, key_big, ((0,), (0,)))
            dpacked[at, cols[0]] = jnp.where(
                lane_half, d_query[:CELLS], d_query[CELLS:]
            ).astype(BF16)
            dpacked[at, cols[1]] = fold_heads(dot(d_scores, query_two)).astype(BF16)
            dpacked[at, cols[2]] = fold_heads(dot(probs_b, grad_two)).astype(BF16)
        return carry

    lax.fori_loop(0, count, one, 0, unroll=6 if count % 6 == 0 else UNROLL)
    if counts is None:
        stores = moves(list(zip((nw, att, dpacked), results)), out_sems)
    else:
        for copy in late:
            copy.wait()
        parts = [old_refs[4 * n : 4 * n + 4] for n in range(before)] + [(nw, att, dpacked, gw)]
        weight_sums(parts, counts, mine_ref[0], acc)
        half = feats // 2
        stores = moves([(acc.at[half:], give_hbm), (acc.at[:half], keep_hbm)], out_sems)

    def back(n, carry):
        at = pl.ds(pl.multiple_of(n * block, block), block)
        datt[at, :] = dot(dpacked[at, :], wqkv_ref[...], ((1,), (1,))).astype(BF16)
        return carry

    lax.fori_loop(0, rows // block, back, 0)
    if back_ref.shape[0] == 1:
        order = (
            lax.broadcasted_iota(jnp.int32, (rows, dn_ref.shape[0]), 0) == back_ref[...]
        ).astype(F32).astype(BF16)
        dn_ref[...] = dot(order, datt[...], ((0,), (0,))).astype(BF16)
    else:
        for p in range(CELLS // GROUP):
            ordered = jnp.concatenate(
                [
                    datt[w * CELLS + p * GROUP : w * CELLS + (p + 1) * GROUP, :]
                    for w in range(count)
                ],
                axis=0,
            )
            dn_ref[p * part : (p + 1) * part, :] = dot(
                back_ref[...], ordered, ((0,), (0,))
            ).astype(BF16)
    for copy in stores:
        copy.wait()


def place_of(i, j, row_count, chips):
    return (j % 2) * row_count * chips + i * chips + j // 2


def weight_sums(parts, counts, mine, acc):
    feats = acc.shape[0]
    row_count, chips = counts
    devices = 2 * row_count * chips
    size = feats // devices
    if size % 16:
        source = lax.broadcasted_iota(jnp.int32, (feats, feats), 1)
        device = source // size
        place = place_of(device // (2 * chips), device % (2 * chips), row_count, chips)
        target = jnp.bitwise_xor(mine, place) * size + source % size
        order = (lax.broadcasted_iota(jnp.int32, (feats, feats), 0) == target).astype(F32).astype(BF16)
    for left, right, start in ((0, 2, 0), (1, 3, 3 * feats)):
        turned = [part[left][...].T for part in parts]
        for t in range(parts[0][right].shape[1] // 256):
            at = slice(t * 256, (t + 1) * 256)
            to = slice(start + t * 256, start + (t + 1) * 256)
            sums = sum(dot(x, part[right][:, at]) for x, part in zip(turned, parts)).astype(BF16)
            if size % 16:
                acc[:, to] = dot(order, sums).astype(BF16)
                continue
            for n in range(devices):
                place = place_of(n // (2 * chips), n % (2 * chips), row_count, chips)
                block = jnp.bitwise_xor(mine, place)
                acc[pl.ds(pl.multiple_of(block * size, size), size), to] = sums[n * size : (n + 1) * size]


def norm_back(d_normed, nhat, rstd, grad, gain):
    scaled = d_normed * gain
    return (
        grad.astype(F32)
        + rstd
        * (
            scaled
            - jnp.mean(scaled, axis=-1, keepdims=True)
            - nhat * jnp.mean(scaled * nhat, axis=-1, keepdims=True)
        )
    ).astype(BF16)


def border_kernel(dn_ref, gain_ref, *refs):
    batches = refs[4].shape[0]
    feats = dn_ref.shape[1]
    size = dn_ref.shape[0] // batches
    for pick, pair, out in zip(refs[:4], refs[4:8], refs[8:]):
        for b in range(batches):
            d_normed = dot(pick[...], dn_ref[b * size : (b + 1) * size, :])
            mixed = pair[b, :, :feats].astype(F32)
            centred = mixed - jnp.mean(mixed, axis=-1, keepdims=True)
            rstd = lax.rsqrt(jnp.mean(centred * centred, axis=-1, keepdims=True) + 1e-05)
            out[b] = norm_back(d_normed, centred * rstd, rstd, pair[b, :, feats:], gain_ref[...])


def sums_kernel(count, *refs):
    orders, refs = refs[:count], refs[count:]
    hbm, refs = refs[:count], refs[count:]
    hbm, (left_ref, right_ref, gain_ref) = hbm + refs[:4], refs[4:7]
    out_ref, sums_ref, dn, side_l, side_r = refs[7:12]
    here, sems = refs[12:-1], refs[-1]
    parts = here[:count]
    stat_ref, mixed_ref, grad_ref, pad_ref = here[count:]
    loads = moves(list(zip(hbm, here)), sems)
    batches, rows, cols, feats = pad_ref.shape
    rows -= 2
    cells = rows * cols
    for copy in loads[:count]:
        copy.wait()
    for b in range(batches):
        total = None
        for order, part in zip(orders, parts):
            size = part.shape[0] // batches
            term = dot(order[...], part[b * size : (b + 1) * size, :])
            total = term if total is None else total + term
        dn[b * cells : (b + 1) * cells, :] = total
    block = 64
    for copy in loads[count : count + 3]:
        copy.wait()

    def norm(n, gain_sum):
        at = pl.ds(pl.multiple_of(n * block, block), block)
        d_normed = dn[at, :]
        rstd = stat_ref[at, 1:2]
        nhat = (mixed_ref[at, :].astype(F32) - stat_ref[at, 0:1]) * rstd
        out_ref[at, :] = norm_back(d_normed, nhat, rstd, grad_ref[at, :], gain_ref[...])
        return gain_sum + jnp.sum((d_normed * nhat).reshape(block // 8, 8, feats), axis=0)

    gain_sum = lax.fori_loop(
        0, batches * cells // block, norm, jnp.zeros((8, feats), F32), unroll=4
    )
    sums_ref[9:10, :] = jnp.sum(gain_sum, axis=0, keepdims=True)
    sums_ref[10:, :] = jnp.zeros((sums_ref.shape[0] - 10, feats), F32)
    loads[count + 3].wait()

    span = 8
    width = 256
    spot = lax.broadcasted_iota(jnp.int32, (cols, width), 0)
    fold = lambda v: jnp.sum(v.reshape(cols // 8, 8, width), axis=0)
    for c in range(feats // width):
        lanes = slice(c * width, (c + 1) * width)
        sums = [jnp.zeros((8, width), F32) for _ in range(9)]
        for b in range(batches):

            def step(n, sums, b=b, lanes=lanes):
                start = n * span
                x = [pad_ref[b, start + r, :, lanes].astype(F32) for r in range(span + 2)]
                sums = list(sums)
                for r in range(span):
                    h = start + r
                    at = pl.ds(pl.multiple_of((b * rows + h) * cols, cols), cols)
                    d_mixed = out_ref[at, lanes].astype(F32)
                    side_l[b, pl.ds(h, 1), lanes] = d_mixed[:1]
                    side_r[b, pl.ds(h, 1), lanes] = d_mixed[cols - 1 :]
                    moved = (
                        jnp.where(spot == cols - 1, 0.0, pltpu.roll(d_mixed, cols - 1, 0)),
                        d_mixed,
                        jnp.where(spot == 0, 0.0, pltpu.roll(d_mixed, 1, 0)),
                    )
                    for i in range(3):
                        for j in range(3):
                            sums[3 * i + j] = sums[3 * i + j] + fold(moved[j] * x[r + i])
                return tuple(sums)

            sums = lax.fori_loop(0, rows // span, step, tuple(sums))
        for n in range(9):
            sums_ref[n : n + 1, lanes] = jnp.sum(sums[n], axis=0, keepdims=True)
    for i in range(3):
        for b in range(batches):
            left, right = left_ref[b].astype(F32), right_ref[b].astype(F32)
            sums_ref[3 * i : 3 * i + 1, :] += jnp.sum(
                side_l[b] * left[i : i + rows], axis=0, keepdims=True
            )
            sums_ref[3 * i + 2 : 3 * i + 3, :] += jnp.sum(
                side_r[b] * right[i : i + rows], axis=0, keepdims=True
            )


def spread_kernel(d_ref, top_ref, bot_ref, left_ref, right_ref, dw_ref, out_ref, pad, side_l, side_r):
    batches, rows, cols, feats = pad.shape
    rows -= 2
    for b in range(batches):
        for h in range(rows):
            pad[b, h + 1] = d_ref[(b * rows + h) * cols : (b * rows + h + 1) * cols, :]
    pad[:, 0] = top_ref[...]
    pad[:, rows + 1] = bot_ref[...]
    convolve(pad, left_ref, right_ref, taps_of(dw_ref, True), side_l, side_r, out_ref)


def finish_kernel(*refs):
    *parts, qkv_ref, wout_ref, gain_ref, kernel_ref = refs
    feats = wout_ref.shape[1]
    level = total([part[...].astype(F32) for part in parts])
    qkv_ref[...] = level[:, : 3 * feats]
    wout_ref[...] = level[:, 3 * feats : 4 * feats]
    sums = level[:, 4 * feats :]
    gain_ref[...] = sums[9:10]
    for i in range(3):
        kernel_ref[i] = sums[3 * i : 3 * i + 3]


def call(body, outs, scratch, args, micros, name, hbm_ins=(), hbm_outs=(), scalars=(), limit=56 << 20):
    moved = sum(int(np.prod(o.shape)) * o.dtype.itemsize for o in (*outs, *args))
    vmem = pl.BlockSpec(memory_space=pltpu.VMEM)
    hbm = pl.BlockSpec(memory_space=pltpu.HBM)
    smem = pl.BlockSpec(memory_space=pltpu.SMEM)
    return pl.pallas_call(
        body,
        out_shape=outs,
        in_specs=[
            smem if n in scalars else hbm if n in hbm_ins else vmem for n in range(len(args))
        ],
        out_specs=[hbm if n in hbm_outs else vmem for n in range(len(outs))],
        scratch_shapes=scratch,
        compiler_params=pltpu.CompilerParams(vmem_limit_bytes=limit),
        cost_estimate=pl.CostEstimate(
            flops=micros * 10**9, bytes_accessed=moved, transcendentals=0
        ),
        name=name,
    )(*args)


def shape(dims, dtype):
    return jax.ShapeDtypeStruct(tuple(dims), dtype)


def shifted(cells, axis, step):
    count = lax.axis_size(axis)
    return lax.ppermute(cells, axis, [(n, n + step) for n in range(count) if 0 <= n + step < count])


def halos(top, bottom, left, right):
    above = shifted(bottom, "row", 1)
    below = shifted(top, "row", -1)
    last = above.shape[1] - 1
    column = lambda own, at: jnp.concatenate(
        [above[:, at : at + 1], own, below[:, at : at + 1]], axis=1
    )
    from_left = shifted(column(right, last), "col", 1)
    from_right = shifted(column(left, 0), "col", -1)
    return above, below, from_left, from_right


def swap(x, axis, step):
    return lax.ppermute(x, axis, [(n, n ^ step) for n in range(lax.axis_size(axis))])


def total(values):
    while len(values) > 1:
        values = [a + b for a, b in zip(values[::2], values[1::2])]
    return values[0]


def scatter(blocks, sums, axis, unit, count):
    size = blocks.shape[0] // count
    sums = sums.reshape(size, -1)
    load = lambda n: jnp.concatenate([blocks[n * size : (n + 1) * size], sums], axis=1).astype(BF16)
    own = jnp.concatenate([blocks[:size], sums], axis=1)
    return [own, *(swap(load(n), axis, unit * n) for n in range(1, count))]


def shards(plan, latent, w_qkv, w_out, ln_gain, dw_kernel, grad_out):
    batches, rows, cols, feats = latent.shape
    row_count, col_count = lax.axis_size("row"), lax.axis_size("col")
    cells = batches * rows * cols
    parts = len(plan.rows)
    gain = ln_gain.reshape(1, feats)
    send = jnp.asarray(plan.send_all, BF16)
    owner = lax.axis_index("row") * col_count + lax.axis_index("col")
    index = lax.dynamic_index_in_dim(jnp.asarray(plan.index), owner % plan.share, keepdims=False)
    back = [jnp.asarray(np.ascontiguousarray(m.T), BF16) for m in plan.send]
    sort = [index, *(jnp.asarray(m, BF16) for m in plan.sort[1:])]
    grouped = [shape((n * CELLS, feats), BF16) for n in plan.windows]
    take = [jnp.asarray(m, BF16) for m in plan.take]
    chunks = [shape((n, feats), BF16) for n in plan.rows]
    trade = lambda x: lax.all_to_all(x, AXES, split_axis=0, concat_axis=0, tiled=True)
    grad_flat = grad_out.reshape(cells, feats)

    flat = shape((cells, feats), BF16)
    (grad_sent,) = call(
        functools.partial(grad_kernel, batches),
        [flat],
        [
            pltpu.VMEM((cells, feats), BF16),
            pltpu.VMEM(send.shape, BF16),
            pltpu.VMEM((cells, feats), BF16),
            pltpu.SemaphoreType.DMA((1 + 2 * batches,)),
        ],
        [grad_flat, send],
        3,
        "grad_send",
        hbm_ins=(0, 1),
        hbm_outs=(0,),
    )
    grad_sent, latent = lax.optimization_barrier((grad_sent, latent))
    grad_win = trade(grad_sent)

    above, below, left, right = halos(latent[:, 0], latent[:, -1], latent[:, :, 0], latent[:, :, -1])
    padded = (batches, rows + 2, cols, feats)
    side = pltpu.VMEM((batches, rows, feats), F32)
    stat_shape = (cells, 2)
    const = lambda m: jnp.asarray(m, BF16)
    sent, mixed_inner, own_rows, own_cols = call(
        inner_kernel,
        [
            flat,
            flat,
            shape((batches, 4, cols, feats), BF16),
            shape((batches, 4 * rows, feats), BF16),
        ],
        [
            pltpu.VMEM((cells, feats), BF16),
            pltpu.VMEM(padded, BF16),
            pltpu.VMEM((cells, feats), BF16),
            side,
            side,
            pltpu.SemaphoreType.DMA((1,)),
        ],
        [latent, dw_kernel, gain, const(plan.send_inner), const(plan.columns)],
        6,
        "inner",
        limit=50 << 20,
        hbm_outs=(1,),
    )
    normed, mixed_border = call(
        edge_kernel,
        [flat, shape((batches, plan.unpick.shape[1], feats), BF16)],
        [],
        [sent, own_rows, own_cols, above, below, left, right, dw_kernel, gain, const(plan.send_border)],
        3,
        "edge",
        limit=50 << 20,
    )
    normed_win = trade(normed)
    ends = (0, cols, 2 * cols, 2 * cols + rows, 2 * cols + 2 * rows)
    grad_ends = (grad_out[:, 0], grad_out[:, -1], grad_out[:, :, 0], grad_out[:, :, -1])
    pairs = halos(
        *(
            jnp.concatenate([mixed_border[:, first:last], x], axis=-1)
            for first, last, x in zip(ends[:-1], ends[1:], grad_ends)
        )
    )
    mixed, stat, pad = call(
        patch_kernel,
        [flat, shape(stat_shape, F32), shape(padded, BF16)],
        [
            pltpu.VMEM((cells, feats), BF16),
            pltpu.VMEM(stat_shape, F32),
            pltpu.VMEM(padded, BF16),
            pltpu.SemaphoreType.DMA((3,)),
        ],
        [mixed_inner, mixed_border, const(plan.unpick), latent, above, below],
        4,
        "patch",
        limit=50 << 20,
        hbm_outs=(0, 1, 2),
    )

    chips = col_count // 2
    normed_win, mixed, stat, pad, *pairs = lax.optimization_barrier(
        (normed_win, mixed, stat, pad, *pairs)
    )
    ahead = call(
        functools.partial(grads_kernel, parts),
        [grouped[n // 2] for n in range(2 * parts)],
        [],
        [grad_win, w_out, *take],
        4,
        "grads",
        limit=50 << 20,
    )
    mine = place_of(lax.axis_index("row"), lax.axis_index("col"), row_count, chips).astype(jnp.int32).reshape(1)
    half = shape((feats // 2, 4 * feats), BF16)
    d_parts, kept = [], []
    for n in range(parts):
        count = plan.windows[n] * CELLS
        last = n == parts - 1
        mat = lambda width: pltpu.VMEM((count, width), BF16)
        args = [normed_win, ahead[2 * n + 1], take[n], sort[n], w_qkv]
        if last:
            outs = [chunks[n], half, half]
            args += [mine, ahead[2 * n], *kept]
            scratch = [
                mat(feats),
                pltpu.VMEM((feats, 4 * feats), BF16),
                pltpu.SemaphoreType.DMA((2,)),
                pltpu.SemaphoreType.DMA((1 + len(kept),)),
                *(pltpu.VMEM(x.shape, BF16) for x in kept),
            ]
        else:
            outs = [chunks[n], grouped[n], grouped[n], shape((count, 3 * feats), BF16)]
            scratch = [pltpu.SemaphoreType.DMA((3,))]
        d_chunk, *saved = call(
            functools.partial(window_kernel, (row_count, chips) if last else None, n),
            outs,
            [
                *scratch,
                pltpu.VMEM((cells, feats), BF16),
                pltpu.VMEM((feats, 3 * feats), BF16),
                mat(feats),
                mat(3 * feats),
                mat(feats),
                mat(feats),
                mat(3 * feats),
                pltpu.VMEM((4 * CELLS, 256), BF16),
                pltpu.VMEM((2 * CELLS, 256), BF16),
                pltpu.SemaphoreType.DMA((3,)),
            ],
            args,
            2 + 20 * count // cells,
            "windows",
        limit=56 << 20,
            hbm_ins=(0, 1, 4, *range(6, len(args))),
            hbm_outs=tuple(range(1, len(outs))),
            scalars=(5,),
        )
        kept += [*saved, ahead[2 * n]]
        d_parts.append(trade(d_chunk))
    keep, give = saved

    d_halos = call(
        border_kernel,
        [shape((*x.shape[:2], feats), BF16) for x in pairs],
        [],
        [d_parts[0], gain, *(jnp.asarray(m, BF16) for m in plan.pieces), *pairs],
        3,
        "border",
        limit=50 << 20,
    )
    weights = (keep.astype(F32) + swap(give, "col", 1).astype(F32)).astype(BF16)
    d_mixed, sums = call(
        functools.partial(sums_kernel, parts),
        [flat, shape((16, feats), F32)],
        [
            pltpu.VMEM((cells, feats), F32),
            side,
            side,
            *(pltpu.VMEM((n, feats), BF16) for n in plan.rows),
            pltpu.VMEM(stat_shape, F32),
            pltpu.VMEM((cells, feats), BF16),
            pltpu.VMEM((cells, feats), BF16),
            pltpu.VMEM(padded, BF16),
            pltpu.SemaphoreType.DMA((parts + 4,)),
        ],
        [*back, *d_parts, stat, mixed, grad_flat, pad, left, right, gain],
        7,
        "sums",
        limit=50 << 20,
        hbm_ins=tuple(range(parts, 2 * parts + 4)),
    )
    wide = 4 * feats
    size = weights.shape[0] // row_count
    gives = [
        swap(weights[n * size : (n + 1) * size], "row", n) for n in range(1, row_count)
    ]
    sums, weights, *gives = lax.optimization_barrier((sums, weights, *gives))
    weights = total([x.astype(F32) for x in (weights[:size], *gives)])
    sums = sums + swap(sums, "col", 1)
    sums = total([sums, *(swap(sums, "row", n) for n in range(1, row_count))])
    sums, d_mixed = lax.optimization_barrier((sums, d_mixed))
    (grad_latent,) = call(
        spread_kernel,
        [flat],
        [pltpu.VMEM(padded, BF16), side, side],
        [d_mixed, *d_halos, dw_kernel],
        5,
        "spread",
        limit=50 << 20,
    )
    level = scatter(weights, sums, "col", 2, chips)
    grad_latent = grad_latent.reshape(latent.shape)
    size = level[0].shape[0]
    if size == 16:
        qkv, wout, gain_sum, kernel_sum = call(
            finish_kernel,
            [
                shape((size, 3 * feats), F32),
                shape((size, feats), F32),
                shape((1, feats), F32),
                shape((3, 3, feats), F32),
            ],
            [],
            level,
            1,
            "finish",
            limit=50 << 20,
        )
        return grad_latent, qkv, wout, gain_sum.reshape(feats), kernel_sum
    level = total([x.astype(F32) for x in level])
    sums = level[:, wide:].reshape(16, feats)
    return (
        grad_latent,
        level[:, : 3 * feats],
        level[:, 3 * feats : wide],
        sums[9],
        sums[:9].reshape(3, 3, feats),
    )


def solution(mesh):
    row_count, col_count = mesh.shape["row"], mesh.shape["col"]

    def run(latent, w_qkv, w_out, ln_gain, dw_kernel, grad_out):
        batches, rows, cols, _ = latent.shape
        plan = Plan(batches, rows // row_count, cols // col_count, row_count, col_count)
        in_specs = (P(None, "row", "col", None), P(), P(), P(), P(), P(None, "row", "col", None))
        out_specs = (
            P(None, "row", "col", None),
            P(AXES, None),
            P(AXES, None),
            P(),
            P(),
        )
        return jax.shard_map(
            functools.partial(shards, plan),
            mesh=mesh,
            in_specs=in_specs,
            out_specs=out_specs,
            check_vma=False,
        )(latent, w_qkv, w_out, ln_gain, dw_kernel, grad_out)

    return run
```
